32 devices in a mesh: seq: 8 (over z, x), fsdp: 4 (over y, core).
Axes of the slice: x: 2, y: 2, z: 4, core: 2. Of those that a mesh axis runs over, the one named last changes fastest.
Arguments:
- tokens: bfloat16 [8, 2048, 768], P('fsdp', 'seq'), may hold values from -6 to 6
- cotangent: bfloat16 [8, 2048, 768], P('fsdp', 'seq'), may hold values from -6 to 6
- segments: int32 [8, 2048], P('fsdp'), may hold values from 0 to 7, never falling along the last dimension, each value on 1 to 2000 neighbouring positions
- routes: int32 [8, 2048, 2], P('fsdp', 'seq'), may hold values from 0 to 15, all different within a row
- norm_attn: bfloat16 [768], P('fsdp'), may hold values from 0.5 to 1.5
- w_qkv: bfloat16 [768, 2304], P('fsdp'), may hold values from -0.21875 to 0.21875
- w_o: bfloat16 [768, 768], P('fsdp'), may hold values from -1.75 to 1.75
- rel_bias: bfloat16 [32, 12], P('fsdp'), may hold values from -4 to 4
- norm_ffn: bfloat16 [768], P('fsdp'), may hold values from 0.5 to 1.5
- router: bfloat16 [768, 16], P('fsdp'), may hold values from -0.15625 to 0.15625
- w_in: bfloat16 [3072, 16, 768], P('fsdp', 'seq'), may hold values from -0.21875 to 0.21875
- w_out: bfloat16 [3072, 16, 768], P('fsdp', 'seq'), may hold values from -0.109375 to 0.109375
- b_out: bfloat16 [16, 768], P('seq', 'fsdp'), may hold values from -0.5 to 0.5
Outputs:
- output: bfloat16 [8, 2048, 768], P('fsdp', 'seq')
- grad_tokens: float32 [8, 2048, 768], P('fsdp', 'seq')
- grad_norm_attn: float32 [768], P('fsdp')
- grad_w_qkv: float32 [768, 2304], P('fsdp')
- grad_w_o: float32 [768, 768], P('fsdp')
- grad_rel_bias: float32 [32, 12], P('fsdp')
- grad_norm_ffn: float32 [768], P('fsdp')
- grad_router: float32 [768, 16], P('fsdp')
- grad_w_in: float32 [3072, 16, 768], P('fsdp', 'seq')
- grad_w_out: float32 [3072, 16, 768], P('fsdp', 'seq')
- grad_b_out: float32 [16, 768], P('seq', 'fsdp')
The draws below stay inside these ranges and needn't reach their ends.
Inputs may be any that keep to these rules, and one draw needn't show every extreme that they name: `segments`: document numbers never fall along a sequence; a sequence has at most 8 documents, each of 1 to 2000 positions, one of exactly 2000. `routes`: the 2 experts of a token differ; every expert is named by some token.
All inputs are finite; a program needn't handle non-finite values.
Results may differ from the reference program's by a relative error of at most 0.02.
Values may be sent and summed in bfloat16 or wider, within the bound.
No kernel may reach another device: no remote copies, remote signals or barrier semaphores. Data moves between devices by JAX's collectives and lax.ppermute only.
A program may use at most 384 MiB of HBM per device.

```python
import math
from functools import partial
import jax
import jax.numpy as jnp
import numpy as np
from jax import lax

D = 768
HEADS = 12
HEAD_DIM = 64
FF = 3072
TOP = 2
SEQ_LEN = 2048
QBLK = 512
BUCKETS = 32
DOCS = 8
DOC_MOST = 2000
TOK_DEV = 512
EXPERTS = 16
GROUP_SEQS = 2
SEQS = 8
SLAB = 256
CAP = 72
N_SEQ = 8
N_FSDP = 4
DEVICES = 32


def shard_levels(key, dims, cuts, least, top_value):
    factor_of, own = 1.0, jax.random.fold_in(key, 6)
    for position, parts in cuts:
        draws = jnp.exp(jax.random.uniform(jax.random.fold_in(own, position), (parts,), jnp.float32, least / len(cuts), top_value / len(cuts)))
        factor_of = factor_of * jnp.repeat(draws, dims[position] // parts).reshape([-1 if axis == position else 1 for axis in range(len(dims))])
    return factor_of


def choose_distinct(stream_key, rows, number_of, top, lift):
    sequence = jax.random.permutation(jax.random.fold_in(stream_key, 1), number_of)
    favour = sequence
    for power in range(3):
        favour = favour * favour // number_of
    favour = favour * lift // number_of
    tickets = jax.random.randint(jax.random.fold_in(stream_key, 2), (rows, number_of), 0, 4096) + favour
    fixed_rows = jax.random.permutation(jax.random.fold_in(stream_key, 3), rows)[jnp.arange(number_of) % rows]
    tickets = jnp.where(jnp.arange(rows)[:, None] == fixed_rows[None, :], 1 << 14, tickets)
    score = tickets * number_of + jnp.arange(number_of)
    return lax.top_k(score.astype(jnp.int32), top)[1].astype(jnp.int32)


def length_profile(count, total, limit, lean):
    loads = [(1 << 20) // math.isqrt(standing ** lean) + 1 for standing in range(2, count + 1)]
    rest, counts = total - limit - (count - 1), [1] * (count - 1)
    while rest > 0:
        candidates = [i for i in range(count - 1) if counts[i] < limit]
        whole, left = sum([loads[i] for i in candidates]), rest
        for i in candidates:
            addition = min(limit - counts[i], max(1, left * loads[i] // whole), rest)
            counts[i] = counts[i] + addition
            rest = rest - addition
    return np.array([limit] + counts)


def ragged(rng, number_of, total, bound, lean):
    if number_of == 2:
        one = jax.random.randint(rng, (), max(1, total - bound), min(bound, total - 1) + 1)
        return jnp.stack([one, total - one])
    tallies = jnp.asarray(length_profile(number_of, total, bound, lean), jnp.int32)
    couples = (number_of - 1) // 2
    source_of, receiver = tallies[1:1 + 2 * couples:2], tallies[2:2 + 2 * couples:2]
    room = jnp.minimum(source_of - 1, bound - receiver)
    shifted = jax.random.randint(jax.random.fold_in(rng, 1), (couples,), 0, 1 << 20) % (room + 1)
    tallies = tallies.at[1:1 + 2 * couples:2].set(source_of - shifted).at[2:2 + 2 * couples:2].set(receiver + shifted)
    return tallies[jax.random.permutation(jax.random.fold_in(rng, 2), number_of)]


def scatter_about(rng, shape, scale, limit, shards=(), held_as=jnp.bfloat16):
    values = scale * jax.random.normal(rng, shape, jnp.float32)
    if shards:
        values = values * shard_levels(rng, shape, shards, -0.22, 0.18)
    return jnp.clip(values, -limit, limit).astype(held_as)


def setup_inputs(seed: int = 0) -> dict:
    seeds = jax.random.split(jax.random.key(seed), 14)
    tokens = scatter_about(seeds[0], (SEQS, SEQ_LEN, D), 1.0, 6.0, ((0, 4), (1, 8)))
    cotangent = scatter_about(seeds[1], (SEQS, SEQ_LEN, D), 1.0, 6.0, ((0, 4), (1, 8)))
    segments = jax.vmap(lambda own: jnp.searchsorted(jnp.cumsum(ragged(own, DOCS, SEQ_LEN, DOC_MOST, 2)), jnp.arange(SEQ_LEN), side="right"))(jax.random.split(seeds[2], SEQS)).reshape((SEQS, SEQ_LEN)).astype(jnp.int32)
    routes = choose_distinct(seeds[3], SEQS * SEQ_LEN, EXPERTS, TOP, 1024).reshape((SEQS, SEQ_LEN, TOP))
    norm_attn = jnp.clip(1.0 + 0.1 * jax.random.normal(seeds[4], (D,), jnp.float32), 0.5, 1.5).astype(jnp.bfloat16)
    w_qkv = scatter_about(seeds[5], (D, 3 * D), D ** -0.5, 0.21875, ((0, 4),))
    w_o = scatter_about(seeds[6], (D, D), (D // 64) ** -0.5, 1.75, ((0, 4),))
    rel_bias = scatter_about(seeds[7], (BUCKETS, HEADS), 1.0, 4.0, ((0, 4),))
    norm_ffn = jnp.clip(1.0 + 0.1 * jax.random.normal(seeds[8], (D,), jnp.float32), 0.5, 1.5).astype(jnp.bfloat16)
    router = scatter_about(seeds[9], (D, EXPERTS), (2 * D) ** -0.5, 0.15625, ((0, 4),))
    w_in = scatter_about(seeds[10], (FF, EXPERTS, D), D ** -0.5, 0.21875, ((0, 4), (1, 8)))
    w_out = scatter_about(seeds[11], (FF, EXPERTS, D), FF ** -0.5, 0.109375, ((0, 4), (1, 8)))
    b_out = scatter_about(seeds[12], (EXPERTS, D), 0.1, 0.5, ((0, 8), (1, 4)))
    return dict(tokens=tokens, cotangent=cotangent, segments=segments, routes=routes, norm_attn=norm_attn, w_qkv=w_qkv, w_o=w_o, rel_bias=rel_bias, norm_ffn=norm_ffn, router=router, w_in=w_in, w_out=w_out, b_out=b_out)


@jax.custom_vjp
def low(v):
    return lax.optimization_barrier(v.astype(jnp.bfloat16)).astype(jnp.float32)

@jax.custom_vjp
def low_back(v):
    return v

def low_keep(v):
    return (low(v), None)

def low_pass(kept, grad):
    return (grad,)

def back_keep(v):
    return (v, None)

def back_low(kept, grad):
    return (low(grad),)
low.defvjp(low_keep, low_pass)
low_back.defvjp(back_keep, back_low)
bucket_edges = tuple((int(math.ceil(16 * 8 ** (step_k / 16))) for step_k in range(1, 16)))
exact_precision = lax.Precision.HIGHEST

def bucket_of(distance):
    far_part = 16 + sum(((distance >= edge_value).astype(jnp.int32) for edge_value in bucket_edges))
    return jnp.where(distance < 16, distance, far_part)

def normed(values, norm_gain):
    return values * lax.rsqrt(lax.optimization_barrier(jnp.mean(values * values, -1, keepdims=True)) + 1e-06) * norm_gain

def gate_softmax(chosen):
    row_top = lax.optimization_barrier(jnp.max(chosen, -1, keepdims=True))
    exp_terms = jnp.exp(chosen - row_top)
    return exp_terms / lax.optimization_barrier(jnp.sum(exp_terms, -1, keepdims=True))

def device_major(values):
    tail_dims = values.shape[2:]
    split_view = values.reshape((N_FSDP, GROUP_SEQS, N_SEQ, SLAB) + tail_dims)
    return jnp.swapaxes(split_view, 1, 2).reshape((DEVICES, TOK_DEV) + tail_dims)

def token_major(values):
    tail_dims = values.shape[2:]
    split_view = values.reshape((N_FSDP, N_SEQ, GROUP_SEQS, SLAB) + tail_dims)
    return jnp.swapaxes(split_view, 1, 2).reshape((SEQS, SEQ_LEN) + tail_dims)

def slot_tables(routes):
    flat_routes = device_major(routes).reshape(DEVICES, TOK_DEV * TOP)
    hit_table = (flat_routes[:, :, None] == jnp.arange(EXPERTS, dtype=jnp.int32)[None, None, :]).astype(jnp.int32)
    pair_rank = lax.optimization_barrier(jnp.sum(jnp.cumsum(hit_table, 1) * hit_table, 2)) - 1
    kept_pair = pair_rank < CAP
    token_ids = device_major(jnp.arange(SEQS * SEQ_LEN, dtype=jnp.int32).reshape(SEQS, SEQ_LEN))
    pair_token = jnp.repeat(token_ids, TOP, axis=1)
    device_ids = jnp.arange(DEVICES, dtype=jnp.int32)[:, None]
    slot_count = EXPERTS * DEVICES * CAP
    slot_index = flat_routes * (DEVICES * CAP) + device_ids * CAP + pair_rank
    target = jnp.where(kept_pair, slot_index, slot_count).reshape(-1)
    slot_token = jnp.full((slot_count,), -1, jnp.int32).at[target].set(pair_token.reshape(-1), mode='drop')
    return (kept_pair, jnp.where(kept_pair, slot_index, 0), slot_token)

def attend_sequence(rel_table, operands):
    queries, key_rows, value_rows, seg_row = operands

    def one_block(block_index):
        row_start = block_index * QBLK
        query_rows = lax.dynamic_slice_in_dim(queries, row_start, QBLK, 0)
        rows_at = row_start + jnp.arange(QBLK, dtype=jnp.int32)
        distance = rows_at[:, None] - jnp.arange(SEQ_LEN, dtype=jnp.int32)[None, :]
        bucket = bucket_of(jnp.maximum(distance, 0))
        rel_terms = jnp.take(rel_table.T, bucket, axis=1)
        raw_scores = jnp.einsum('qhd,khd->hqk', query_rows, key_rows, precision=exact_precision) * HEAD_DIM ** (-0.5)
        scores = low_back(raw_scores + rel_terms)
        seg_query = lax.dynamic_slice_in_dim(seg_row, row_start, QBLK, 0)
        allowed = (distance >= 0) & (seg_query[:, None] == seg_row[None, :])
        masked = jnp.where(allowed[None], scores, -1e+30)
        row_peak = lax.optimization_barrier(jnp.max(masked, -1, keepdims=True))
        lse_rows = row_peak + jnp.log(lax.optimization_barrier(jnp.sum(jnp.exp(masked - row_peak), -1, keepdims=True)))
        attn_probs = low(jnp.exp(masked - lse_rows))
        return jnp.einsum('hqk,khd->qhd', attn_probs, value_rows, precision=exact_precision)
    blocks = lax.map(jax.checkpoint(one_block), jnp.arange(SEQ_LEN // QBLK, dtype=jnp.int32))
    return blocks.reshape(SEQ_LEN, HEADS, HEAD_DIM)

def expert_apply(operands):
    rows_in, weight_in, weight_out, bias_out = operands
    pre_act = low_back(jnp.einsum('rd,fd->rf', rows_in, weight_in, precision=exact_precision))
    act_rows = low(jax.nn.gelu(pre_act, approximate=True))
    result_rows = jnp.einsum('rf,fd->rd', act_rows, weight_out, precision=exact_precision) + bias_out
    return low(low_back(result_rows))

def forward(tokens, norm_attn, w_qkv, w_o, rel_bias, norm_ffn, router, w_in, w_out, b_out, segments, routes, slot_info):
    first = low(normed(tokens, norm_attn))
    qkv = jnp.einsum('slm,mc->slc', first, w_qkv, precision=exact_precision)
    qkv = low(low_back(qkv)).reshape(SEQS, SEQ_LEN, 3, HEADS, HEAD_DIM)
    attended = lax.map(partial(attend_sequence, rel_bias), (qkv[:, :, 0], qkv[:, :, 1], qkv[:, :, 2], segments))
    attended = low(low_back(attended)).reshape(SEQS, SEQ_LEN, D)
    residual_mid = tokens + low_back(jnp.einsum('slm,mn->sln', attended, w_o, precision=exact_precision))
    second = low(normed(residual_mid, norm_ffn))
    logits = low_back(jnp.einsum('slm,me->sle', second, router, precision=exact_precision))
    chosen = jnp.take_along_axis(logits, routes, axis=2)
    gates = gate_softmax(chosen)
    kept_pair, pair_slot, slot_token = slot_info
    flat_second = second.reshape(SEQS * SEQ_LEN, D)
    filled = (slot_token >= 0)[:, None]
    dispatched = jnp.where(filled, jnp.take(flat_second, jnp.maximum(slot_token, 0), axis=0), 0.0)
    dispatched = low_back(dispatched).reshape(EXPERTS, DEVICES * CAP, D)
    results = lax.map(jax.checkpoint(expert_apply), (dispatched, jnp.swapaxes(w_in, 0, 1), jnp.swapaxes(w_out, 0, 1), b_out))
    flat_results = results.reshape(EXPERTS * DEVICES * CAP, D)
    pair_rows = jnp.where(kept_pair[..., None], jnp.take(flat_results, pair_slot, axis=0), 0.0)
    pair_gates = device_major(gates).reshape(DEVICES, TOK_DEV * TOP)
    mixed = lax.optimization_barrier(jnp.sum((pair_rows * pair_gates[..., None]).reshape(DEVICES, TOK_DEV, TOP, D), 2))
    return residual_mid + token_major(mixed)

def reference(tokens, cotangent, segments, routes, norm_attn, w_qkv, w_o, rel_bias, norm_ffn, router, w_in, w_out, b_out):
    slot_info = slot_tables(routes)
    floats = tuple((source_arr.astype(jnp.float32) for source_arr in (tokens, norm_attn, w_qkv, w_o, rel_bias, norm_ffn, router, w_in, w_out, b_out)))

    def closed(tok_in, gain_one, qkv_in, proj_in, rel_in, gain_two, route_in, first_in, second_in, bias_in):
        return forward(tok_in, gain_one, qkv_in, proj_in, rel_in, gain_two, route_in, first_in, second_in, bias_in, segments, routes, slot_info)
    result, pull_back = jax.vjp(closed, floats[0], floats[1], floats[2], floats[3], floats[4], floats[5], floats[6], floats[7], floats[8], floats[9])
    grads = pull_back(cotangent.astype(jnp.float32))
    return (result.astype(jnp.bfloat16), grads[0], grads[1], grads[2], grads[3], grads[4], grads[5], grads[6], grads[7], grads[8], grads[9])
```

```python
import functools
import math

import jax
import jax.numpy as jnp
from jax import lax
from jax.experimental import pallas as pl
from jax.experimental.pallas import tpu as pltpu
from jax.sharding import PartitionSpec as P

D = 768
HEADS = 12
HEAD_DIM = 64
TOP = 2
SEQ_LEN = 2048
BUCKETS = 32
DOCS = 8
QB = 256
BAND = QB + 128
EPS = 1e-06
NEG = -1e30
F32 = jnp.float32
BF = jnp.bfloat16
bucket_starts = tuple(range(17)) + tuple(
    int(math.ceil(16 * 8 ** (step_k / 16))) for step_k in range(1, 16)
)
VMEM_MOST = 56 << 20
COST_SHARE = 1
FILLER = 0.02
G_AFTER = 8


def dot(lhs, rhs, lhs_dim, rhs_dim):
    return lax.dot_general(
        lhs, rhs, (((lhs_dim,), (rhs_dim,)), ((), ())), preferred_element_type=F32
    )


def params():
    return pltpu.CompilerParams(vmem_limit_bytes=VMEM_MOST)


def cost(flops, bytes_accessed, transcendentals=0):
    return pl.CostEstimate(
        flops=int(flops * COST_SHARE), bytes_accessed=int(bytes_accessed * COST_SHARE),
        transcendentals=int(transcendentals * COST_SHARE),
    )


def shape(dims, dtype):
    return jax.ShapeDtypeStruct(dims, dtype)


def load_pair(qkv_ref, seg_ref, qt, kt, vt):
    slabs, _, slab = qkv_ref.shape
    for index in range(slabs):
        cols = slice(index * slab, (index + 1) * slab)
        qt[0:64, cols] = qkv_ref[index, 0:64, :] * jnp.asarray(0.125, BF)
        kt[0:64, cols] = qkv_ref[index, 64:128, :]
        vt[0:64, cols] = qkv_ref[index, 128:192, :]
    row = lax.broadcasted_iota(jnp.int32, (16, SEQ_LEN), 0)
    same = seg_ref[...] == row
    kt[64:80, :] = jnp.where(same, 1.0, 0.0).astype(BF)
    qt[64:80, :] = jnp.where(same | (row >= DOCS), 0.0, NEG).astype(BF)


def key_parts(block):
    end = (block + 1) * QB
    near = max(end - BAND, 0)
    return [(near, end)] + ([(0, near)] if near > 0 else [])


def fwd_kernel(qkv_ref, seg_ref, band_ref, o_ref, wide_ref, lse_ref, qt, kt, vt, k_rows):
    slabs, _, slab = qkv_ref.shape
    load_pair(qkv_ref, seg_ref, qt, kt, vt)
    k_rows[...] = kt[...].T
    for block in range(SEQ_LEN // QB):
        start, end = block * QB, (block + 1) * QB
        query = qt[:, start:end]
        scores = []
        for low, high in key_parts(block):
            part = dot(k_rows[low:high], query, 1, 0)
            if high == end:
                part = part + band_ref[0, BAND - (high - low) :, :]
            scores.append((low, high, part))
        peak = functools.reduce(
            jnp.maximum, [jnp.max(part, 0, keepdims=True) for _, _, part in scores]
        )
        total, out = 0.0, 0.0
        for low, high, part in scores:
            terms = jnp.exp(part - peak)
            total = total + jnp.sum(terms, 0, keepdims=True)
            out = out + dot(vt[:, low:high], terms.astype(BF), 1, 0)
        wide_ref[0, :, start:end] = out * (1.0 / total)
        lse_ref[0, :, start:end] = peak + jnp.log(total)
    for index in range(slabs):
        o_ref[index] = wide_ref[0, :, index * slab : (index + 1) * slab].astype(BF)


def bwd_kernel(
    qkv_ref, seg_ref, band_ref, wide_ref, lse_ref, do_ref, d_ref, hist_ref,
    qt, kt, vt, k_rows, v_rows, do_t, dq, dk, dv,
):
    slabs, _, slab = qkv_ref.shape
    load_pair(qkv_ref, seg_ref, qt, kt, vt)
    k_rows[...] = kt[...].T
    v_rows[...] = vt[...].T
    for index in range(slabs):
        do_t[:, index * slab : (index + 1) * slab] = do_ref[index]
    dk[...] = jnp.zeros_like(dk)
    dv[...] = jnp.zeros_like(dv)
    hist_ref[...] = jnp.zeros_like(hist_ref)
    for block in range(SEQ_LEN // QB):
        start, end = block * QB, (block + 1) * QB
        query, grad = qt[:, start:end], do_t[:, start:end]
        delta = jnp.sum(grad.astype(F32) * wide_ref[0, :, start:end], 0, keepdims=True)
        lse = lse_ref[0, :, start:end]
        grad_query = 0.0
        for low, high in key_parts(block):
            part = dot(k_rows[low:high], query, 1, 0)
            off = BAND - (high - low)
            if high == end:
                part = part + band_ref[0, off:, :]
            probs = jnp.exp(part - lse)
            grad_probs = dot(v_rows[low:high], grad, 1, 0)
            grad_scores = (probs * (grad_probs - delta)).astype(BF)
            if high == end:
                hist_ref[0, off:, :] += grad_scores.astype(F32)
            dv[:, low:high] += dot(grad, probs.astype(BF), 1, 1)
            dk[:, low:high] += dot(query[0:64], grad_scores, 1, 1)
            grad_query = grad_query + dot(kt[0:64, low:high], grad_scores, 1, 0)
        dq[:, start:end] = grad_query * 0.125
    for index in range(slabs):
        cols = slice(index * slab, (index + 1) * slab)
        d_ref[index, 0:64, :] = dq[:, cols].astype(BF)
        d_ref[index, 64:128, :] = dk[:, cols].astype(BF)
        d_ref[index, 128:192, :] = dv[:, cols].astype(BF)


def attention_specs(slabs, slab):
    qkv = pl.BlockSpec((slabs, 192, slab), lambda p: (0, p, 0))
    one = pl.BlockSpec((slabs, 64, slab), lambda p: (0, p, 0))
    seg = pl.BlockSpec((1, SEQ_LEN), lambda p: (0, 0))
    band = pl.BlockSpec((1, BAND, QB), lambda p: (p, 0, 0))
    wide = pl.BlockSpec((1, 64, SEQ_LEN), lambda p: (p, 0, 0))
    lse = pl.BlockSpec((1, 1, SEQ_LEN), lambda p: (p, 0, 0))
    return qkv, one, seg, band, wide, lse


def attention_fwd(qkv, seg, bands):
    slabs, rows, slab = qkv.shape
    pairs = rows // 192
    qkv_s, one_s, seg_s, band_s, wide_s, lse_s = attention_specs(slabs, slab)
    return pl.pallas_call(
        fwd_kernel,
        grid=(pairs,),
        out_shape=(
            shape((slabs, 64 * pairs, slab), BF),
            shape((pairs, 64, SEQ_LEN), F32),
            shape((pairs, 1, SEQ_LEN), F32),
        ),
        in_specs=[qkv_s, seg_s, band_s],
        out_specs=(one_s, wide_s, lse_s),
        scratch_shapes=[
            pltpu.VMEM((80, SEQ_LEN), BF),
            pltpu.VMEM((80, SEQ_LEN), BF),
            pltpu.VMEM((64, SEQ_LEN), BF),
            pltpu.VMEM((SEQ_LEN, 80), BF),
        ],
        compiler_params=params(),
        cost_estimate=cost(pairs * 6e9, pairs * 2e6, pairs * 2.4e6),
    )(qkv, seg, bands)


def attention_bwd(qkv, seg, bands, wide, lse, grad):
    slabs, rows, slab = qkv.shape
    pairs = rows // 192
    qkv_s, one_s, seg_s, band_s, wide_s, lse_s = attention_specs(slabs, slab)
    return pl.pallas_call(
        bwd_kernel,
        grid=(pairs,),
        out_shape=(shape(qkv.shape, BF), shape((pairs, BAND, QB), F32)),
        in_specs=[qkv_s, seg_s, band_s, wide_s, lse_s, one_s],
        out_specs=(qkv_s, band_s),
        scratch_shapes=[
            pltpu.VMEM((80, SEQ_LEN), BF),
            pltpu.VMEM((80, SEQ_LEN), BF),
            pltpu.VMEM((64, SEQ_LEN), BF),
            pltpu.VMEM((SEQ_LEN, 80), BF),
            pltpu.VMEM((SEQ_LEN, 64), BF),
            pltpu.VMEM((64, SEQ_LEN), BF),
            pltpu.VMEM((64, SEQ_LEN), F32),
            pltpu.VMEM((64, SEQ_LEN), F32),
            pltpu.VMEM((64, SEQ_LEN), F32),
        ],
        compiler_params=params(),
        cost_estimate=cost(pairs * 10e9, pairs * 3e6, pairs * 2.4e6),
    )(qkv, seg, bands, wide, lse, grad)


def rms(values):
    return lax.rsqrt(jnp.mean(values * values, -1, keepdims=True) + EPS)


def one_step(kernel, outs, operands, flops, scratch=(), smem=0):
    size = sum(math.prod(a.shape) * a.dtype.itemsize for a in (*operands, *outs))
    return pl.pallas_call(
        kernel,
        out_shape=tuple(outs),
        in_specs=[pl.BlockSpec(memory_space=pltpu.SMEM)] * smem
        + [pl.BlockSpec(memory_space=pltpu.VMEM)] * (len(operands) - smem),
        out_specs=tuple([pl.BlockSpec(memory_space=pltpu.VMEM)] * len(outs)),
        scratch_shapes=list(scratch),
        compiler_params=params(),
        cost_estimate=cost(flops * FILLER, size * FILLER),
    )(*operands)


BIAS_ROW, B_ROW, ROUTER_ROW = 2, 5, 8


def pack_kernel(hg_ref, w_ref, o_ref, attn_ref, ffn_ref, bias_ref, b_ref, router_ref, out_ref, lines):
    part = o_ref.shape[0]
    local, experts = b_ref.shape[0], router_ref.shape[1]
    width = (out_ref.shape[1] - D - 128) // 3
    pairs = width // 64
    out_ref[:, 0:D] = o_ref[...]
    lines[...] = jnp.zeros_like(lines)
    lines[0:1, 0:part] = attn_ref[...].astype(F32)
    lines[1:2, 0:part] = ffn_ref[...].astype(F32)
    lines[B_ROW : B_ROW + local, 0:part] = b_ref[...].astype(F32)
    turned = lines[...].T
    column = lax.broadcasted_iota(jnp.int32, (part, 128), 1)
    router = jnp.concatenate([router_ref[...], jnp.zeros((part, 128 - experts), BF)], 1)
    router = pltpu.roll(router.astype(F32), ROUTER_ROW, 1)
    narrow = jnp.where(column < ROUTER_ROW, turned[0:part], router)
    out_ref[:, D : D + 128] = narrow.astype(BF)
    for mine in range(D // width):

        @pl.when(hg_ref[0] == mine)
        def _():
            for which in range(3):
                source, to = which * D + mine * width, D + 128 + which * width
                out_ref[:, to : to + width] = w_ref[:, source : source + width]
            out_ref[0 : bias_ref.shape[0], D + BIAS_ROW : D + BIAS_ROW + pairs] = bias_ref[
                :, mine * pairs : (mine + 1) * pairs
            ]


def unpack_kernel(me_ref, *refs, offsets, pairs):
    part_refs, (w_ref, o_ref, small_ref, band_ref, narrow) = refs[: len(offsets)], refs[len(offsets) :]
    rows = part_refs[0].shape[0]
    for offset, ref in zip(offsets, part_refs):
        at = pl.ds(pl.multiple_of((me_ref[0] ^ offset) * rows, 32), rows)
        o_ref[at, :] = ref[:, 0:D]
        narrow[at, :] = ref[:, D : D + 128].astype(F32)
        w_ref[at, :] = ref[:, D + 128 :]
    small_ref[...] = narrow[...].T
    row = lax.broadcasted_iota(jnp.int32, (BAND, QB), 0)
    col = lax.broadcasted_iota(jnp.int32, (BAND, QB), 1)
    distance = col + (BAND - QB) - row
    per_owner = BUCKETS * rows // D
    for pair in range(pairs):
        source = BIAS_ROW + pair

        def entry(index_b):
            lane = index_b // per_owner * rows + index_b % per_owner
            return small_ref[source : source + 1, lane : lane + 1]

        last = entry(BUCKETS - 1)
        table = jnp.where(distance < 0, NEG, entry(0) - last)
        for index_b in range(1, BUCKETS):
            table = jnp.where(distance >= bucket_starts[index_b], entry(index_b) - last, table)
        band_ref[pair] = table


def project_kernel(me_ref, small_ref, w_ref, *refs, offsets):
    tok_refs, (qkv_ref, first_ref) = refs[:-2], refs[-2:]
    pairs = w_ref.shape[1] // 192
    for offset, ref in zip(offsets, tok_refs):
        at = me_ref[0] ^ offset
        x = ref[...].astype(F32)
        first = (x * rms(x) * small_ref[0:1, :]).astype(BF)
        first_ref[at] = first
        result = dot(w_ref[...], first, 0, 1).astype(BF)
        for pair in range(pairs):
            for which in range(3):
                to, source = pair * 192 + which * 64, (which * pairs + pair) * 64
                qkv_ref[at, to : to + 64, :] = result[source : source + 64, :]


def route_kernel(
    col_ref, row_ref, base_col_ref, base_row_ref, g_ref, sc_ref, sr_ref, other_ref, *gd_refs,
    experts, capacity,
):
    count = col_ref.shape[0]
    each = gd_refs[0].shape[0]
    slots = each * len(gd_refs)
    r0, r1 = col_ref[:, 0:1], col_ref[:, 1:2]
    expert = lax.broadcasted_iota(jnp.int32, (count, experts), 1)
    is0, is1 = expert == r0, expert == r1
    hits = jnp.where(is0 | is1, 1.0, 0.0).astype(BF)
    row_i = lax.broadcasted_iota(jnp.int32, (count, count), 0)
    col_i = lax.broadcasted_iota(jnp.int32, (count, count), 1)
    earlier = jnp.where(col_i < row_i, 1.0, 0.0).astype(BF)
    ranks = dot(earlier, hits, 1, 0)
    for k, own in ((0, is0), (1, is1)):
        rank = jnp.sum(jnp.where(own, ranks, 0.0), 1, keepdims=True).astype(jnp.int32)
        sc_ref[:, k : k + 1] = jnp.where(rank < capacity, base_col_ref[:, k : k + 1] + rank, -1)
    expert = lax.broadcasted_iota(jnp.int32, (experts, count), 0)
    is0, is1 = expert == row_ref[0:1, :], expert == row_ref[1:2, :]
    hits = jnp.where(is0 | is1, 1.0, 0.0).astype(BF)
    later = jnp.where(row_i < col_i, 1.0, 0.0).astype(BF)
    ranks = dot(hits, later, 1, 0)
    slot_rows = []
    for k, own in ((0, is0), (1, is1)):
        rank = jnp.sum(jnp.where(own, ranks, 0.0), 0, keepdims=True).astype(jnp.int32)
        slot_rows.append(jnp.where(rank < capacity, base_row_ref[k : k + 1, :] + rank, -1))
        sr_ref[k : k + 1, :] = slot_rows[k]
    slot = lax.broadcasted_iota(jnp.int32, (slots, count), 0)
    at0 = jnp.where(slot == slot_rows[0], 1.0, 0.0).astype(BF)
    at1 = jnp.where(slot == slot_rows[1], 1.0, 0.0).astype(BF)
    both = at0 + at1
    for index, ref in enumerate(gd_refs):
        ref[...] = dot(both[index * each : (index + 1) * each], g_ref[...], 1, 0).astype(BF)
    r0 = jnp.broadcast_to(row_ref[0:1, :], (8, count)).astype(F32).astype(BF)
    r1 = jnp.broadcast_to(row_ref[1:2, :], (8, count)).astype(F32).astype(BF)
    other_ref[...] = dot(r1, at0, 1, 1) + dot(r0, at1, 1, 1)


def middle_kernel(
    tok_ref, small_ref, w_ref, col_ref, slot_ref, chunk_ref, mid_ref, gate_ref, *disp_refs, experts
):
    groups, slab, _ = tok_ref.shape
    per_group = chunk_ref.shape[0] // groups
    each = disp_refs[0].shape[0]
    count, slots = groups * slab, each * len(disp_refs)
    for group in range(groups):
        att = chunk_ref[group * per_group : (group + 1) * per_group].reshape(D, slab)
        mid_ref[group * slab : (group + 1) * slab, :] = tok_ref[group].astype(F32) + dot(
            att, w_ref[...], 0, 0
        )
    mid = mid_ref[...]
    second = (mid * rms(mid) * small_ref[1:2, :]).astype(BF)
    logits = dot(second, small_ref[ROUTER_ROW : ROUTER_ROW + experts].astype(BF), 1, 1)
    expert = lax.broadcasted_iota(jnp.int32, logits.shape, 1)
    c0 = jnp.sum(jnp.where(expert == col_ref[:, 0:1], logits, 0.0), 1, keepdims=True)
    c1 = jnp.sum(jnp.where(expert == col_ref[:, 1:2], logits, 0.0), 1, keepdims=True)
    top = jnp.maximum(c0, c1)
    e0, e1 = jnp.exp(c0 - top), jnp.exp(c1 - top)
    gate_ref[:, 0:1] = e0 / (e0 + e1)
    gate_ref[:, 1:2] = e1 / (e0 + e1)
    slot = lax.broadcasted_iota(jnp.int32, (slots, count), 0)
    at = jnp.where((slot == slot_ref[0:1, :]) | (slot == slot_ref[1:2, :]), 1.0, 0.0).astype(BF)
    for index, ref in enumerate(disp_refs):
        ref[...] = dot(at[index * each : (index + 1) * each], second, 1, 0).astype(BF)


def split_rows(me_ref, source_ref, keep_ref, send_ref):
    half, rows, _ = keep_ref.shape
    for index in range(2 * half):
        start = pl.multiple_of((me_ref[0] ^ index) * rows, 32)
        ref = send_ref if index % 2 else keep_ref
        ref[index // 2] = source_ref[pl.ds(start, rows), :].astype(BF)


def return_kernel(
    dgate_ref, slot_ref, col_ref, gate_ref, mid_ref, g_ref, small_ref, w_ref, att_ref,
    *refs, local, experts,
):
    dd_refs, refs = refs[:local], refs[local:]
    gb_refs, refs = refs[:local], refs[local:]
    dmid_ref, datt_ref, mixed_ref, narrow, total = refs
    count = mid_ref.shape[0]
    each = dd_refs[0].shape[0]
    slots = each * local
    slabs, rows, slab = att_ref.shape
    groups = count // slab
    per_group = slabs // groups
    slot = lax.broadcasted_iota(jnp.int32, (count, slots), 1)
    own = [slot == slot_ref[:, k : k + 1] for k in range(TOP)]
    at = jnp.where(own[0] | own[1], 1.0, 0.0).astype(BF)
    dsecond = 0.0
    for index, ref in enumerate(dd_refs):
        dsecond = dsecond + dot(at[:, index * each : (index + 1) * each], ref[...], 1, 0)
    dgate = [jnp.sum(jnp.where(o, dgate_ref[...], 0.0), 1, keepdims=True) for o in own]
    gate = [gate_ref[:, k : k + 1] for k in range(TOP)]
    both = gate[0] * dgate[0] + gate[1] * dgate[1]
    expert = lax.broadcasted_iota(jnp.int32, (count, experts), 1)
    dlogits = jnp.zeros((count, experts), F32)
    for k in range(TOP):
        dlogits = jnp.where(expert == col_ref[:, k : k + 1], gate[k] * (dgate[k] - both), dlogits)
    dlogits = dlogits.astype(BF)
    mid = mid_ref[...]
    r = rms(mid)
    n = mid * r
    gain = small_ref[1:2, :]
    second = (n * gain).astype(BF)
    dsecond = dsecond + dot(dlogits, small_ref[ROUTER_ROW : ROUTER_ROW + experts].astype(BF), 1, 0)
    u = dsecond * gain
    dmid = g_ref[...].astype(F32) + r * (u - n * jnp.mean(u * n, -1, keepdims=True))
    dmid_ref[...] = dmid
    dproj = dmid.astype(BF)
    for group in range(groups):
        part = dproj[group * slab : (group + 1) * slab]
        datt = dot(w_ref[...], part, 1, 1).astype(BF)
        for index in range(per_group):
            datt_ref[group * per_group + index] = datt[index * rows : (index + 1) * rows]
        att = att_ref[group * per_group : (group + 1) * per_group].reshape(D, slab)
        term = dot(att, part, 1, 0)
        if group == 0:
            total[...] = term
        else:
            total[...] += term
    narrow[...] = jnp.zeros_like(narrow)
    narrow[0:1, :] = jnp.sum(dsecond * n, 0, keepdims=True)
    for index, ref in enumerate(gb_refs):
        narrow[1 + index : 2 + index, :] = ref[...]
    narrow[ROUTER_ROW : ROUTER_ROW + experts, :] = dot(dlogits, second, 0, 0)
    mixed_ref[:, 0:D] = total[...].astype(BF)
    mixed_ref[:, D : D + 128] = narrow[...].T.astype(BF)
    mixed_ref[:, D + 128 :] = jnp.zeros((D, 128), BF)


def qkv_grad_kernel(
    me_ref, first_ref, d_ref, band_ref, mixed_ref, keep_ref, send_ref, acc, total
):
    slabs, rows, _ = d_ref.shape
    pairs = rows // 192
    half, part, _ = keep_ref.shape
    value = 0.0
    for index in range(slabs):
        value = value + dot(d_ref[index], first_ref[index], 1, 0)
    for pair in range(pairs):
        for which in range(3):
            to, source = (which * pairs + pair) * 64, pair * 192 + which * 64
            acc[to : to + 64, :] = value[source : source + 64, :]
    total[:, rows : rows + 64] = jnp.zeros((D, 64), F32)
    total[:, rows + 64 :] = mixed_ref[...].astype(F32)
    total[:, 0:rows] = acc[...].T
    row = lax.broadcasted_iota(jnp.int32, (BAND, QB), 0)
    col = lax.broadcasted_iota(jnp.int32, (BAND, QB), 1)
    near = col + (BAND - QB) - row < 128
    bucket_at = lax.broadcasted_iota(jnp.int32, (BUCKETS, 128), 0)
    lane = lax.broadcasted_iota(jnp.int32, (BUCKETS, 128), 1)
    bucket = jnp.zeros_like(lane)
    for index_b in range(1, BUCKETS):
        bucket = jnp.where(lane >= bucket_starts[index_b], index_b, bucket)
    mask = (bucket == bucket_at) & (bucket_at < BUCKETS - 1)
    flip_row = lax.broadcasted_iota(jnp.int32, (BAND, BAND), 0)
    flip_col = lax.broadcasted_iota(jnp.int32, (BAND, BAND), 1)
    flip = jnp.where(flip_row + flip_col == BAND - 1, 1.0, 0.0).astype(BF)
    sub = lax.broadcasted_iota(jnp.int32, (BUCKETS, 1), 0)
    per_owner = BUCKETS // (2 * half)
    for pair in range(pairs):
        values = jnp.where(near, band_ref[pair], 0.0)
        high = values.astype(BF)
        values = dot(flip, high, 1, 0) + dot(flip, (values - high.astype(F32)).astype(BF), 1, 0)
        values = pltpu.roll(values, 1, 1, stride=1, stride_axis=0)
        line = jnp.sum(values, 0, keepdims=True)[:, 0:128]
        sums = jnp.sum(jnp.where(mask, line, 0.0), 1, keepdims=True)
        sums = jnp.where(sub == BUCKETS - 1, -jnp.sum(sums, 0, keepdims=True), sums)
        for owner in range(2 * half):
            total[owner * part : owner * part + per_owner, rows + pair : rows + pair + 1] = sums[
                owner * per_owner : (owner + 1) * per_owner
            ]
    split_rows(me_ref, total, keep_ref, send_ref)


def last_kernel(tok_ref, small_ref, w_ref, dmid_ref, d_ref, gtok_ref, full):
    groups, slab, _ = tok_ref.shape
    slabs, rows, _ = d_ref.shape
    per_dest = rows // 192
    per_group = slabs // groups
    for group in range(groups):
        for which in range(3):
            for head in range(HEADS):
                dest = group * per_group + head // per_dest
                row = (head % per_dest) * 192 + which * 64
                to = which * D + head * 64
                full[to : to + 64, :] = d_ref[dest, row : row + 64, :]
        x = tok_ref[group].astype(F32)
        r = rms(x)
        n = x * r
        u = dot(w_ref[...], full[...], 1, 0).T * small_ref[0:1, :]
        gtok_ref[group] = dmid_ref[group * slab : (group + 1) * slab, :] + r * (
            u - n * jnp.mean(u * n, -1, keepdims=True)
        )


def finish_kernel(mine_ref, w_ref, gain_ref, *refs, pairs, experts):
    block_refs, refs = refs[:-8], refs[-8:]
    gw_ref, gnorm_ref, gbias_ref, gwo_ref, gffn_ref, grouter_ref, mixed, square = refs
    rows = gw_ref.shape[0]
    width = pairs * 64
    buckets = gbias_ref.shape[0]
    per_group = len(block_refs)
    quarter = mixed.shape[1] // per_group
    for mine in range(per_group):

        @pl.when(mine_ref[0] == mine)
        def _():
            for offset, ref in enumerate(block_refs):
                hg = mine ^ offset
                for which in range(3):
                    to = which * D + hg * width
                    gw_ref[:, to : to + width] = ref[:, which * width : (which + 1) * width].astype(F32)
                gbias_ref[:, hg * pairs : (hg + 1) * pairs] = ref[
                    0:buckets, 3 * width : 3 * width + pairs
                ].astype(F32)
                mixed[:, hg * quarter : (hg + 1) * quarter] = ref[:, 3 * width + 64 :].astype(F32)

    gnorm = jnp.sum(gw_ref[...] * w_ref[...].astype(F32), 1, keepdims=True)
    gwo_ref[...] = mixed[:, 0:D]
    square[...] = jnp.zeros_like(square)
    square[0:rows, :] = mixed[:, D : D + 128]
    square[0:rows, 1:2] = gnorm
    lines = square[...].T[:, 0:rows]
    gffn_ref[...] = lines[0:1]
    gnorm_ref[...] = lines[1:2] / gain_ref[...].astype(F32)
    grouter_ref[...] = lines[ROUTER_ROW : ROUTER_ROW + experts]


def output_kernel(mid_ref, slot_ref, gate_ref, *refs):
    back_refs, out_ref = refs[:-1], refs[-1]
    count = mid_ref.shape[0]
    each = back_refs[0].shape[0]
    slot = lax.broadcasted_iota(jnp.int32, (count, each), 1)
    total = mid_ref[...]
    for k in range(TOP):
        rows = 0.0
        for index, ref in enumerate(back_refs):
            at = jnp.where(slot + index * each == slot_ref[:, k : k + 1], 1.0, 0.0).astype(BF)
            rows = rows + dot(at, ref[...], 1, 0)
        total = total + gate_ref[:, k : k + 1] * rows
    out_ref[...] = total.astype(BF)


def expert_kernel(
    own_ref, rows_ref, g_ref, other_ref, small_ref, w_ref,
    out_ref, dd_ref, dgate_ref, dslot_ref, act_ref, dpre_ref, gb_ref, acc_out, acc_dd,
    *, index, local, experts,
):
    step, steps = pl.program_id(0), pl.num_programs(0)
    rows = rows_ref[...]

    @pl.when(step == 0)
    def _():
        own = own_ref[0] * local + index
        logits = dot(rows, small_ref[8 : 8 + experts].astype(BF), 1, 1)
        expert = lax.broadcasted_iota(jnp.int32, logits.shape, 1)
        mine = jnp.sum(jnp.where(expert == own, logits, 0.0), 1, keepdims=True)
        theirs = jnp.sum(jnp.where(expert == other_ref[...], logits, 0.0), 1, keepdims=True)
        gate = 1.0 / (1.0 + jnp.exp(theirs - mine))
        dslot = (g_ref[...].astype(F32) * gate).astype(BF)
        dslot_ref[...] = dslot
        gb_ref[...] = jnp.sum(dslot.astype(F32), 0, keepdims=True)
        acc_out[...] = jnp.zeros_like(acc_out)
        acc_dd[...] = jnp.zeros_like(acc_dd)

    w_in, w_out = w_ref[0, 0], w_ref[0, 1]
    pre = dot(rows, w_in, 1, 1)
    dact = dot(dslot_ref[...], w_out, 1, 1)
    root = math.sqrt(2 / math.pi)
    square = pre * pre
    tanh = jnp.tanh(pre * (root + (root * 0.044715) * square))
    half = 0.5 + 0.5 * tanh
    act = (pre * half).astype(BF)
    slope = half + (pre * (half - half * half)) * (2 * root + (6 * root * 0.044715) * square)
    act_ref[0] = act
    dpre = (dact * slope).astype(BF)
    dpre_ref[0] = dpre
    acc_dd[...] += dot(dpre, w_in, 1, 0)
    acc_out[...] += dot(act, w_out, 1, 0)

    @pl.when(step == steps - 1)
    def _():
        out = (acc_out[...] + small_ref[B_ROW + index : B_ROW + index + 1, :]).astype(BF)
        out_ref[...] = out
        dd_ref[...] = acc_dd[...].astype(BF)
        dgate = jnp.sum(out.astype(F32) * g_ref[...].astype(F32), 1, keepdims=True)
        dgate = jnp.broadcast_to(dgate, (dgate.shape[0], 128)).T
        high = dgate.astype(BF).astype(F32)
        middle = (dgate - high).astype(BF).astype(F32)
        line = lax.broadcasted_iota(jnp.int32, dgate.shape, 0)
        parts = jnp.where(line == 0, high, jnp.where(line == 1, middle, dgate - high - middle))
        dgate_ref[...] = parts[0:16].astype(BF)


def expert_pass(index, local, experts, own, rows, g_rows, other, small, weights):
    count, _ = rows.shape
    parts, _, units, _ = weights.shape
    token_s = pl.BlockSpec((count, D), lambda f: (0, 0))
    narrow_s = pl.BlockSpec((count, 1), lambda f: (0, 0))
    line_s = pl.BlockSpec((16, count), lambda f: (0, 0))
    weight_s = pl.BlockSpec((1, 2, units, D), lambda f: (f, 0, 0, 0))
    bias_s = pl.BlockSpec((1, D), lambda f: (0, 0))
    hidden_s = pl.BlockSpec((1, count, units), lambda f: (f, 0, 0))
    hidden = shape((parts, count, units), BF)
    return pl.pallas_call(
        functools.partial(expert_kernel, index=index, local=local, experts=experts),
        grid=(parts,),
        out_shape=(
            shape(rows.shape, BF),
            shape(rows.shape, BF),
            shape((16, count), BF),
            shape(rows.shape, BF),
            hidden,
            hidden,
            shape((1, D), F32),
        ),
        in_specs=[
            pl.BlockSpec(memory_space=pltpu.SMEM),
            token_s,
            token_s,
            narrow_s,
            pl.BlockSpec(small.shape, lambda f: (0, 0)),
            weight_s,
        ],
        out_specs=(token_s, token_s, line_s, token_s, hidden_s, hidden_s, bias_s),
        scratch_shapes=[pltpu.VMEM((count, D), F32), pltpu.VMEM((count, D), F32)],
        compiler_params=params(),
        cost_estimate=cost(10 * count * D * units * parts, 6 * D * units * parts * 2),
    )(own, rows, g_rows, other, small, weights)


def weight_kernel(*refs, local, parts):
    out_ref = refs[-1]
    for index in range(local):
        rows_ref, dslot_ref, act_ref, dpre_ref = refs[4 * index : 4 * index + 4]

        @pl.when(pl.program_id(0) // parts == index)
        def _():
            out_ref[0, 0, 0] = dot(dpre_ref[0], rows_ref[...], 0, 0).astype(BF)
            out_ref[0, 0, 1] = dot(act_ref[0], dslot_ref[...], 0, 0).astype(BF)


def weight_grads(operands):
    local = len(operands)
    count = operands[0][0].shape[0]
    parts, _, units = operands[0][2].shape
    token_s = pl.BlockSpec((count, D), lambda i: (0, 0))

    def hidden_s(index):
        return pl.BlockSpec(
            (1, count, units),
            lambda i: (jnp.clip(i - index * parts, 0, parts - 1), 0, 0),
        )

    return pl.pallas_call(
        functools.partial(weight_kernel, local=local, parts=parts),
        grid=(local * parts,),
        out_shape=shape((parts, local, 2, units, D), BF),
        in_specs=[
            spec
            for index in range(local)
            for spec in (token_s, token_s, hidden_s(index), hidden_s(index))
        ],
        out_specs=pl.BlockSpec(
            (1, 1, 2, units, D), lambda i: (lax.rem(i, parts), i // parts, 0, 0, 0)
        ),
        compiler_params=params(),
        cost_estimate=cost(1e6, 1e6),
    )(*[a for of in operands for a in of])


def spread_kernel(*refs):
    x_refs, (in_ref, out_ref) = refs[:-2], refs[-2:]
    for index, ref in enumerate(x_refs):
        in_ref[:, index, :] = ref[0].astype(F32)
        out_ref[:, index, :] = ref[1].astype(F32)


def spread_grads(owned):
    local = len(owned)
    units = owned[0].shape[1]
    rows = min(128, units)
    out_s = pl.BlockSpec((rows, local, D), lambda i: (i, 0, 0))
    return pl.pallas_call(
        spread_kernel,
        grid=(units // rows,),
        in_specs=[pl.BlockSpec((2, rows, D), lambda i: (0, i, 0))] * local,
        out_specs=(out_s, out_s),
        out_shape=[shape((units, local, D), F32)] * 2,
        compiler_params=params(),
        cost_estimate=cost(1e6, 1e6),
    )(*owned)


def after(array, *others):
    return lax.optimization_barrier((array, *others))[0]


def swap(array, axis, bit):
    size = lax.axis_size(axis)
    return lax.ppermute(array, axis, [(i, i ^ bit) for i in range(size)])


def gather_parts(array):
    bit = lax.axis_size("fsdp") // 2
    held = [(0, array)]
    while bit:
        held = held + [(off ^ bit, swap(a, "fsdp", bit)) for off, a in held]
        bit //= 2
    return [off for off, _ in held], [a for _, a in held]


def exchange(array):
    return lax.all_to_all(array, "seq", split_axis=0, concat_axis=0, tiled=True)


def add(*arrays):
    return sum(a.astype(F32) for a in arrays).astype(BF)


def fold_first(keep, send):
    send = swap(send, "fsdp", 1)
    return [add(keep[index], send[index]) for index in range(keep.shape[0])]


def fold_rest(held):
    bit = 2
    while len(held) > 1:
        held = [add(a, swap(b, "fsdp", bit)) for a, b in zip(held[::2], held[1::2])]
        bit *= 2
    return held[0]


def slabs_of_sequence(tokens, me, per_group, packed):
    slabs = lax.axis_size("seq")
    groups = tokens.shape[0]
    if (slabs, groups, per_group) == (8, 2, 4):
        mine = lax.dynamic_index_in_dim(tokens, me // 4, 0, keepdims=False)
        theirs = lax.dynamic_index_in_dim(tokens, 1 - me // 4, 0, keepdims=False)
        far = swap(theirs, "seq", 4)
        found = {0: mine, 4: far}
        for bit in (1, 2, 3):
            found[bit] = swap(mine, "seq", bit)
        far = after(far, packed, *[found[bit] for bit in (1, 2, 3)])
        for bit in (1, 2, 3):
            found[4 ^ bit] = swap(far, "seq", bit)
        return me, list(found), list(found.values())
    rows = exchange(jnp.repeat(tokens, per_group, axis=0))
    return me * 0, list(range(slabs)), [rows[index] for index in range(slabs)]


def scalar(value):
    return value.reshape(1).astype(jnp.int32)


def per_device(
    tokens, cotangent, segments, routes, norm_attn, w_qkv, w_o, rel_bias, norm_ffn, router, w_in,
    w_out, b_out,
):
    slabs, owners = lax.axis_size("seq"), lax.axis_size("fsdp")
    me = lax.axis_index("seq")
    me_f = scalar(lax.axis_index("fsdp"))
    groups, slab = tokens.shape[0], tokens.shape[1]
    count = groups * slab
    experts, local = router.shape[1], b_out.shape[0]
    capacity = max(2, 9 * count * TOP // (8 * experts))
    slots = experts * capacity
    each = slots // local
    pairs = groups * HEADS // slabs
    per_group = HEADS // pairs
    width = pairs * HEAD_DIM
    part = D // owners
    head_group = lax.rem(me, per_group)
    grad_flat = cotangent.reshape(count, D)

    pack = one_step(
        pack_kernel,
        [shape((part, D + 128 + 3 * width), BF)],
        (
            scalar(head_group), w_qkv, w_o, norm_attn[None], norm_ffn[None], rel_bias, b_out,
            router,
        ),
        1e9,
        scratch=[pltpu.VMEM((128, 256), F32)],
        smem=1,
    )[0]
    offsets, packed = gather_parts(pack)
    base, slab_offsets, slab_rows = slabs_of_sequence(tokens, me, per_group, packed[1])
    w_columns, w_o_full, small, bands = one_step(
        functools.partial(unpack_kernel, offsets=offsets, pairs=pairs),
        [
            shape((D, 3 * width), BF),
            shape((D, D), BF),
            shape((128, D), F32),
            shape((pairs, BAND, QB), F32),
        ],
        (me_f, *packed),
        3e9,
        scratch=[pltpu.VMEM((D, 128), F32)],
        smem=1,
    )

    route_col = after(routes, slab_rows[5], small).reshape(count, TOP)
    base_col = (route_col % local) * each + (route_col // local) * capacity
    slot_col, slot_row, other, *g_slots = one_step(
        functools.partial(route_kernel, experts=experts, capacity=capacity),
        [
            shape((count, TOP), jnp.int32),
            shape((TOP, count), jnp.int32),
            shape((8, slots), F32),
        ]
        + [shape((each, D), BF)] * local,
        (route_col, route_col.T, base_col, base_col.T, grad_flat),
        5e9,
    )

    def cross(array):
        return exchange(array.reshape(slabs, capacity, D)).reshape(each, D)

    ids = other[0].reshape(local, slabs, capacity).swapaxes(0, 1).reshape(slabs, 1, -1)
    ids = jnp.pad(ids.astype(BF), ((0, 0), (0, 7), (0, D - local * capacity)))
    g_all = jnp.concatenate([a.reshape(slabs, capacity, D) for a in g_slots] + [ids], 1)
    g_all = exchange(after(g_all, *slab_rows[:G_AFTER]))

    def g_part(index):
        return g_all[:, index * capacity : (index + 1) * capacity].reshape(each, D)

    def other_part(index):
        at = slice(index * capacity, (index + 1) * capacity)
        return g_all[:, local * capacity, at].reshape(each, 1).astype(jnp.int32)

    seg = lax.dynamic_slice_in_dim(segments, me // per_group, 1, 0)
    qkv, first = one_step(
        functools.partial(project_kernel, offsets=slab_offsets),
        [shape((slabs, 3 * width, slab), BF), shape((slabs, slab, D), BF)],
        (scalar(base), small, w_columns, *slab_rows),
        4 * SEQ_LEN * D * 3 * width,
        smem=1,
    )
    out, wide, lse = attention_fwd(qkv, seg, bands)
    out, g_all = lax.optimization_barrier((out, g_all))
    att = exchange(out)
    mid, gates, *disp = one_step(
        functools.partial(middle_kernel, experts=experts),
        [shape((count, D), F32), shape((count, TOP), F32)] + [shape((each, D), BF)] * local,
        (tokens, small, w_o_full, route_col, slot_row, att),
        4 * count * D * (D + slots),
    )

    relaid = jnp.stack([w_in, w_out]).transpose(2, 0, 1, 3)
    weights = [
        lax.all_gather(relaid[index], "fsdp", axis=0, tiled=False) for index in range(local)
    ]
    w_qkv_late, _ = lax.optimization_barrier((w_qkv, att))
    w_qkv_full = lax.all_gather(w_qkv_late, "fsdp", axis=0, tiled=True)
    rows, passes = [], []
    for index in range(local):
        rows.append(cross(after(disp[index], *rows)))
    big = []
    for index in range(local):
        if index:
            arrived = rows[index]
            rows[index] = after(arrived, passes[-1][1], big[-1])
            big[-1] = after(big[-1], arrived)
        passes.append(
            expert_pass(
                index, local, experts, scalar(me), rows[index], g_part(index),
                other_part(index), small, weights[index],
            )
        )
        act, dpre = passes[-1][4], passes[-1][5]
        act = after(act, passes[-1][1])
        big.append(weight_grads([(rows[index], passes[-1][3], act, dpre)]))
    results, dd, dgate, _, _, _, grad_b = map(list, zip(*passes))
    parts = jnp.stack([a[0:3] for a in dgate], 1).reshape(3 * local, slabs, capacity)
    parts = parts.swapaxes(0, 1).reshape(slabs, 1, -1)
    parts = jnp.pad(parts, ((0, 0), (0, 7), (0, D - parts.shape[2])))
    dd_back = [cross(a) for a in dd[:-1]]
    last = jnp.concatenate([dd[-1].reshape(slabs, capacity, D), parts], 1)
    last = exchange(after(last, *dd_back))
    dd_back.append(last[:, :capacity].reshape(each, D))
    parts = last[:, capacity, : 3 * local * capacity].astype(F32)
    dgate_back = jnp.sum(parts.reshape(slabs, 3, local, capacity), 1)
    dgate_back = dgate_back.swapaxes(0, 1).reshape(1, slots)
    *dd_back, big[-1] = lax.optimization_barrier((*dd_back, big[-1]))
    big = [lax.psum_scatter(a, "fsdp", scatter_dimension=0, tiled=True)[0, 0] for a in big]
    grad_w_in, grad_w_out = spread_grads(big)

    dmid, grad_att, mixed = one_step(
        functools.partial(return_kernel, local=local, experts=experts),
        [shape((count, D), F32), shape((slabs, width, slab), BF), shape((D, D + 256), BF)],
        (
            dgate_back, slot_col, route_col, gates, mid, grad_flat, small, w_o_full, att,
            *dd_back, *grad_b,
        ),
        4 * count * D * (slots + 2 * D),
        scratch=[pltpu.VMEM((128, D), F32), pltpu.VMEM((D, D), F32)],
    )
    results_back = [cross(after(results[0], *dd_back))]
    grad_heads = exchange(after(grad_att, *results_back))
    for a in results[1:]:
        results_back.append(cross(after(a, grad_heads, *results_back)))
    d_qkv, band_sums = attention_bwd(qkv, seg, bands, wide, lse, grad_heads)
    d_back = exchange(after(d_qkv, *results_back))
    output = one_step(
        output_kernel,
        (shape((count, D), BF),),
        (after(mid, d_qkv), slot_col, gates, *results_back),
        4 * count * D * slots,
    )[0].reshape(groups, slab, D)

    keep, send = one_step(
        qkv_grad_kernel,
        [shape((owners // 2, part, 3 * width + D + 320), BF)] * 2,
        (me_f, first, d_qkv, band_sums, mixed),
        4 * SEQ_LEN * D * 3 * width,
        scratch=[pltpu.VMEM((3 * width, D), F32), pltpu.VMEM((D, 3 * width + D + 320), F32)],
        smem=1,
    )
    grad_tokens = one_step(
        last_kernel,
        [shape((groups, slab, D), F32)],
        (tokens, small, w_qkv_full, dmid, after(d_back, keep, output)),
        4 * count * D * 3 * D,
        scratch=[pltpu.VMEM((3 * D, slab), BF)],
    )[0]
    folded = fold_rest(fold_first(keep, send))
    grad_qkv, mixed = folded[:, : 3 * width + 64], folded[:, 3 * width + 64 :]
    grad_b_own = mixed[:, D + 1 : D + 1 + local].astype(F32).T
    quarter = (D + 256) // per_group

    def quarter_of(offset):
        return lax.dynamic_slice_in_dim(mixed, (head_group ^ offset) * quarter, quarter, 1)

    mixed = add(quarter_of(0), *[swap(quarter_of(k), "seq", k) for k in range(1, per_group)])
    block = after(jnp.concatenate([grad_qkv, mixed], 1), grad_tokens)
    bit = per_group
    while bit < slabs:
        block = add(block, swap(block, "seq", bit))
        bit *= 2
    blocks = [block] + [swap(block, "seq", k) for k in range(1, per_group)]
    blocks[0], grad_w_in, grad_w_out = lax.optimization_barrier((blocks[0], grad_w_in, grad_w_out))
    grad_wqkv, grad_gain_attn, grad_bias, grad_wo, grad_gain_ffn, grad_router = one_step(
        functools.partial(finish_kernel, pairs=pairs, experts=experts),
        [
            shape((part, 3 * D), F32),
            shape((1, part), F32),
            shape(rel_bias.shape, F32),
            shape((part, D), F32),
            shape((1, part), F32),
            shape((experts, part), F32),
        ],
        (scalar(head_group), w_qkv, norm_attn[None], *blocks),
        1e9,
        scratch=[pltpu.VMEM((part, D + 256), F32), pltpu.VMEM((256, 128), F32)],
        smem=1,
    )
    return (
        output,
        grad_tokens,
        grad_gain_attn[0],
        grad_wqkv,
        grad_wo,
        grad_bias,
        grad_gain_ffn[0],
        grad_router.T,
        grad_w_in,
        grad_w_out,
        grad_b_own,
    )


def solution(mesh):
    in_specs = (
        P("fsdp", "seq", None),
        P("fsdp", "seq", None),
        P("fsdp", None),
        P("fsdp", "seq", None),
        P("fsdp"),
        P("fsdp", None),
        P("fsdp", None),
        P("fsdp", None),
        P("fsdp"),
        P("fsdp", None),
        P("fsdp", "seq", None),
        P("fsdp", "seq", None),
        P("seq", "fsdp"),
    )
    out_specs = (
        P("fsdp", "seq", None),
        P("fsdp", "seq", None),
        P("fsdp"),
        P("fsdp", None),
        P("fsdp", None),
        P("fsdp", None),
        P("fsdp"),
        P("fsdp", None),
        P("fsdp", "seq", None),
        P("fsdp", "seq", None),
        P("seq", "fsdp"),
    )
    return jax.shard_map(
        per_device, mesh=mesh, in_specs=in_specs, out_specs=out_specs, check_vma=False
    )
```

```python
import functools
import math

import jax
import jax.numpy as jnp
from jax import lax
from jax.experimental import pallas as pl
from jax.experimental.pallas import tpu as pltpu
from jax.sharding import PartitionSpec as P

D = 768
HEADS = 12
HEAD_DIM = 64
TOP = 2
SEQ_LEN = 2048
BUCKETS = 32
DOCS = 8
QB = 256
BAND = QB + 128
EPS = 1e-06
NEG = -1e30
F32 = jnp.float32
BF = jnp.bfloat16
bucket_starts = tuple(range(17)) + tuple(
    int(math.ceil(16 * 8 ** (step_k / 16))) for step_k in range(1, 16)
)
VMEM_MOST = 56 << 20
COST_SHARE = 1
FILLER = 0.02
G_AFTER = 8


def dot(lhs, rhs, lhs_dim, rhs_dim):
    return lax.dot_general(
        lhs, rhs, (((lhs_dim,), (rhs_dim,)), ((), ())), preferred_element_type=F32
    )


def params():
    return pltpu.CompilerParams(vmem_limit_bytes=VMEM_MOST)


def cost(flops, bytes_accessed, transcendentals=0):
    return pl.CostEstimate(
        flops=int(flops * COST_SHARE), bytes_accessed=int(bytes_accessed * COST_SHARE),
        transcendentals=int(transcendentals * COST_SHARE),
    )


def shape(dims, dtype):
    return jax.ShapeDtypeStruct(dims, dtype)


def load_pair(qkv_ref, seg_ref, qt, kt, vt):
    slabs, _, slab = qkv_ref.shape
    for index in range(slabs):
        cols = slice(index * slab, (index + 1) * slab)
        qt[0:64, cols] = qkv_ref[index, 0:64, :] * jnp.asarray(0.125, BF)
        kt[0:64, cols] = qkv_ref[index, 64:128, :]
        vt[0:64, cols] = qkv_ref[index, 128:192, :]
    row = lax.broadcasted_iota(jnp.int32, (16, SEQ_LEN), 0)
    same = seg_ref[...] == row
    kt[64:80, :] = jnp.where(same, 1.0, 0.0).astype(BF)
    qt[64:80, :] = jnp.where(same | (row >= DOCS), 0.0, NEG).astype(BF)


def key_parts(block):
    end = (block + 1) * QB
    near = max(end - BAND, 0)
    return [(near, end)] + ([(0, near)] if near > 0 else [])


def fwd_kernel(qkv_ref, seg_ref, band_ref, o_ref, wide_ref, lse_ref, qt, kt, vt, k_rows):
    slabs, _, slab = qkv_ref.shape
    load_pair(qkv_ref, seg_ref, qt, kt, vt)
    k_rows[...] = kt[...].T
    for block in range(SEQ_LEN // QB):
        start, end = block * QB, (block + 1) * QB
        query = qt[:, start:end]
        scores = []
        for low, high in key_parts(block):
            part = dot(k_rows[low:high], query, 1, 0)
            if high == end:
                part = part + band_ref[0, BAND - (high - low) :, :]
            scores.append((low, high, part))
        peak = functools.reduce(
            jnp.maximum, [jnp.max(part, 0, keepdims=True) for _, _, part in scores]
        )
        total, out = 0.0, 0.0
        for low, high, part in scores:
            terms = jnp.exp(part - peak)
            total = total + jnp.sum(terms, 0, keepdims=True)
            out = out + dot(vt[:, low:high], terms.astype(BF), 1, 0)
        wide_ref[0, :, start:end] = out * (1.0 / total)
        lse_ref[0, :, start:end] = peak + jnp.log(total)
    for index in range(slabs):
        o_ref[index] = wide_ref[0, :, index * slab : (index + 1) * slab].astype(BF)


def bwd_kernel(
    qkv_ref, seg_ref, band_ref, wide_ref, lse_ref, do_ref, d_ref, hist_ref,
    qt, kt, vt, k_rows, v_rows, do_t, dq, dk, dv,
):
    slabs, _, slab = qkv_ref.shape
    load_pair(qkv_ref, seg_ref, qt, kt, vt)
    k_rows[...] = kt[...].T
    v_rows[...] = vt[...].T
    for index in range(slabs):
        do_t[:, index * slab : (index + 1) * slab] = do_ref[index]
    dk[...] = jnp.zeros_like(dk)
    dv[...] = jnp.zeros_like(dv)
    hist_ref[...] = jnp.zeros_like(hist_ref)
    for block in range(SEQ_LEN // QB):
        start, end = block * QB, (block + 1) * QB
        query, grad = qt[:, start:end], do_t[:, start:end]
        delta = jnp.sum(grad.astype(F32) * wide_ref[0, :, start:end], 0, keepdims=True)
        lse = lse_ref[0, :, start:end]
        grad_query = 0.0
        for low, high in key_parts(block):
            part = dot(k_rows[low:high], query, 1, 0)
            off = BAND - (high - low)
            if high == end:
                part = part + band_ref[0, off:, :]
            probs = jnp.exp(part - lse)
            grad_probs = dot(v_rows[low:high], grad, 1, 0)
            grad_scores = (probs * (grad_probs - delta)).astype(BF)
            if high == end:
                hist_ref[0, off:, :] += grad_scores.astype(F32)
            dv[:, low:high] += dot(grad, probs.astype(BF), 1, 1)
            dk[:, low:high] += dot(query[0:64], grad_scores, 1, 1)
            grad_query = grad_query + dot(kt[0:64, low:high], grad_scores, 1, 0)
        dq[:, start:end] = grad_query * 0.125
    for index in range(slabs):
        cols = slice(index * slab, (index + 1) * slab)
        d_ref[index, 0:64, :] = dq[:, cols].astype(BF)
        d_ref[index, 64:128, :] = dk[:, cols].astype(BF)
        d_ref[index, 128:192, :] = dv[:, cols].astype(BF)


def attention_specs(slabs, slab):
    qkv = pl.BlockSpec((slabs, 192, slab), lambda p: (0, p, 0))
    one = pl.BlockSpec((slabs, 64, slab), lambda p: (0, p, 0))
    seg = pl.BlockSpec((1, SEQ_LEN), lambda p: (0, 0))
    band = pl.BlockSpec((1, BAND, QB), lambda p: (p, 0, 0))
    wide = pl.BlockSpec((1, 64, SEQ_LEN), lambda p: (p, 0, 0))
    lse = pl.BlockSpec((1, 1, SEQ_LEN), lambda p: (p, 0, 0))
    return qkv, one, seg, band, wide, lse


def attention_fwd(qkv, seg, bands):
    slabs, rows, slab = qkv.shape
    pairs = rows // 192
    qkv_s, one_s, seg_s, band_s, wide_s, lse_s = attention_specs(slabs, slab)
    return pl.pallas_call(
        fwd_kernel,
        grid=(pairs,),
        out_shape=(
            shape((slabs, 64 * pairs, slab), BF),
            shape((pairs, 64, SEQ_LEN), F32),
            shape((pairs, 1, SEQ_LEN), F32),
        ),
        in_specs=[qkv_s, seg_s, band_s],
        out_specs=(one_s, wide_s, lse_s),
        scratch_shapes=[
            pltpu.VMEM((80, SEQ_LEN), BF),
            pltpu.VMEM((80, SEQ_LEN), BF),
            pltpu.VMEM((64, SEQ_LEN), BF),
            pltpu.VMEM((SEQ_LEN, 80), BF),
        ],
        compiler_params=params(),
        cost_estimate=cost(pairs * 6e9, pairs * 2e6, pairs * 2.4e6),
    )(qkv, seg, bands)


def attention_bwd(qkv, seg, bands, wide, lse, grad):
    slabs, rows, slab = qkv.shape
    pairs = rows // 192
    qkv_s, one_s, seg_s, band_s, wide_s, lse_s = attention_specs(slabs, slab)
    return pl.pallas_call(
        bwd_kernel,
        grid=(pairs,),
        out_shape=(shape(qkv.shape, BF), shape((pairs, BAND, QB), F32)),
        in_specs=[qkv_s, seg_s, band_s, wide_s, lse_s, one_s],
        out_specs=(qkv_s, band_s),
        scratch_shapes=[
            pltpu.VMEM((80, SEQ_LEN), BF),
            pltpu.VMEM((80, SEQ_LEN), BF),
            pltpu.VMEM((64, SEQ_LEN), BF),
            pltpu.VMEM((SEQ_LEN, 80), BF),
            pltpu.VMEM((SEQ_LEN, 64), BF),
            pltpu.VMEM((64, SEQ_LEN), BF),
            pltpu.VMEM((64, SEQ_LEN), F32),
            pltpu.VMEM((64, SEQ_LEN), F32),
            pltpu.VMEM((64, SEQ_LEN), F32),
        ],
        compiler_params=params(),
        cost_estimate=cost(pairs * 10e9, pairs * 3e6, pairs * 2.4e6),
    )(qkv, seg, bands, wide, lse, grad)


def rms(values):
    return lax.rsqrt(jnp.mean(values * values, -1, keepdims=True) + EPS)


def one_step(kernel, outs, operands, flops, scratch=(), smem=0):
    size = sum(math.prod(a.shape) * a.dtype.itemsize for a in (*operands, *outs))
    return pl.pallas_call(
        kernel,
        out_shape=tuple(outs),
        in_specs=[pl.BlockSpec(memory_space=pltpu.SMEM)] * smem
        + [pl.BlockSpec(memory_space=pltpu.VMEM)] * (len(operands) - smem),
        out_specs=tuple([pl.BlockSpec(memory_space=pltpu.VMEM)] * len(outs)),
        scratch_shapes=list(scratch),
        compiler_params=params(),
        cost_estimate=cost(flops * FILLER, size * FILLER),
    )(*operands)


BIAS_ROW, B_ROW, ROUTER_ROW = 2, 5, 8


def pack_kernel(hg_ref, w_ref, o_ref, attn_ref, ffn_ref, bias_ref, b_ref, router_ref, out_ref, lines):
    part = o_ref.shape[0]
    local, experts = b_ref.shape[0], router_ref.shape[1]
    width = (out_ref.shape[1] - D - 128) // 3
    pairs = width // 64
    out_ref[:, 0:D] = o_ref[...]
    lines[...] = jnp.zeros_like(lines)
    lines[0:1, 0:part] = attn_ref[...].astype(F32)
    lines[1:2, 0:part] = ffn_ref[...].astype(F32)
    lines[B_ROW : B_ROW + local, 0:part] = b_ref[...].astype(F32)
    turned = lines[...].T
    column = lax.broadcasted_iota(jnp.int32, (part, 128), 1)
    router = jnp.concatenate([router_ref[...], jnp.zeros((part, 128 - experts), BF)], 1)
    router = pltpu.roll(router.astype(F32), ROUTER_ROW, 1)
    narrow = jnp.where(column < ROUTER_ROW, turned[0:part], router)
    out_ref[:, D : D + 128] = narrow.astype(BF)
    for mine in range(D // width):

        @pl.when(hg_ref[0] == mine)
        def _():
            for which in range(3):
                source, to = which * D + mine * width, D + 128 + which * width
                out_ref[:, to : to + width] = w_ref[:, source : source + width]
            out_ref[0 : bias_ref.shape[0], D + BIAS_ROW : D + BIAS_ROW + pairs] = bias_ref[
                :, mine * pairs : (mine + 1) * pairs
            ]


def unpack_kernel(me_ref, *refs, offsets, pairs):
    part_refs, (w_ref, o_ref, small_ref, band_ref, narrow) = refs[: len(offsets)], refs[len(offsets) :]
    rows = part_refs[0].shape[0]
    for offset, ref in zip(offsets, part_refs):
        at = pl.ds(pl.multiple_of((me_ref[0] ^ offset) * rows, 32), rows)
        o_ref[at, :] = ref[:, 0:D]
        narrow[at, :] = ref[:, D : D + 128].astype(F32)
        w_ref[at, :] = ref[:, D + 128 :]
    small_ref[...] = narrow[...].T
    row = lax.broadcasted_iota(jnp.int32, (BAND, QB), 0)
    col = lax.broadcasted_iota(jnp.int32, (BAND, QB), 1)
    distance = col + (BAND - QB) - row
    per_owner = BUCKETS * rows // D
    for pair in range(pairs):
        source = BIAS_ROW + pair

        def entry(index_b):
            lane = index_b // per_owner * rows + index_b % per_owner
            return small_ref[source : source + 1, lane : lane + 1]

        last = entry(BUCKETS - 1)
        table = jnp.where(distance < 0, NEG, entry(0) - last)
        for index_b in range(1, BUCKETS):
            table = jnp.where(distance >= bucket_starts[index_b], entry(index_b) - last, table)
        band_ref[pair] = table


def project_kernel(me_ref, small_ref, w_ref, *refs, offsets):
    tok_refs, (qkv_ref, first_ref) = refs[:-2], refs[-2:]
    pairs = w_ref.shape[1] // 192
    for offset, ref in zip(offsets, tok_refs):
        at = me_ref[0] ^ offset
        x = ref[...].astype(F32)
        first = (x * rms(x) * small_ref[0:1, :]).astype(BF)
        first_ref[at] = first
        result = dot(w_ref[...], first, 0, 1).astype(BF)
        for pair in range(pairs):
            for which in range(3):
                to, source = pair * 192 + which * 64, (which * pairs + pair) * 64
                qkv_ref[at, to : to + 64, :] = result[source : source + 64, :]


def route_kernel(
    col_ref, row_ref, base_col_ref, base_row_ref, g_ref, sc_ref, sr_ref, other_ref, *gd_refs,
    experts, capacity,
):
    count = col_ref.shape[0]
    each = gd_refs[0].shape[0]
    slots = each * len(gd_refs)
    r0, r1 = col_ref[:, 0:1], col_ref[:, 1:2]
    expert = lax.broadcasted_iota(jnp.int32, (count, experts), 1)
    is0, is1 = expert == r0, expert == r1
    hits = jnp.where(is0 | is1, 1.0, 0.0).astype(BF)
    row_i = lax.broadcasted_iota(jnp.int32, (count, count), 0)
    col_i = lax.broadcasted_iota(jnp.int32, (count, count), 1)
    earlier = jnp.where(col_i < row_i, 1.0, 0.0).astype(BF)
    ranks = dot(earlier, hits, 1, 0)
    for k, own in ((0, is0), (1, is1)):
        rank = jnp.sum(jnp.where(own, ranks, 0.0), 1, keepdims=True).astype(jnp.int32)
        sc_ref[:, k : k + 1] = jnp.where(rank < capacity, base_col_ref[:, k : k + 1] + rank, -1)
    expert = lax.broadcasted_iota(jnp.int32, (experts, count), 0)
    is0, is1 = expert == row_ref[0:1, :], expert == row_ref[1:2, :]
    hits = jnp.where(is0 | is1, 1.0, 0.0).astype(BF)
    later = jnp.where(row_i < col_i, 1.0, 0.0).astype(BF)
    ranks = dot(hits, later, 1, 0)
    slot_rows = []
    for k, own in ((0, is0), (1, is1)):
        rank = jnp.sum(jnp.where(own, ranks, 0.0), 0, keepdims=True).astype(jnp.int32)
        slot_rows.append(jnp.where(rank < capacity, base_row_ref[k : k + 1, :] + rank, -1))
        sr_ref[k : k + 1, :] = slot_rows[k]
    slot = lax.broadcasted_iota(jnp.int32, (slots, count), 0)
    at0 = jnp.where(slot == slot_rows[0], 1.0, 0.0).astype(BF)
    at1 = jnp.where(slot == slot_rows[1], 1.0, 0.0).astype(BF)
    both = at0 + at1
    for index, ref in enumerate(gd_refs):
        ref[...] = dot(both[index * each : (index + 1) * each], g_ref[...], 1, 0).astype(BF)
    r0 = jnp.broadcast_to(row_ref[0:1, :], (8, count)).astype(F32).astype(BF)
    r1 = jnp.broadcast_to(row_ref[1:2, :], (8, count)).astype(F32).astype(BF)
    other_ref[...] = dot(r1, at0, 1, 1) + dot(r0, at1, 1, 1)


def middle_kernel(
    tok_ref, small_ref, w_ref, col_ref, slot_ref, chunk_ref, mid_ref, gate_ref, *disp_refs, experts
):
    groups, slab, _ = tok_ref.shape
    per_group = chunk_ref.shape[0] // groups
    each = disp_refs[0].shape[0]
    count, slots = groups * slab, each * len(disp_refs)
    for group in range(groups):
        att = chunk_ref[group * per_group : (group + 1) * per_group].reshape(D, slab)
        mid_ref[group * slab : (group + 1) * slab, :] = tok_ref[group].astype(F32) + dot(
            att, w_ref[...], 0, 0
        )
    mid = mid_ref[...]
    second = (mid * rms(mid) * small_ref[1:2, :]).astype(BF)
    logits = dot(second, small_ref[ROUTER_ROW : ROUTER_ROW + experts].astype(BF), 1, 1)
    expert = lax.broadcasted_iota(jnp.int32, logits.shape, 1)
    c0 = jnp.sum(jnp.where(expert == col_ref[:, 0:1], logits, 0.0), 1, keepdims=True)
    c1 = jnp.sum(jnp.where(expert == col_ref[:, 1:2], logits, 0.0), 1, keepdims=True)
    top = jnp.maximum(c0, c1)
    e0, e1 = jnp.exp(c0 - top), jnp.exp(c1 - top)
    gate_ref[:, 0:1] = e0 / (e0 + e1)
    gate_ref[:, 1:2] = e1 / (e0 + e1)
    slot = lax.broadcasted_iota(jnp.int32, (slots, count), 0)
    at = jnp.where((slot == slot_ref[0:1, :]) | (slot == slot_ref[1:2, :]), 1.0, 0.0).astype(BF)
    for index, ref in enumerate(disp_refs):
        ref[...] = dot(at[index * each : (index + 1) * each], second, 1, 0).astype(BF)


def split_rows(me_ref, source_ref, keep_ref, send_ref):
    half, rows, _ = keep_ref.shape
    for index in range(2 * half):
        start = pl.multiple_of((me_ref[0] ^ index) * rows, 32)
        ref = send_ref if index % 2 else keep_ref
        ref[index // 2] = source_ref[pl.ds(start, rows), :].astype(BF)


def return_kernel(
    me_ref, dgate_ref, slot_ref, col_ref, gate_ref, mid_ref, g_ref, small_ref, w_ref, att_ref,
    *refs, local, experts,
):
    dd_refs, refs = refs[:local], refs[local:]
    gb_refs, refs = refs[:local], refs[local:]
    dmid_ref, datt_ref, keep_ref, send_ref, narrow, total = refs
    count = mid_ref.shape[0]
    each = dd_refs[0].shape[0]
    slots = each * local
    slabs, rows, slab = att_ref.shape
    groups = count // slab
    per_group = slabs // groups
    slot = lax.broadcasted_iota(jnp.int32, (count, slots), 1)
    own = [slot == slot_ref[:, k : k + 1] for k in range(TOP)]
    at = jnp.where(own[0] | own[1], 1.0, 0.0).astype(BF)
    dsecond = 0.0
    for index, ref in enumerate(dd_refs):
        dsecond = dsecond + dot(at[:, index * each : (index + 1) * each], ref[...], 1, 0)
    dgate = [jnp.sum(jnp.where(o, dgate_ref[...], 0.0), 1, keepdims=True) for o in own]
    gate = [gate_ref[:, k : k + 1] for k in range(TOP)]
    both = gate[0] * dgate[0] + gate[1] * dgate[1]
    expert = lax.broadcasted_iota(jnp.int32, (count, experts), 1)
    dlogits = jnp.zeros((count, experts), F32)
    for k in range(TOP):
        dlogits = jnp.where(expert == col_ref[:, k : k + 1], gate[k] * (dgate[k] - both), dlogits)
    dlogits = dlogits.astype(BF)
    mid = mid_ref[...]
    r = rms(mid)
    n = mid * r
    gain = small_ref[1:2, :]
    second = (n * gain).astype(BF)
    dsecond = dsecond + dot(dlogits, small_ref[ROUTER_ROW : ROUTER_ROW + experts].astype(BF), 1, 0)
    u = dsecond * gain
    dmid = g_ref[...].astype(F32) + r * (u - n * jnp.mean(u * n, -1, keepdims=True))
    dmid_ref[...] = dmid
    dproj = dmid.astype(BF)
    for group in range(groups):
        part = dproj[group * slab : (group + 1) * slab]
        datt = dot(w_ref[...], part, 1, 1).astype(BF)
        for index in range(per_group):
            datt_ref[group * per_group + index] = datt[index * rows : (index + 1) * rows]
        att = att_ref[group * per_group : (group + 1) * per_group].reshape(D, slab)
        term = dot(att, part, 1, 0)
        if group == 0:
            total[:, 0:D] = term
        else:
            total[:, 0:D] += term
    narrow[...] = jnp.zeros_like(narrow)
    narrow[0:1, :] = jnp.sum(dsecond * n, 0, keepdims=True)
    for index, ref in enumerate(gb_refs):
        narrow[1 + index : 2 + index, :] = ref[...]
    narrow[ROUTER_ROW : ROUTER_ROW + experts, :] = dot(dlogits, second, 0, 0)
    total[:, D : D + 128] = narrow[...].T
    total[:, D + 128 :] = jnp.zeros((D, 128), F32)
    split_rows(me_ref, total, keep_ref, send_ref)


def qkv_grad_kernel(
    me_ref, first_ref, d_ref, band_ref, keep_ref, send_ref, acc, total
):
    slabs, rows, _ = d_ref.shape
    pairs = rows // 192
    half, part, _ = keep_ref.shape
    value = 0.0
    for index in range(slabs):
        value = value + dot(d_ref[index], first_ref[index], 1, 0)
    for pair in range(pairs):
        for which in range(3):
            to, source = (which * pairs + pair) * 64, pair * 192 + which * 64
            acc[to : to + 64, :] = value[source : source + 64, :]
    total[:, rows : rows + 64] = jnp.zeros((D, 64), F32)
    total[:, 0:rows] = acc[...].T
    row = lax.broadcasted_iota(jnp.int32, (BAND, QB), 0)
    col = lax.broadcasted_iota(jnp.int32, (BAND, QB), 1)
    near = col + (BAND - QB) - row < 128
    bucket_at = lax.broadcasted_iota(jnp.int32, (BUCKETS, 128), 0)
    lane = lax.broadcasted_iota(jnp.int32, (BUCKETS, 128), 1)
    bucket = jnp.zeros_like(lane)
    for index_b in range(1, BUCKETS):
        bucket = jnp.where(lane >= bucket_starts[index_b], index_b, bucket)
    mask = (bucket == bucket_at) & (bucket_at < BUCKETS - 1)
    flip_row = lax.broadcasted_iota(jnp.int32, (BAND, BAND), 0)
    flip_col = lax.broadcasted_iota(jnp.int32, (BAND, BAND), 1)
    flip = jnp.where(flip_row + flip_col == BAND - 1, 1.0, 0.0).astype(BF)
    sub = lax.broadcasted_iota(jnp.int32, (BUCKETS, 1), 0)
    per_owner = BUCKETS // (2 * half)
    for pair in range(pairs):
        values = jnp.where(near, band_ref[pair], 0.0)
        high = values.astype(BF)
        values = dot(flip, high, 1, 0) + dot(flip, (values - high.astype(F32)).astype(BF), 1, 0)
        values = pltpu.roll(values, 1, 1, stride=1, stride_axis=0)
        line = jnp.sum(values, 0, keepdims=True)[:, 0:128]
        sums = jnp.sum(jnp.where(mask, line, 0.0), 1, keepdims=True)
        sums = jnp.where(sub == BUCKETS - 1, -jnp.sum(sums, 0, keepdims=True), sums)
        for owner in range(2 * half):
            total[owner * part : owner * part + per_owner, rows + pair : rows + pair + 1] = sums[
                owner * per_owner : (owner + 1) * per_owner
            ]
    split_rows(me_ref, total, keep_ref, send_ref)


def last_kernel(tok_ref, small_ref, w_ref, dmid_ref, d_ref, gtok_ref, full):
    groups, slab, _ = tok_ref.shape
    slabs, rows, _ = d_ref.shape
    per_dest = rows // 192
    per_group = slabs // groups
    for group in range(groups):
        for which in range(3):
            for head in range(HEADS):
                dest = group * per_group + head // per_dest
                row = (head % per_dest) * 192 + which * 64
                to = which * D + head * 64
                full[to : to + 64, :] = d_ref[dest, row : row + 64, :]
        x = tok_ref[group].astype(F32)
        r = rms(x)
        n = x * r
        u = dot(w_ref[...], full[...], 1, 0).T * small_ref[0:1, :]
        gtok_ref[group] = dmid_ref[group * slab : (group + 1) * slab, :] + r * (
            u - n * jnp.mean(u * n, -1, keepdims=True)
        )


def finish_kernel(mine_ref, w_ref, gain_ref, *refs, pairs, experts):
    block_refs, refs = refs[:-8], refs[-8:]
    gw_ref, gnorm_ref, gbias_ref, gwo_ref, gffn_ref, grouter_ref, mixed, square = refs
    rows = gw_ref.shape[0]
    width = pairs * 64
    buckets = gbias_ref.shape[0]
    per_group = len(block_refs)
    quarter = mixed.shape[1] // per_group
    for mine in range(per_group):

        @pl.when(mine_ref[0] == mine)
        def _():
            for offset, ref in enumerate(block_refs):
                hg = mine ^ offset
                for which in range(3):
                    to = which * D + hg * width
                    gw_ref[:, to : to + width] = ref[:, which * width : (which + 1) * width].astype(F32)
                gbias_ref[:, hg * pairs : (hg + 1) * pairs] = ref[
                    0:buckets, 3 * width : 3 * width + pairs
                ].astype(F32)
                mixed[:, hg * quarter : (hg + 1) * quarter] = ref[:, 3 * width + 64 :].astype(F32)

    gnorm = jnp.sum(gw_ref[...] * w_ref[...].astype(F32), 1, keepdims=True)
    gwo_ref[...] = mixed[:, 0:D]
    square[...] = jnp.zeros_like(square)
    square[0:rows, :] = mixed[:, D : D + 128]
    square[0:rows, 1:2] = gnorm
    lines = square[...].T[:, 0:rows]
    gffn_ref[...] = lines[0:1]
    gnorm_ref[...] = lines[1:2] / gain_ref[...].astype(F32)
    grouter_ref[...] = lines[ROUTER_ROW : ROUTER_ROW + experts]


def output_kernel(mid_ref, slot_ref, gate_ref, *refs):
    back_refs, out_ref = refs[:-1], refs[-1]
    count = mid_ref.shape[0]
    each = back_refs[0].shape[0]
    slot = lax.broadcasted_iota(jnp.int32, (count, each), 1)
    total = mid_ref[...]
    for k in range(TOP):
        rows = 0.0
        for index, ref in enumerate(back_refs):
            at = jnp.where(slot + index * each == slot_ref[:, k : k + 1], 1.0, 0.0).astype(BF)
            rows = rows + dot(at, ref[...], 1, 0)
        total = total + gate_ref[:, k : k + 1] * rows
    out_ref[...] = total.astype(BF)


def expert_kernel(
    own_ref, rows_ref, g_ref, other_ref, small_ref, w_ref,
    out_ref, dd_ref, dgate_ref, dslot_ref, act_ref, dpre_ref, gb_ref, acc_out, acc_dd,
    *, index, local, experts,
):
    step, steps = pl.program_id(0), pl.num_programs(0)
    rows = rows_ref[...]

    @pl.when(step == 0)
    def _():
        own = own_ref[0] * local + index
        logits = dot(rows, small_ref[8 : 8 + experts].astype(BF), 1, 1)
        expert = lax.broadcasted_iota(jnp.int32, logits.shape, 1)
        mine = jnp.sum(jnp.where(expert == own, logits, 0.0), 1, keepdims=True)
        theirs = jnp.sum(jnp.where(expert == other_ref[...], logits, 0.0), 1, keepdims=True)
        gate = 1.0 / (1.0 + jnp.exp(theirs - mine))
        dslot = (g_ref[...].astype(F32) * gate).astype(BF)
        dslot_ref[...] = dslot
        gb_ref[...] = jnp.sum(dslot.astype(F32), 0, keepdims=True)
        acc_out[...] = jnp.zeros_like(acc_out)
        acc_dd[...] = jnp.zeros_like(acc_dd)

    w_in, w_out = w_ref[0, 0], w_ref[0, 1]
    pre = dot(rows, w_in, 1, 1)
    dact = dot(dslot_ref[...], w_out, 1, 1)
    root = math.sqrt(2 / math.pi)
    square = pre * pre
    tanh = jnp.tanh(pre * (root + (root * 0.044715) * square))
    half = 0.5 + 0.5 * tanh
    act = (pre * half).astype(BF)
    slope = half + (pre * (half - half * half)) * (2 * root + (6 * root * 0.044715) * square)
    act_ref[0] = act
    dpre = (dact * slope).astype(BF)
    dpre_ref[0] = dpre
    acc_dd[...] += dot(dpre, w_in, 1, 0)
    acc_out[...] += dot(act, w_out, 1, 0)

    @pl.when(step == steps - 1)
    def _():
        out = (acc_out[...] + small_ref[B_ROW + index : B_ROW + index + 1, :]).astype(BF)
        out_ref[...] = out
        dd_ref[...] = acc_dd[...].astype(BF)
        dgate = jnp.sum(out.astype(F32) * g_ref[...].astype(F32), 1, keepdims=True)
        dgate = jnp.broadcast_to(dgate, (dgate.shape[0], 128)).T
        high = dgate.astype(BF).astype(F32)
        middle = (dgate - high).astype(BF).astype(F32)
        line = lax.broadcasted_iota(jnp.int32, dgate.shape, 0)
        parts = jnp.where(line == 0, high, jnp.where(line == 1, middle, dgate - high - middle))
        dgate_ref[...] = parts[0:16].astype(BF)


def expert_pass(index, local, experts, own, rows, g_rows, other, small, weights):
    count, _ = rows.shape
    parts, _, units, _ = weights.shape
    token_s = pl.BlockSpec((count, D), lambda f: (0, 0))
    narrow_s = pl.BlockSpec((count, 1), lambda f: (0, 0))
    line_s = pl.BlockSpec((16, count), lambda f: (0, 0))
    weight_s = pl.BlockSpec((1, 2, units, D), lambda f: (f, 0, 0, 0))
    bias_s = pl.BlockSpec((1, D), lambda f: (0, 0))
    hidden_s = pl.BlockSpec((1, count, units), lambda f: (f, 0, 0))
    hidden = shape((parts, count, units), BF)
    return pl.pallas_call(
        functools.partial(expert_kernel, index=index, local=local, experts=experts),
        grid=(parts,),
        out_shape=(
            shape(rows.shape, BF),
            shape(rows.shape, BF),
            shape((16, count), BF),
            shape(rows.shape, BF),
            hidden,
            hidden,
            shape((1, D), F32),
        ),
        in_specs=[
            pl.BlockSpec(memory_space=pltpu.SMEM),
            token_s,
            token_s,
            narrow_s,
            pl.BlockSpec(small.shape, lambda f: (0, 0)),
            weight_s,
        ],
        out_specs=(token_s, token_s, line_s, token_s, hidden_s, hidden_s, bias_s),
        scratch_shapes=[pltpu.VMEM((count, D), F32), pltpu.VMEM((count, D), F32)],
        compiler_params=params(),
        cost_estimate=cost(10 * count * D * units * parts, 6 * D * units * parts * 2),
    )(own, rows, g_rows, other, small, weights)


def weight_kernel(*refs, local, parts):
    out_ref = refs[-1]
    for index in range(local):
        rows_ref, dslot_ref, act_ref, dpre_ref = refs[4 * index : 4 * index + 4]

        @pl.when(pl.program_id(0) // parts == index)
        def _():
            out_ref[0, 0, 0] = dot(dpre_ref[0], rows_ref[...], 0, 0).astype(BF)
            out_ref[0, 0, 1] = dot(act_ref[0], dslot_ref[...], 0, 0).astype(BF)


def weight_grads(operands):
    local = len(operands)
    count = operands[0][0].shape[0]
    parts, _, units = operands[0][2].shape
    token_s = pl.BlockSpec((count, D), lambda i: (0, 0))

    def hidden_s(index):
        return pl.BlockSpec(
            (1, count, units),
            lambda i: (jnp.clip(i - index * parts, 0, parts - 1), 0, 0),
        )

    return pl.pallas_call(
        functools.partial(weight_kernel, local=local, parts=parts),
        grid=(local * parts,),
        out_shape=shape((parts, local, 2, units, D), BF),
        in_specs=[
            spec
            for index in range(local)
            for spec in (token_s, token_s, hidden_s(index), hidden_s(index))
        ],
        out_specs=pl.BlockSpec(
            (1, 1, 2, units, D), lambda i: (lax.rem(i, parts), i // parts, 0, 0, 0)
        ),
        compiler_params=params(),
        cost_estimate=cost(1e6, 1e6),
    )(*[a for of in operands for a in of])


def spread_kernel(x_ref, in_ref, out_ref):
    for index in range(x_ref.shape[0]):
        in_ref[:, index, :] = x_ref[index, 0].astype(F32)
        out_ref[:, index, :] = x_ref[index, 1].astype(F32)


def spread_grads(owned):
    local, _, units, _ = owned.shape
    rows = min(128, units)
    out_s = pl.BlockSpec((rows, local, D), lambda i: (i, 0, 0))
    return pl.pallas_call(
        spread_kernel,
        grid=(units // rows,),
        in_specs=[pl.BlockSpec((local, 2, rows, D), lambda i: (0, 0, i, 0))],
        out_specs=(out_s, out_s),
        out_shape=[shape((units, local, D), F32)] * 2,
        compiler_params=params(),
        cost_estimate=cost(1e6, 1e6),
    )(owned)


def after(array, *others):
    return lax.optimization_barrier((array, *others))[0]


def swap(array, axis, bit):
    size = lax.axis_size(axis)
    return lax.ppermute(array, axis, [(i, i ^ bit) for i in range(size)])


def gather_parts(array):
    bit = lax.axis_size("fsdp") // 2
    held = [(0, array)]
    while bit:
        held = held + [(off ^ bit, swap(a, "fsdp", bit)) for off, a in held]
        bit //= 2
    return [off for off, _ in held], [a for _, a in held]


def exchange(array):
    return lax.all_to_all(array, "seq", split_axis=0, concat_axis=0, tiled=True)


def add(*arrays):
    return sum(a.astype(F32) for a in arrays).astype(BF)


def fold_first(keep, send):
    send = swap(send, "fsdp", 1)
    return [add(keep[index], send[index]) for index in range(keep.shape[0])]


def fold_rest(held):
    bit = 2
    while len(held) > 1:
        held = [add(a, swap(b, "fsdp", bit)) for a, b in zip(held[::2], held[1::2])]
        bit *= 2
    return held[0]


def slabs_of_sequence(tokens, me, per_group, packed):
    slabs = lax.axis_size("seq")
    groups = tokens.shape[0]
    if (slabs, groups, per_group) == (8, 2, 4):
        mine = lax.dynamic_index_in_dim(tokens, me // 4, 0, keepdims=False)
        theirs = lax.dynamic_index_in_dim(tokens, 1 - me // 4, 0, keepdims=False)
        far = swap(theirs, "seq", 4)
        found = {0: mine, 4: far}
        for bit in (1, 2, 3):
            found[bit] = swap(mine, "seq", bit)
        far = after(far, packed, *[found[bit] for bit in (1, 2, 3)])
        for bit in (1, 2, 3):
            found[4 ^ bit] = swap(far, "seq", bit)
        return me, list(found), list(found.values())
    rows = exchange(jnp.repeat(tokens, per_group, axis=0))
    return me * 0, list(range(slabs)), [rows[index] for index in range(slabs)]


def scalar(value):
    return value.reshape(1).astype(jnp.int32)


def per_device(
    tokens, cotangent, segments, routes, norm_attn, w_qkv, w_o, rel_bias, norm_ffn, router, w_in,
    w_out, b_out,
):
    slabs, owners = lax.axis_size("seq"), lax.axis_size("fsdp")
    me = lax.axis_index("seq")
    me_f = scalar(lax.axis_index("fsdp"))
    groups, slab = tokens.shape[0], tokens.shape[1]
    count = groups * slab
    experts, local = router.shape[1], b_out.shape[0]
    capacity = max(2, 9 * count * TOP // (8 * experts))
    slots = experts * capacity
    each = slots // local
    pairs = groups * HEADS // slabs
    per_group = HEADS // pairs
    width = pairs * HEAD_DIM
    part = D // owners
    head_group = lax.rem(me, per_group)
    grad_flat = cotangent.reshape(count, D)

    pack = one_step(
        pack_kernel,
        [shape((part, D + 128 + 3 * width), BF)],
        (
            scalar(head_group), w_qkv, w_o, norm_attn[None], norm_ffn[None], rel_bias, b_out,
            router,
        ),
        1e9,
        scratch=[pltpu.VMEM((128, 256), F32)],
        smem=1,
    )[0]
    offsets, packed = gather_parts(pack)
    base, slab_offsets, slab_rows = slabs_of_sequence(tokens, me, per_group, packed[1])
    w_columns, w_o_full, small, bands = one_step(
        functools.partial(unpack_kernel, offsets=offsets, pairs=pairs),
        [
            shape((D, 3 * width), BF),
            shape((D, D), BF),
            shape((128, D), F32),
            shape((pairs, BAND, QB), F32),
        ],
        (me_f, *packed),
        3e9,
        scratch=[pltpu.VMEM((D, 128), F32)],
        smem=1,
    )

    route_col = after(routes, slab_rows[5], small).reshape(count, TOP)
    base_col = (route_col % local) * each + (route_col // local) * capacity
    slot_col, slot_row, other, *g_slots = one_step(
        functools.partial(route_kernel, experts=experts, capacity=capacity),
        [
            shape((count, TOP), jnp.int32),
            shape((TOP, count), jnp.int32),
            shape((8, slots), F32),
        ]
        + [shape((each, D), BF)] * local,
        (route_col, route_col.T, base_col, base_col.T, grad_flat),
        5e9,
    )

    def cross(array):
        return exchange(array.reshape(slabs, capacity, D)).reshape(each, D)

    ids = other[0].reshape(local, slabs, capacity).swapaxes(0, 1).reshape(slabs, 1, -1)
    ids = jnp.pad(ids.astype(BF), ((0, 0), (0, 7), (0, D - local * capacity)))
    g_all = jnp.concatenate([a.reshape(slabs, capacity, D) for a in g_slots] + [ids], 1)
    g_all = exchange(after(g_all, *slab_rows[:G_AFTER]))

    def g_part(index):
        return g_all[:, index * capacity : (index + 1) * capacity].reshape(each, D)

    def other_part(index):
        at = slice(index * capacity, (index + 1) * capacity)
        return g_all[:, local * capacity, at].reshape(each, 1).astype(jnp.int32)

    seg = lax.dynamic_slice_in_dim(segments, me // per_group, 1, 0)
    qkv, first = one_step(
        functools.partial(project_kernel, offsets=slab_offsets),
        [shape((slabs, 3 * width, slab), BF), shape((slabs, slab, D), BF)],
        (scalar(base), small, w_columns, *slab_rows),
        4 * SEQ_LEN * D * 3 * width,
        smem=1,
    )
    out, wide, lse = attention_fwd(qkv, seg, bands)
    out, g_all = lax.optimization_barrier((out, g_all))
    att = exchange(out)
    mid, gates, *disp = one_step(
        functools.partial(middle_kernel, experts=experts),
        [shape((count, D), F32), shape((count, TOP), F32)] + [shape((each, D), BF)] * local,
        (tokens, small, w_o_full, route_col, slot_row, att),
        4 * count * D * (D + slots),
    )

    relaid = jnp.stack([w_in, w_out]).transpose(2, 0, 1, 3)
    weights = [
        lax.all_gather(relaid[index], "fsdp", axis=0, tiled=False) for index in range(local)
    ]
    w_qkv_late, _ = lax.optimization_barrier((w_qkv, att))
    w_qkv_full = lax.all_gather(w_qkv_late, "fsdp", axis=0, tiled=True)
    rows, passes = [], []
    for index in range(local):
        rows.append(cross(after(disp[index], *rows)))
    for index in range(local):
        if index:
            rows[index] = after(rows[index], passes[-1][1])
        passes.append(
            expert_pass(
                index, local, experts, scalar(me), rows[index], g_part(index),
                other_part(index), small, weights[index],
            )
        )
    results, dd, dgate, dslot, act, dpre, grad_b = map(list, zip(*passes))
    parts = jnp.stack([a[0:3] for a in dgate], 1).reshape(3 * local, slabs, capacity)
    parts = parts.swapaxes(0, 1).reshape(slabs, 1, -1)
    parts = jnp.pad(parts, ((0, 0), (0, 7), (0, D - parts.shape[2])))
    dd_back = [cross(a) for a in dd[:-1]]
    last = jnp.concatenate([dd[-1].reshape(slabs, capacity, D), parts], 1)
    last = exchange(after(last, *dd_back))
    dd_back.append(last[:, :capacity].reshape(each, D))
    parts = last[:, capacity, : 3 * local * capacity].astype(F32)
    dgate_back = jnp.sum(parts.reshape(slabs, 3, local, capacity), 1)
    dgate_back = dgate_back.swapaxes(0, 1).reshape(1, slots)
    act = [after(a, dd[-1]) for a in act]
    big = weight_grads(list(zip(rows, dslot, act, dpre)))
    *dd_back, big = lax.optimization_barrier((*dd_back, big))
    big = lax.psum_scatter(big, "fsdp", scatter_dimension=0, tiled=True)[0]

    dmid, grad_att, keep, send = one_step(
        functools.partial(return_kernel, local=local, experts=experts),
        [shape((count, D), F32), shape((slabs, width, slab), BF)]
        + [shape((owners // 2, part, D + 256), BF)] * 2,
        (
            me_f, dgate_back, slot_col, route_col, gates, mid, grad_flat, small, w_o_full, att,
            *dd_back, *grad_b,
        ),
        4 * count * D * (slots + 2 * D),
        scratch=[pltpu.VMEM((128, D), F32), pltpu.VMEM((D, D + 256), F32)],
        smem=1,
    )
    results_back = [cross(after(results[0], *dd_back))]
    grad_heads = exchange(after(grad_att, *results_back))
    for a in results[1:]:
        results_back.append(cross(after(a, grad_heads, *results_back)))
    mixed = fold_first(after(keep, grad_heads), send)
    d_qkv, band_sums = attention_bwd(qkv, seg, bands, wide, lse, grad_heads)
    mixed[0] = after(mixed[0], d_qkv)
    mixed = fold_rest(mixed)
    d_back = exchange(after(d_qkv, *results_back))
    output = one_step(
        output_kernel,
        (shape((count, D), BF),),
        (after(mid, d_qkv), slot_col, gates, *results_back),
        4 * count * D * slots,
    )[0].reshape(groups, slab, D)

    keep, send = one_step(
        qkv_grad_kernel,
        [shape((owners // 2, part, 3 * width + 64), BF)] * 2,
        (me_f, first, d_qkv, band_sums),
        4 * SEQ_LEN * D * 3 * width,
        scratch=[pltpu.VMEM((3 * width, D), F32), pltpu.VMEM((D, 3 * width + 64), F32)],
        smem=1,
    )
    grad_tokens = one_step(
        last_kernel,
        [shape((groups, slab, D), F32)],
        (tokens, small, w_qkv_full, dmid, after(d_back, keep, output)),
        4 * count * D * 3 * D,
        scratch=[pltpu.VMEM((3 * D, slab), BF)],
    )[0]
    grad_qkv = fold_rest(fold_first(keep, send))
    grad_b_own = mixed[:, D + 1 : D + 1 + local].astype(F32).T
    quarter = (D + 256) // per_group

    def quarter_of(offset):
        return lax.dynamic_slice_in_dim(mixed, (head_group ^ offset) * quarter, quarter, 1)

    mixed = add(quarter_of(0), *[swap(quarter_of(k), "seq", k) for k in range(1, per_group)])
    block = jnp.concatenate([grad_qkv, mixed], 1)
    bit = per_group
    while bit < slabs:
        block = add(block, swap(block, "seq", bit))
        bit *= 2
    blocks = [block] + [swap(block, "seq", k) for k in range(1, per_group)]
    big = after(big, grad_tokens)
    grad_w_in, grad_w_out = spread_grads(big)
    blocks[0], grad_w_in, grad_w_out = lax.optimization_barrier((blocks[0], grad_w_in, grad_w_out))
    grad_wqkv, grad_gain_attn, grad_bias, grad_wo, grad_gain_ffn, grad_router = one_step(
        functools.partial(finish_kernel, pairs=pairs, experts=experts),
        [
            shape((part, 3 * D), F32),
            shape((1, part), F32),
            shape(rel_bias.shape, F32),
            shape((part, D), F32),
            shape((1, part), F32),
            shape((experts, part), F32),
        ],
        (scalar(head_group), w_qkv, norm_attn[None], *blocks),
        1e9,
        scratch=[pltpu.VMEM((part, D + 256), F32), pltpu.VMEM((256, 128), F32)],
        smem=1,
    )
    return (
        output,
        grad_tokens,
        grad_gain_attn[0],
        grad_wqkv,
        grad_wo,
        grad_bias,
        grad_gain_ffn[0],
        grad_router.T,
        grad_w_in,
        grad_w_out,
        grad_b_own,
    )


def solution(mesh):
    in_specs = (
        P("fsdp", "seq", None),
        P("fsdp", "seq", None),
        P("fsdp", None),
        P("fsdp", "seq", None),
        P("fsdp"),
        P("fsdp", None),
        P("fsdp", None),
        P("fsdp", None),
        P("fsdp"),
        P("fsdp", None),
        P("fsdp", "seq", None),
        P("fsdp", "seq", None),
        P("seq", "fsdp"),
    )
    out_specs = (
        P("fsdp", "seq", None),
        P("fsdp", "seq", None),
        P("fsdp"),
        P("fsdp", None),
        P("fsdp", None),
        P("fsdp", None),
        P("fsdp"),
        P("fsdp", None),
        P("fsdp", "seq", None),
        P("fsdp", "seq", None),
        P("seq", "fsdp"),
    )
    return jax.shard_map(
        per_device, mesh=mesh, in_specs=in_specs, out_specs=out_specs, check_vma=False
    )
```

```python
import functools
import math

import jax
import jax.numpy as jnp
from jax import lax
from jax.experimental import pallas as pl
from jax.experimental.pallas import tpu as pltpu
from jax.sharding import PartitionSpec as P

D = 768
HEADS = 12
HEAD_DIM = 64
TOP = 2
SEQ_LEN = 2048
BUCKETS = 32
DOCS = 8
QB = 256
BAND = QB + 128
EPS = 1e-06
NEG = -1e30
F32 = jnp.float32
BF = jnp.bfloat16
bucket_starts = tuple(range(17)) + tuple(
    int(math.ceil(16 * 8 ** (step_k / 16))) for step_k in range(1, 16)
)
VMEM_MOST = 56 << 20
COST_SHARE = 1
FILLER = 0.02
G_AFTER = 8


def dot(lhs, rhs, lhs_dim, rhs_dim):
    return lax.dot_general(
        lhs, rhs, (((lhs_dim,), (rhs_dim,)), ((), ())), preferred_element_type=F32
    )


def params():
    return pltpu.CompilerParams(vmem_limit_bytes=VMEM_MOST)


def cost(flops, bytes_accessed, transcendentals=0):
    return pl.CostEstimate(
        flops=int(flops * COST_SHARE), bytes_accessed=int(bytes_accessed * COST_SHARE),
        transcendentals=int(transcendentals * COST_SHARE),
    )


def shape(dims, dtype):
    return jax.ShapeDtypeStruct(dims, dtype)


def load_pair(qkv_ref, seg_ref, qt, kt, vt):
    slabs, _, slab = qkv_ref.shape
    for index in range(slabs):
        cols = slice(index * slab, (index + 1) * slab)
        qt[0:64, cols] = qkv_ref[index, 0:64, :] * jnp.asarray(0.125, BF)
        kt[0:64, cols] = qkv_ref[index, 64:128, :]
        vt[0:64, cols] = qkv_ref[index, 128:192, :]
    row = lax.broadcasted_iota(jnp.int32, (16, SEQ_LEN), 0)
    same = seg_ref[...] == row
    kt[64:80, :] = jnp.where(same, 1.0, 0.0).astype(BF)
    qt[64:80, :] = jnp.where(same | (row >= DOCS), 0.0, NEG).astype(BF)


def key_parts(block):
    end = (block + 1) * QB
    near = max(end - BAND, 0)
    return [(near, end)] + ([(0, near)] if near > 0 else [])


def fwd_kernel(qkv_ref, seg_ref, band_ref, o_ref, wide_ref, lse_ref, qt, kt, vt, k_rows):
    slabs, _, slab = qkv_ref.shape
    load_pair(qkv_ref, seg_ref, qt, kt, vt)
    k_rows[...] = kt[...].T
    for block in range(SEQ_LEN // QB):
        start, end = block * QB, (block + 1) * QB
        query = qt[:, start:end]
        scores = []
        for low, high in key_parts(block):
            part = dot(k_rows[low:high], query, 1, 0)
            if high == end:
                part = part + band_ref[0, BAND - (high - low) :, :]
            scores.append((low, high, part))
        peak = functools.reduce(
            jnp.maximum, [jnp.max(part, 0, keepdims=True) for _, _, part in scores]
        )
        total, out = 0.0, 0.0
        for low, high, part in scores:
            terms = jnp.exp(part - peak)
            total = total + jnp.sum(terms, 0, keepdims=True)
            out = out + dot(vt[:, low:high], terms.astype(BF), 1, 0)
        wide_ref[0, :, start:end] = out * (1.0 / total)
        lse_ref[0, :, start:end] = peak + jnp.log(total)
    for index in range(slabs):
        o_ref[index] = wide_ref[0, :, index * slab : (index + 1) * slab].astype(BF)


def bwd_kernel(
    qkv_ref, seg_ref, band_ref, wide_ref, lse_ref, do_ref, d_ref, hist_ref,
    qt, kt, vt, k_rows, v_rows, do_t, dq, dk, dv,
):
    slabs, _, slab = qkv_ref.shape
    load_pair(qkv_ref, seg_ref, qt, kt, vt)
    k_rows[...] = kt[...].T
    v_rows[...] = vt[...].T
    for index in range(slabs):
        do_t[:, index * slab : (index + 1) * slab] = do_ref[index]
    dk[...] = jnp.zeros_like(dk)
    dv[...] = jnp.zeros_like(dv)
    hist_ref[...] = jnp.zeros_like(hist_ref)
    for block in range(SEQ_LEN // QB):
        start, end = block * QB, (block + 1) * QB
        query, grad = qt[:, start:end], do_t[:, start:end]
        delta = jnp.sum(grad.astype(F32) * wide_ref[0, :, start:end], 0, keepdims=True)
        lse = lse_ref[0, :, start:end]
        grad_query = 0.0
        for low, high in key_parts(block):
            part = dot(k_rows[low:high], query, 1, 0)
            off = BAND - (high - low)
            if high == end:
                part = part + band_ref[0, off:, :]
            probs = jnp.exp(part - lse)
            grad_probs = dot(v_rows[low:high], grad, 1, 0)
            grad_scores = (probs * (grad_probs - delta)).astype(BF)
            if high == end:
                hist_ref[0, off:, :] += grad_scores.astype(F32)
            dv[:, low:high] += dot(grad, probs.astype(BF), 1, 1)
            dk[:, low:high] += dot(query[0:64], grad_scores, 1, 1)
            grad_query = grad_query + dot(kt[0:64, low:high], grad_scores, 1, 0)
        dq[:, start:end] = grad_query * 0.125
    for index in range(slabs):
        cols = slice(index * slab, (index + 1) * slab)
        d_ref[index, 0:64, :] = dq[:, cols].astype(BF)
        d_ref[index, 64:128, :] = dk[:, cols].astype(BF)
        d_ref[index, 128:192, :] = dv[:, cols].astype(BF)


def attention_specs(slabs, slab):
    qkv = pl.BlockSpec((slabs, 192, slab), lambda p: (0, p, 0))
    one = pl.BlockSpec((slabs, 64, slab), lambda p: (0, p, 0))
    seg = pl.BlockSpec((1, SEQ_LEN), lambda p: (0, 0))
    band = pl.BlockSpec((1, BAND, QB), lambda p: (p, 0, 0))
    wide = pl.BlockSpec((1, 64, SEQ_LEN), lambda p: (p, 0, 0))
    lse = pl.BlockSpec((1, 1, SEQ_LEN), lambda p: (p, 0, 0))
    return qkv, one, seg, band, wide, lse


def attention_fwd(qkv, seg, bands):
    slabs, rows, slab = qkv.shape
    pairs = rows // 192
    qkv_s, one_s, seg_s, band_s, wide_s, lse_s = attention_specs(slabs, slab)
    return pl.pallas_call(
        fwd_kernel,
        grid=(pairs,),
        out_shape=(
            shape((slabs, 64 * pairs, slab), BF),
            shape((pairs, 64, SEQ_LEN), F32),
            shape((pairs, 1, SEQ_LEN), F32),
        ),
        in_specs=[qkv_s, seg_s, band_s],
        out_specs=(one_s, wide_s, lse_s),
        scratch_shapes=[
            pltpu.VMEM((80, SEQ_LEN), BF),
            pltpu.VMEM((80, SEQ_LEN), BF),
            pltpu.VMEM((64, SEQ_LEN), BF),
            pltpu.VMEM((SEQ_LEN, 80), BF),
        ],
        compiler_params=params(),
        cost_estimate=cost(pairs * 6e9, pairs * 2e6, pairs * 2.4e6),
    )(qkv, seg, bands)


def attention_bwd(qkv, seg, bands, wide, lse, grad):
    slabs, rows, slab = qkv.shape
    pairs = rows // 192
    qkv_s, one_s, seg_s, band_s, wide_s, lse_s = attention_specs(slabs, slab)
    return pl.pallas_call(
        bwd_kernel,
        grid=(pairs,),
        out_shape=(shape(qkv.shape, BF), shape((pairs, BAND, QB), F32)),
        in_specs=[qkv_s, seg_s, band_s, wide_s, lse_s, one_s],
        out_specs=(qkv_s, band_s),
        scratch_shapes=[
            pltpu.VMEM((80, SEQ_LEN), BF),
            pltpu.VMEM((80, SEQ_LEN), BF),
            pltpu.VMEM((64, SEQ_LEN), BF),
            pltpu.VMEM((SEQ_LEN, 80), BF),
            pltpu.VMEM((SEQ_LEN, 64), BF),
            pltpu.VMEM((64, SEQ_LEN), BF),
            pltpu.VMEM((64, SEQ_LEN), F32),
            pltpu.VMEM((64, SEQ_LEN), F32),
            pltpu.VMEM((64, SEQ_LEN), F32),
        ],
        compiler_params=params(),
        cost_estimate=cost(pairs * 10e9, pairs * 3e6, pairs * 2.4e6),
    )(qkv, seg, bands, wide, lse, grad)


def rms(values):
    return lax.rsqrt(jnp.mean(values * values, -1, keepdims=True) + EPS)


def one_step(kernel, outs, operands, flops, scratch=(), smem=0):
    size = sum(math.prod(a.shape) * a.dtype.itemsize for a in (*operands, *outs))
    return pl.pallas_call(
        kernel,
        out_shape=tuple(outs),
        in_specs=[pl.BlockSpec(memory_space=pltpu.SMEM)] * smem
        + [pl.BlockSpec(memory_space=pltpu.VMEM)] * (len(operands) - smem),
        out_specs=tuple([pl.BlockSpec(memory_space=pltpu.VMEM)] * len(outs)),
        scratch_shapes=list(scratch),
        compiler_params=params(),
        cost_estimate=cost(flops * FILLER, size * FILLER),
    )(*operands)


BIAS_ROW, B_ROW, ROUTER_ROW = 2, 5, 8


def pack_kernel(hg_ref, w_ref, o_ref, attn_ref, ffn_ref, bias_ref, b_ref, router_ref, out_ref, lines):
    part = o_ref.shape[0]
    local, experts = b_ref.shape[0], router_ref.shape[0]
    width = (out_ref.shape[1] - D - 128) // 3
    pairs = width // 64
    out_ref[:, 0:D] = o_ref[...]
    lines[...] = jnp.zeros_like(lines)
    lines[0:1, 0:part] = attn_ref[...].astype(F32)
    lines[1:2, 0:part] = ffn_ref[...].astype(F32)
    lines[B_ROW : B_ROW + local, 0:part] = b_ref[...].astype(F32)
    lines[ROUTER_ROW : ROUTER_ROW + experts, 0:part] = router_ref[...].astype(F32)
    out_ref[:, D : D + 128] = lines[...].T[0:part].astype(BF)
    for mine in range(D // width):

        @pl.when(hg_ref[0] == mine)
        def _():
            for which in range(3):
                source, to = which * D + mine * width, D + 128 + which * width
                out_ref[:, to : to + width] = w_ref[:, source : source + width]
            out_ref[0 : bias_ref.shape[0], D + BIAS_ROW : D + BIAS_ROW + pairs] = bias_ref[
                :, mine * pairs : (mine + 1) * pairs
            ]


def unpack_kernel(me_ref, *refs, offsets, pairs):
    part_refs, (w_ref, o_ref, small_ref, band_ref, narrow) = refs[: len(offsets)], refs[len(offsets) :]
    rows = part_refs[0].shape[0]
    for offset, ref in zip(offsets, part_refs):
        at = pl.ds(pl.multiple_of((me_ref[0] ^ offset) * rows, 32), rows)
        o_ref[at, :] = ref[:, 0:D]
        narrow[at, :] = ref[:, D : D + 128].astype(F32)
        w_ref[at, :] = ref[:, D + 128 :]
    small_ref[...] = narrow[...].T
    row = lax.broadcasted_iota(jnp.int32, (BAND, QB), 0)
    col = lax.broadcasted_iota(jnp.int32, (BAND, QB), 1)
    distance = col + (BAND - QB) - row
    per_owner = BUCKETS * rows // D
    for pair in range(pairs):
        source = BIAS_ROW + pair

        def entry(index_b):
            lane = index_b // per_owner * rows + index_b % per_owner
            return small_ref[source : source + 1, lane : lane + 1]

        last = entry(BUCKETS - 1)
        table = jnp.where(distance < 0, NEG, entry(0) - last)
        for index_b in range(1, BUCKETS):
            table = jnp.where(distance >= bucket_starts[index_b], entry(index_b) - last, table)
        band_ref[pair] = table


def project_kernel(me_ref, small_ref, w_ref, *refs, offsets):
    tok_refs, (qkv_ref, first_ref) = refs[:-2], refs[-2:]
    pairs = w_ref.shape[1] // 192
    for offset, ref in zip(offsets, tok_refs):
        at = me_ref[0] ^ offset
        x = ref[...].astype(F32)
        first = (x * rms(x) * small_ref[0:1, :]).astype(BF)
        first_ref[at] = first
        result = dot(w_ref[...], first, 0, 1).astype(BF)
        for pair in range(pairs):
            for which in range(3):
                to, source = pair * 192 + which * 64, (which * pairs + pair) * 64
                qkv_ref[at, to : to + 64, :] = result[source : source + 64, :]


def route_kernel(
    col_ref, row_ref, base_col_ref, base_row_ref, g_ref, sc_ref, sr_ref, other_ref, *gd_refs,
    experts, capacity,
):
    count = col_ref.shape[0]
    each = gd_refs[0].shape[0]
    slots = each * len(gd_refs)
    r0, r1 = col_ref[:, 0:1], col_ref[:, 1:2]
    expert = lax.broadcasted_iota(jnp.int32, (count, experts), 1)
    is0, is1 = expert == r0, expert == r1
    hits = jnp.where(is0 | is1, 1.0, 0.0).astype(BF)
    row_i = lax.broadcasted_iota(jnp.int32, (count, count), 0)
    col_i = lax.broadcasted_iota(jnp.int32, (count, count), 1)
    earlier = jnp.where(col_i < row_i, 1.0, 0.0).astype(BF)
    ranks = dot(earlier, hits, 1, 0)
    for k, own in ((0, is0), (1, is1)):
        rank = jnp.sum(jnp.where(own, ranks, 0.0), 1, keepdims=True).astype(jnp.int32)
        sc_ref[:, k : k + 1] = jnp.where(rank < capacity, base_col_ref[:, k : k + 1] + rank, -1)
    expert = lax.broadcasted_iota(jnp.int32, (experts, count), 0)
    is0, is1 = expert == row_ref[0:1, :], expert == row_ref[1:2, :]
    hits = jnp.where(is0 | is1, 1.0, 0.0).astype(BF)
    later = jnp.where(row_i < col_i, 1.0, 0.0).astype(BF)
    ranks = dot(hits, later, 1, 0)
    slot_rows = []
    for k, own in ((0, is0), (1, is1)):
        rank = jnp.sum(jnp.where(own, ranks, 0.0), 0, keepdims=True).astype(jnp.int32)
        slot_rows.append(jnp.where(rank < capacity, base_row_ref[k : k + 1, :] + rank, -1))
        sr_ref[k : k + 1, :] = slot_rows[k]
    slot = lax.broadcasted_iota(jnp.int32, (slots, count), 0)
    at0 = jnp.where(slot == slot_rows[0], 1.0, 0.0).astype(BF)
    at1 = jnp.where(slot == slot_rows[1], 1.0, 0.0).astype(BF)
    both = at0 + at1
    for index, ref in enumerate(gd_refs):
        ref[...] = dot(both[index * each : (index + 1) * each], g_ref[...], 1, 0).astype(BF)
    r0 = jnp.broadcast_to(row_ref[0:1, :], (8, count)).astype(F32).astype(BF)
    r1 = jnp.broadcast_to(row_ref[1:2, :], (8, count)).astype(F32).astype(BF)
    other_ref[...] = dot(r1, at0, 1, 1) + dot(r0, at1, 1, 1)


def middle_kernel(
    tok_ref, small_ref, w_ref, col_ref, slot_ref, chunk_ref, mid_ref, gate_ref, *disp_refs, experts
):
    groups, slab, _ = tok_ref.shape
    per_group = chunk_ref.shape[0] // groups
    each = disp_refs[0].shape[0]
    count, slots = groups * slab, each * len(disp_refs)
    for group in range(groups):
        att = chunk_ref[group * per_group : (group + 1) * per_group].reshape(D, slab)
        mid_ref[group * slab : (group + 1) * slab, :] = tok_ref[group].astype(F32) + dot(
            att, w_ref[...], 0, 0
        )
    mid = mid_ref[...]
    second = (mid * rms(mid) * small_ref[1:2, :]).astype(BF)
    logits = dot(second, small_ref[ROUTER_ROW : ROUTER_ROW + experts].astype(BF), 1, 1)
    expert = lax.broadcasted_iota(jnp.int32, logits.shape, 1)
    c0 = jnp.sum(jnp.where(expert == col_ref[:, 0:1], logits, 0.0), 1, keepdims=True)
    c1 = jnp.sum(jnp.where(expert == col_ref[:, 1:2], logits, 0.0), 1, keepdims=True)
    top = jnp.maximum(c0, c1)
    e0, e1 = jnp.exp(c0 - top), jnp.exp(c1 - top)
    gate_ref[:, 0:1] = e0 / (e0 + e1)
    gate_ref[:, 1:2] = e1 / (e0 + e1)
    slot = lax.broadcasted_iota(jnp.int32, (slots, count), 0)
    at = jnp.where((slot == slot_ref[0:1, :]) | (slot == slot_ref[1:2, :]), 1.0, 0.0).astype(BF)
    for index, ref in enumerate(disp_refs):
        ref[...] = dot(at[index * each : (index + 1) * each], second, 1, 0).astype(BF)


def split_rows(me_ref, source_ref, keep_ref, send_ref):
    half, rows, _ = keep_ref.shape
    for index in range(2 * half):
        start = pl.multiple_of((me_ref[0] ^ index) * rows, 32)
        ref = send_ref if index % 2 else keep_ref
        ref[index // 2] = source_ref[pl.ds(start, rows), :].astype(BF)


def return_kernel(
    me_ref, dgate_ref, slot_ref, col_ref, gate_ref, mid_ref, g_ref, small_ref, w_ref, att_ref,
    *refs, local, experts,
):
    dd_refs, refs = refs[:local], refs[local:]
    gb_refs, refs = refs[:local], refs[local:]
    dmid_ref, datt_ref, keep_ref, send_ref, narrow, total = refs
    count = mid_ref.shape[0]
    each = dd_refs[0].shape[0]
    slots = each * local
    slabs, rows, slab = att_ref.shape
    groups = count // slab
    per_group = slabs // groups
    slot = lax.broadcasted_iota(jnp.int32, (count, slots), 1)
    own = [slot == slot_ref[:, k : k + 1] for k in range(TOP)]
    at = jnp.where(own[0] | own[1], 1.0, 0.0).astype(BF)
    dsecond = 0.0
    for index, ref in enumerate(dd_refs):
        dsecond = dsecond + dot(at[:, index * each : (index + 1) * each], ref[...], 1, 0)
    dgate = [jnp.sum(jnp.where(o, dgate_ref[...], 0.0), 1, keepdims=True) for o in own]
    gate = [gate_ref[:, k : k + 1] for k in range(TOP)]
    both = gate[0] * dgate[0] + gate[1] * dgate[1]
    expert = lax.broadcasted_iota(jnp.int32, (count, experts), 1)
    dlogits = jnp.zeros((count, experts), F32)
    for k in range(TOP):
        dlogits = jnp.where(expert == col_ref[:, k : k + 1], gate[k] * (dgate[k] - both), dlogits)
    dlogits = dlogits.astype(BF)
    mid = mid_ref[...]
    r = rms(mid)
    n = mid * r
    gain = small_ref[1:2, :]
    second = (n * gain).astype(BF)
    dsecond = dsecond + dot(dlogits, small_ref[ROUTER_ROW : ROUTER_ROW + experts].astype(BF), 1, 0)
    u = dsecond * gain
    dmid = g_ref[...].astype(F32) + r * (u - n * jnp.mean(u * n, -1, keepdims=True))
    dmid_ref[...] = dmid
    dproj = dmid.astype(BF)
    for group in range(groups):
        part = dproj[group * slab : (group + 1) * slab]
        datt = dot(w_ref[...], part, 1, 1).astype(BF)
        for index in range(per_group):
            datt_ref[group * per_group + index] = datt[index * rows : (index + 1) * rows]
        att = att_ref[group * per_group : (group + 1) * per_group].reshape(D, slab)
        term = dot(att, part, 1, 0)
        if group == 0:
            total[:, 0:D] = term
        else:
            total[:, 0:D] += term
    narrow[...] = jnp.zeros_like(narrow)
    narrow[0:1, :] = jnp.sum(dsecond * n, 0, keepdims=True)
    for index, ref in enumerate(gb_refs):
        narrow[1 + index : 2 + index, :] = ref[...]
    narrow[ROUTER_ROW : ROUTER_ROW + experts, :] = dot(dlogits, second, 0, 0)
    total[:, D : D + 128] = narrow[...].T
    total[:, D + 128 :] = jnp.zeros((D, 128), F32)
    split_rows(me_ref, total, keep_ref, send_ref)


def qkv_grad_kernel(
    me_ref, first_ref, d_ref, band_ref, keep_ref, send_ref, acc, total
):
    slabs, rows, _ = d_ref.shape
    pairs = rows // 192
    half, part, _ = keep_ref.shape
    value = 0.0
    for index in range(slabs):
        value = value + dot(d_ref[index], first_ref[index], 1, 0)
    for pair in range(pairs):
        for which in range(3):
            to, source = (which * pairs + pair) * 64, pair * 192 + which * 64
            acc[to : to + 64, :] = value[source : source + 64, :]
    total[:, rows : rows + 64] = jnp.zeros((D, 64), F32)
    total[:, 0:rows] = acc[...].T
    row = lax.broadcasted_iota(jnp.int32, (BAND, QB), 0)
    col = lax.broadcasted_iota(jnp.int32, (BAND, QB), 1)
    near = col + (BAND - QB) - row < 128
    bucket_at = lax.broadcasted_iota(jnp.int32, (BUCKETS, 128), 0)
    lane = lax.broadcasted_iota(jnp.int32, (BUCKETS, 128), 1)
    bucket = jnp.zeros_like(lane)
    for index_b in range(1, BUCKETS):
        bucket = jnp.where(lane >= bucket_starts[index_b], index_b, bucket)
    mask = (bucket == bucket_at) & (bucket_at < BUCKETS - 1)
    flip_row = lax.broadcasted_iota(jnp.int32, (BAND, BAND), 0)
    flip_col = lax.broadcasted_iota(jnp.int32, (BAND, BAND), 1)
    flip = jnp.where(flip_row + flip_col == BAND - 1, 1.0, 0.0).astype(BF)
    sub = lax.broadcasted_iota(jnp.int32, (BUCKETS, 1), 0)
    per_owner = BUCKETS // (2 * half)
    for pair in range(pairs):
        values = jnp.where(near, band_ref[pair], 0.0)
        high = values.astype(BF)
        values = dot(flip, high, 1, 0) + dot(flip, (values - high.astype(F32)).astype(BF), 1, 0)
        values = pltpu.roll(values, 1, 1, stride=1, stride_axis=0)
        line = jnp.sum(values, 0, keepdims=True)[:, 0:128]
        sums = jnp.sum(jnp.where(mask, line, 0.0), 1, keepdims=True)
        sums = jnp.where(sub == BUCKETS - 1, -jnp.sum(sums, 0, keepdims=True), sums)
        for owner in range(2 * half):
            total[owner * part : owner * part + per_owner, rows + pair : rows + pair + 1] = sums[
                owner * per_owner : (owner + 1) * per_owner
            ]
    split_rows(me_ref, total, keep_ref, send_ref)


def last_kernel(tok_ref, small_ref, w_ref, dmid_ref, d_ref, gtok_ref, full):
    groups, slab, _ = tok_ref.shape
    slabs, rows, _ = d_ref.shape
    per_dest = rows // 192
    per_group = slabs // groups
    for group in range(groups):
        for which in range(3):
            for head in range(HEADS):
                dest = group * per_group + head // per_dest
                row = (head % per_dest) * 192 + which * 64
                to = which * D + head * 64
                full[to : to + 64, :] = d_ref[dest, row : row + 64, :]
        x = tok_ref[group].astype(F32)
        r = rms(x)
        n = x * r
        u = dot(w_ref[...], full[...], 1, 0).T * small_ref[0:1, :]
        gtok_ref[group] = dmid_ref[group * slab : (group + 1) * slab, :] + r * (
            u - n * jnp.mean(u * n, -1, keepdims=True)
        )


def finish_kernel(mine_ref, w_ref, gain_ref, *refs, pairs, experts):
    block_refs, refs = refs[:-8], refs[-8:]
    gw_ref, gnorm_ref, gbias_ref, gwo_ref, gffn_ref, grouter_ref, mixed, square = refs
    rows = gw_ref.shape[0]
    width = pairs * 64
    buckets = gbias_ref.shape[0]
    per_group = len(block_refs)
    quarter = mixed.shape[1] // per_group
    for mine in range(per_group):

        @pl.when(mine_ref[0] == mine)
        def _():
            for offset, ref in enumerate(block_refs):
                hg = mine ^ offset
                for which in range(3):
                    to = which * D + hg * width
                    gw_ref[:, to : to + width] = ref[:, which * width : (which + 1) * width].astype(F32)
                gbias_ref[:, hg * pairs : (hg + 1) * pairs] = ref[
                    0:buckets, 3 * width : 3 * width + pairs
                ].astype(F32)
                mixed[:, hg * quarter : (hg + 1) * quarter] = ref[:, 3 * width + 64 :].astype(F32)

    gnorm = jnp.sum(gw_ref[...] * w_ref[...].astype(F32), 1, keepdims=True)
    gwo_ref[...] = mixed[:, 0:D]
    square[...] = jnp.zeros_like(square)
    square[0:rows, :] = mixed[:, D : D + 128]
    square[0:rows, 1:2] = gnorm
    lines = square[...].T[:, 0:rows]
    gffn_ref[...] = lines[0:1]
    gnorm_ref[...] = lines[1:2] / gain_ref[...].astype(F32)
    grouter_ref[...] = lines[ROUTER_ROW : ROUTER_ROW + experts]


def output_kernel(mid_ref, slot_ref, gate_ref, *refs):
    back_refs, out_ref = refs[:-1], refs[-1]
    count = mid_ref.shape[0]
    each = back_refs[0].shape[0]
    slot = lax.broadcasted_iota(jnp.int32, (count, each), 1)
    total = mid_ref[...]
    for k in range(TOP):
        rows = 0.0
        for index, ref in enumerate(back_refs):
            at = jnp.where(slot + index * each == slot_ref[:, k : k + 1], 1.0, 0.0).astype(BF)
            rows = rows + dot(at, ref[...], 1, 0)
        total = total + gate_ref[:, k : k + 1] * rows
    out_ref[...] = total.astype(BF)


def expert_kernel(
    own_ref, rows_ref, g_ref, other_ref, small_ref, w_ref,
    out_ref, dd_ref, dgate_ref, dslot_ref, act_ref, dpre_ref, gb_ref, acc_out, acc_dd,
    *, index, local, experts,
):
    step, steps = pl.program_id(0), pl.num_programs(0)
    rows = rows_ref[...]

    @pl.when(step == 0)
    def _():
        own = own_ref[0] * local + index
        logits = dot(rows, small_ref[8 : 8 + experts].astype(BF), 1, 1)
        expert = lax.broadcasted_iota(jnp.int32, logits.shape, 1)
        mine = jnp.sum(jnp.where(expert == own, logits, 0.0), 1, keepdims=True)
        theirs = jnp.sum(jnp.where(expert == other_ref[...], logits, 0.0), 1, keepdims=True)
        gate = 1.0 / (1.0 + jnp.exp(theirs - mine))
        dslot = (g_ref[...].astype(F32) * gate).astype(BF)
        dslot_ref[...] = dslot
        gb_ref[...] = jnp.sum(dslot.astype(F32), 0, keepdims=True)
        acc_out[...] = jnp.zeros_like(acc_out)
        acc_dd[...] = jnp.zeros_like(acc_dd)

    w_in, w_out = w_ref[0, 0], w_ref[0, 1]
    pre = dot(rows, w_in, 1, 1)
    dact = dot(dslot_ref[...], w_out, 1, 1)
    root = math.sqrt(2 / math.pi)
    square = pre * pre
    tanh = jnp.tanh(pre * (root + (root * 0.044715) * square))
    half = 0.5 + 0.5 * tanh
    act = (pre * half).astype(BF)
    slope = half + (pre * (half - half * half)) * (2 * root + (6 * root * 0.044715) * square)
    act_ref[0] = act
    dpre = (dact * slope).astype(BF)
    dpre_ref[0] = dpre
    acc_dd[...] += dot(dpre, w_in, 1, 0)
    acc_out[...] += dot(act, w_out, 1, 0)

    @pl.when(step == steps - 1)
    def _():
        out = (acc_out[...] + small_ref[B_ROW + index : B_ROW + index + 1, :]).astype(BF)
        out_ref[...] = out
        dd_ref[...] = acc_dd[...].astype(BF)
        dgate = jnp.sum(out.astype(F32) * g_ref[...].astype(F32), 1, keepdims=True)
        dgate = jnp.broadcast_to(dgate, (dgate.shape[0], 128)).T
        high = dgate.astype(BF).astype(F32)
        middle = (dgate - high).astype(BF).astype(F32)
        line = lax.broadcasted_iota(jnp.int32, dgate.shape, 0)
        parts = jnp.where(line == 0, high, jnp.where(line == 1, middle, dgate - high - middle))
        dgate_ref[...] = parts[0:16].astype(BF)


def expert_pass(index, local, experts, own, rows, g_rows, other, small, weights):
    count, _ = rows.shape
    parts, _, units, _ = weights.shape
    token_s = pl.BlockSpec((count, D), lambda f: (0, 0))
    narrow_s = pl.BlockSpec((count, 1), lambda f: (0, 0))
    line_s = pl.BlockSpec((16, count), lambda f: (0, 0))
    weight_s = pl.BlockSpec((1, 2, units, D), lambda f: (f, 0, 0, 0))
    bias_s = pl.BlockSpec((1, D), lambda f: (0, 0))
    hidden_s = pl.BlockSpec((1, count, units), lambda f: (f, 0, 0))
    hidden = shape((parts, count, units), BF)
    return pl.pallas_call(
        functools.partial(expert_kernel, index=index, local=local, experts=experts),
        grid=(parts,),
        out_shape=(
            shape(rows.shape, BF),
            shape(rows.shape, BF),
            shape((16, count), BF),
            shape(rows.shape, BF),
            hidden,
            hidden,
            shape((1, D), F32),
        ),
        in_specs=[
            pl.BlockSpec(memory_space=pltpu.SMEM),
            token_s,
            token_s,
            narrow_s,
            pl.BlockSpec(small.shape, lambda f: (0, 0)),
            weight_s,
        ],
        out_specs=(token_s, token_s, line_s, token_s, hidden_s, hidden_s, bias_s),
        scratch_shapes=[pltpu.VMEM((count, D), F32), pltpu.VMEM((count, D), F32)],
        compiler_params=params(),
        cost_estimate=cost(10 * count * D * units * parts, 6 * D * units * parts * 2),
    )(own, rows, g_rows, other, small, weights)


def weight_kernel(*refs, local, parts):
    out_ref = refs[-1]
    for index in range(local):
        rows_ref, dslot_ref, act_ref, dpre_ref = refs[4 * index : 4 * index + 4]

        @pl.when(pl.program_id(0) // parts == index)
        def _():
            out_ref[0, 0, 0] = dot(dpre_ref[0], rows_ref[...], 0, 0).astype(BF)
            out_ref[0, 0, 1] = dot(act_ref[0], dslot_ref[...], 0, 0).astype(BF)


def weight_grads(operands):
    local = len(operands)
    count = operands[0][0].shape[0]
    parts, _, units = operands[0][2].shape
    token_s = pl.BlockSpec((count, D), lambda i: (0, 0))

    def hidden_s(index):
        return pl.BlockSpec(
            (1, count, units),
            lambda i: (jnp.clip(i - index * parts, 0, parts - 1), 0, 0),
        )

    return pl.pallas_call(
        functools.partial(weight_kernel, local=local, parts=parts),
        grid=(local * parts,),
        out_shape=shape((parts, local, 2, units, D), BF),
        in_specs=[
            spec
            for index in range(local)
            for spec in (token_s, token_s, hidden_s(index), hidden_s(index))
        ],
        out_specs=pl.BlockSpec(
            (1, 1, 2, units, D), lambda i: (lax.rem(i, parts), i // parts, 0, 0, 0)
        ),
        compiler_params=params(),
        cost_estimate=cost(1e6, 1e6),
    )(*[a for of in operands for a in of])


def spread_kernel(x_ref, in_ref, out_ref):
    for index in range(x_ref.shape[0]):
        in_ref[:, index, :] = x_ref[index, 0].astype(F32)
        out_ref[:, index, :] = x_ref[index, 1].astype(F32)


def spread_grads(owned):
    local, _, units, _ = owned.shape
    rows = min(128, units)
    out_s = pl.BlockSpec((rows, local, D), lambda i: (i, 0, 0))
    return pl.pallas_call(
        spread_kernel,
        grid=(units // rows,),
        in_specs=[pl.BlockSpec((local, 2, rows, D), lambda i: (0, 0, i, 0))],
        out_specs=(out_s, out_s),
        out_shape=[shape((units, local, D), F32)] * 2,
        compiler_params=params(),
        cost_estimate=cost(1e6, 1e6),
    )(owned)


def after(array, *others):
    return lax.optimization_barrier((array, *others))[0]


def swap(array, axis, bit):
    size = lax.axis_size(axis)
    return lax.ppermute(array, axis, [(i, i ^ bit) for i in range(size)])


def gather_parts(array):
    bit = lax.axis_size("fsdp") // 2
    held = [(0, array)]
    while bit:
        held = held + [(off ^ bit, swap(a, "fsdp", bit)) for off, a in held]
        bit //= 2
    return [off for off, _ in held], [a for _, a in held]


def exchange(array):
    return lax.all_to_all(array, "seq", split_axis=0, concat_axis=0, tiled=True)


def add(*arrays):
    return sum(a.astype(F32) for a in arrays).astype(BF)


def fold_first(keep, send):
    send = swap(send, "fsdp", 1)
    return [add(keep[index], send[index]) for index in range(keep.shape[0])]


def fold_rest(held):
    bit = 2
    while len(held) > 1:
        held = [add(a, swap(b, "fsdp", bit)) for a, b in zip(held[::2], held[1::2])]
        bit *= 2
    return held[0]


def slabs_of_sequence(tokens, me, per_group, packed):
    slabs = lax.axis_size("seq")
    groups = tokens.shape[0]
    if (slabs, groups, per_group) == (8, 2, 4):
        mine = lax.dynamic_index_in_dim(tokens, me // 4, 0, keepdims=False)
        theirs = lax.dynamic_index_in_dim(tokens, 1 - me // 4, 0, keepdims=False)
        far = swap(theirs, "seq", 4)
        found = {0: mine, 4: far}
        for bit in (1, 2, 3):
            found[bit] = swap(mine, "seq", bit)
        far = after(far, packed, *[found[bit] for bit in (1, 2, 3)])
        for bit in (1, 2, 3):
            found[4 ^ bit] = swap(far, "seq", bit)
        return me, list(found), list(found.values())
    rows = exchange(jnp.repeat(tokens, per_group, axis=0))
    return me * 0, list(range(slabs)), [rows[index] for index in range(slabs)]


def scalar(value):
    return value.reshape(1).astype(jnp.int32)


def per_device(
    tokens, cotangent, segments, routes, norm_attn, w_qkv, w_o, rel_bias, norm_ffn, router, w_in,
    w_out, b_out,
):
    slabs, owners = lax.axis_size("seq"), lax.axis_size("fsdp")
    me = lax.axis_index("seq")
    me_f = scalar(lax.axis_index("fsdp"))
    groups, slab = tokens.shape[0], tokens.shape[1]
    count = groups * slab
    experts, local = router.shape[1], b_out.shape[0]
    capacity = max(2, 9 * count * TOP // (8 * experts))
    slots = experts * capacity
    each = slots // local
    pairs = groups * HEADS // slabs
    per_group = HEADS // pairs
    width = pairs * HEAD_DIM
    part = D // owners
    head_group = lax.rem(me, per_group)
    grad_flat = cotangent.reshape(count, D)

    pack = one_step(
        pack_kernel,
        [shape((part, D + 128 + 3 * width), BF)],
        (
            scalar(head_group), w_qkv, w_o, norm_attn[None], norm_ffn[None], rel_bias, b_out,
            router.T,
        ),
        1e9,
        scratch=[pltpu.VMEM((128, 256), F32)],
        smem=1,
    )[0]
    offsets, packed = gather_parts(pack)
    base, slab_offsets, slab_rows = slabs_of_sequence(tokens, me, per_group, packed[1])
    w_columns, w_o_full, small, bands = one_step(
        functools.partial(unpack_kernel, offsets=offsets, pairs=pairs),
        [
            shape((D, 3 * width), BF),
            shape((D, D), BF),
            shape((128, D), F32),
            shape((pairs, BAND, QB), F32),
        ],
        (me_f, *packed),
        3e9,
        scratch=[pltpu.VMEM((D, 128), F32)],
        smem=1,
    )

    route_col = after(routes, slab_rows[5], small).reshape(count, TOP)
    base_col = (route_col % local) * each + (route_col // local) * capacity
    slot_col, slot_row, other, *g_slots = one_step(
        functools.partial(route_kernel, experts=experts, capacity=capacity),
        [
            shape((count, TOP), jnp.int32),
            shape((TOP, count), jnp.int32),
            shape((8, slots), F32),
        ]
        + [shape((each, D), BF)] * local,
        (route_col, route_col.T, base_col, base_col.T, grad_flat),
        5e9,
    )

    def cross(array):
        return exchange(array.reshape(slabs, capacity, D)).reshape(each, D)

    ids = other[0].reshape(local, slabs, capacity).swapaxes(0, 1).reshape(slabs, 1, -1)
    ids = jnp.pad(ids.astype(BF), ((0, 0), (0, 7), (0, D - local * capacity)))
    g_all = jnp.concatenate([a.reshape(slabs, capacity, D) for a in g_slots] + [ids], 1)
    g_all = exchange(after(g_all, *slab_rows[:G_AFTER]))

    def g_part(index):
        return g_all[:, index * capacity : (index + 1) * capacity].reshape(each, D)

    def other_part(index):
        at = slice(index * capacity, (index + 1) * capacity)
        return g_all[:, local * capacity, at].reshape(each, 1).astype(jnp.int32)

    seg = lax.dynamic_slice_in_dim(segments, me // per_group, 1, 0)
    qkv, first = one_step(
        functools.partial(project_kernel, offsets=slab_offsets),
        [shape((slabs, 3 * width, slab), BF), shape((slabs, slab, D), BF)],
        (scalar(base), small, w_columns, *slab_rows),
        4 * SEQ_LEN * D * 3 * width,
        smem=1,
    )
    out, wide, lse = attention_fwd(qkv, seg, bands)
    out, g_all = lax.optimization_barrier((out, g_all))
    att = exchange(out)
    mid, gates, *disp = one_step(
        functools.partial(middle_kernel, experts=experts),
        [shape((count, D), F32), shape((count, TOP), F32)] + [shape((each, D), BF)] * local,
        (tokens, small, w_o_full, route_col, slot_row, att),
        4 * count * D * (D + slots),
    )

    relaid = jnp.stack([w_in, w_out]).transpose(2, 0, 1, 3)
    weights = [
        lax.all_gather(relaid[index], "fsdp", axis=0, tiled=False) for index in range(local)
    ]
    w_qkv_late, _ = lax.optimization_barrier((w_qkv, att))
    w_qkv_full = lax.all_gather(w_qkv_late, "fsdp", axis=0, tiled=True)
    rows, passes = [], []
    for index in range(local):
        rows.append(cross(after(disp[index], *rows)))
    for index in range(local):
        if index:
            rows[index] = after(rows[index], passes[-1][1])
        passes.append(
            expert_pass(
                index, local, experts, scalar(me), rows[index], g_part(index),
                other_part(index), small, weights[index],
            )
        )
    results, dd, dgate, dslot, act, dpre, grad_b = map(list, zip(*passes))
    parts = jnp.stack([a[0:3] for a in dgate], 1).reshape(3 * local, slabs, capacity)
    parts = parts.swapaxes(0, 1).reshape(slabs, 1, -1)
    parts = jnp.pad(parts, ((0, 0), (0, 7), (0, D - parts.shape[2])))
    dd_back = [cross(a) for a in dd[:-1]]
    last = jnp.concatenate([dd[-1].reshape(slabs, capacity, D), parts], 1)
    last = exchange(after(last, *dd_back))
    dd_back.append(last[:, :capacity].reshape(each, D))
    parts = last[:, capacity, : 3 * local * capacity].astype(F32)
    dgate_back = jnp.sum(parts.reshape(slabs, 3, local, capacity), 1)
    dgate_back = dgate_back.swapaxes(0, 1).reshape(1, slots)
    act = [after(a, dd[-1]) for a in act]
    big = weight_grads(list(zip(rows, dslot, act, dpre)))
    *dd_back, big = lax.optimization_barrier((*dd_back, big))
    big = lax.psum_scatter(big, "fsdp", scatter_dimension=0, tiled=True)[0]

    dmid, grad_att, keep, send = one_step(
        functools.partial(return_kernel, local=local, experts=experts),
        [shape((count, D), F32), shape((slabs, width, slab), BF)]
        + [shape((owners // 2, part, D + 256), BF)] * 2,
        (
            me_f, dgate_back, slot_col, route_col, gates, mid, grad_flat, small, w_o_full, att,
            *dd_back, *grad_b,
        ),
        4 * count * D * (slots + 2 * D),
        scratch=[pltpu.VMEM((128, D), F32), pltpu.VMEM((D, D + 256), F32)],
        smem=1,
    )
    results_back = [cross(after(results[0], *dd_back))]
    grad_heads = exchange(after(grad_att, *results_back))
    for a in results[1:]:
        results_back.append(cross(after(a, grad_heads, *results_back)))
    mixed = fold_first(after(keep, grad_heads), send)
    d_qkv, band_sums = attention_bwd(qkv, seg, bands, wide, lse, grad_heads)
    mixed[0] = after(mixed[0], d_qkv)
    mixed = fold_rest(mixed)
    d_back = exchange(after(d_qkv, *results_back))
    output = one_step(
        output_kernel,
        (shape((count, D), BF),),
        (after(mid, d_qkv), slot_col, gates, *results_back),
        4 * count * D * slots,
    )[0].reshape(groups, slab, D)

    keep, send = one_step(
        qkv_grad_kernel,
        [shape((owners // 2, part, 3 * width + 64), BF)] * 2,
        (me_f, first, d_qkv, band_sums),
        4 * SEQ_LEN * D * 3 * width,
        scratch=[pltpu.VMEM((3 * width, D), F32), pltpu.VMEM((D, 3 * width + 64), F32)],
        smem=1,
    )
    grad_tokens = one_step(
        last_kernel,
        [shape((groups, slab, D), F32)],
        (tokens, small, w_qkv_full, dmid, after(d_back, keep, output)),
        4 * count * D * 3 * D,
        scratch=[pltpu.VMEM((3 * D, slab), BF)],
    )[0]
    grad_qkv = fold_rest(fold_first(keep, send))
    grad_b_own = mixed[:, D + 1 : D + 1 + local].astype(F32).T
    quarter = (D + 256) // per_group

    def quarter_of(offset):
        return lax.dynamic_slice_in_dim(mixed, (head_group ^ offset) * quarter, quarter, 1)

    mixed = add(quarter_of(0), *[swap(quarter_of(k), "seq", k) for k in range(1, per_group)])
    block = jnp.concatenate([grad_qkv, mixed], 1)
    bit = per_group
    while bit < slabs:
        block = add(after(block, output), swap(block, "seq", bit))
        bit *= 2
    blocks = [block] + [swap(block, "seq", k) for k in range(1, per_group)]
    big = after(big, grad_tokens)
    grad_w_in, grad_w_out = spread_grads(big)
    blocks[0], grad_w_in, grad_w_out = lax.optimization_barrier((blocks[0], grad_w_in, grad_w_out))
    grad_wqkv, grad_gain_attn, grad_bias, grad_wo, grad_gain_ffn, grad_router = one_step(
        functools.partial(finish_kernel, pairs=pairs, experts=experts),
        [
            shape((part, 3 * D), F32),
            shape((1, part), F32),
            shape(rel_bias.shape, F32),
            shape((part, D), F32),
            shape((1, part), F32),
            shape((experts, part), F32),
        ],
        (scalar(head_group), w_qkv, norm_attn[None], *blocks),
        1e9,
        scratch=[pltpu.VMEM((part, D + 256), F32), pltpu.VMEM((256, 128), F32)],
        smem=1,
    )
    return (
        output,
        grad_tokens,
        grad_gain_attn[0],
        grad_wqkv,
        grad_wo,
        grad_bias,
        grad_gain_ffn[0],
        grad_router.T,
        grad_w_in,
        grad_w_out,
        grad_b_own,
    )


def solution(mesh):
    in_specs = (
        P("fsdp", "seq", None),
        P("fsdp", "seq", None),
        P("fsdp", None),
        P("fsdp", "seq", None),
        P("fsdp"),
        P("fsdp", None),
        P("fsdp", None),
        P("fsdp", None),
        P("fsdp"),
        P("fsdp", None),
        P("fsdp", "seq", None),
        P("fsdp", "seq", None),
        P("seq", "fsdp"),
    )
    out_specs = (
        P("fsdp", "seq", None),
        P("fsdp", "seq", None),
        P("fsdp"),
        P("fsdp", None),
        P("fsdp", None),
        P("fsdp", None),
        P("fsdp"),
        P("fsdp", None),
        P("fsdp", "seq", None),
        P("fsdp", "seq", None),
        P("seq", "fsdp"),
    )
    return jax.shard_map(
        per_device, mesh=mesh, in_specs=in_specs, out_specs=out_specs, check_vma=False
    )
```

```python
import functools
import math

import jax
import jax.numpy as jnp
from jax import lax
from jax.experimental import pallas as pl
from jax.experimental.pallas import tpu as pltpu
from jax.sharding import PartitionSpec as P

D = 768
HEADS = 12
HEAD_DIM = 64
TOP = 2
SEQ_LEN = 2048
BUCKETS = 32
DOCS = 8
QB = 256
BAND = QB + 128
EPS = 1e-06
NEG = -1e30
F32 = jnp.float32
BF = jnp.bfloat16
bucket_starts = tuple(range(17)) + tuple(
    int(math.ceil(16 * 8 ** (step_k / 16))) for step_k in range(1, 16)
)
VMEM_MOST = 56 << 20
COST_SHARE = 0.4
FILLER = 0.02
G_AFTER = 8


def dot(lhs, rhs, lhs_dim, rhs_dim):
    return lax.dot_general(
        lhs, rhs, (((lhs_dim,), (rhs_dim,)), ((), ())), preferred_element_type=F32
    )


def params():
    return pltpu.CompilerParams(vmem_limit_bytes=VMEM_MOST)


def cost(flops, bytes_accessed, transcendentals=0):
    return pl.CostEstimate(
        flops=int(flops * COST_SHARE), bytes_accessed=int(bytes_accessed * COST_SHARE),
        transcendentals=int(transcendentals * COST_SHARE),
    )


def shape(dims, dtype):
    return jax.ShapeDtypeStruct(dims, dtype)


def load_pair(qkv_ref, seg_ref, qt, kt, vt):
    slabs, _, slab = qkv_ref.shape
    for index in range(slabs):
        cols = slice(index * slab, (index + 1) * slab)
        qt[0:64, cols] = qkv_ref[index, 0:64, :] * jnp.asarray(0.125, BF)
        kt[0:64, cols] = qkv_ref[index, 64:128, :]
        vt[0:64, cols] = qkv_ref[index, 128:192, :]
    row = lax.broadcasted_iota(jnp.int32, (16, SEQ_LEN), 0)
    same = seg_ref[...] == row
    kt[64:80, :] = jnp.where(same, 1.0, 0.0).astype(BF)
    qt[64:80, :] = jnp.where(same | (row >= DOCS), 0.0, NEG).astype(BF)


def key_parts(block):
    end = (block + 1) * QB
    near = max(end - BAND, 0)
    return [(near, end)] + ([(0, near)] if near > 0 else [])


def fwd_kernel(qkv_ref, seg_ref, band_ref, o_ref, wide_ref, lse_ref, qt, kt, vt, k_rows):
    slabs, _, slab = qkv_ref.shape
    load_pair(qkv_ref, seg_ref, qt, kt, vt)
    k_rows[...] = kt[...].T
    for block in range(SEQ_LEN // QB):
        start, end = block * QB, (block + 1) * QB
        query = qt[:, start:end]
        scores = []
        for low, high in key_parts(block):
            part = dot(k_rows[low:high], query, 1, 0)
            if high == end:
                part = part + band_ref[0, BAND - (high - low) :, :]
            scores.append((low, high, part))
        peak = functools.reduce(
            jnp.maximum, [jnp.max(part, 0, keepdims=True) for _, _, part in scores]
        )
        total, out = 0.0, 0.0
        for low, high, part in scores:
            terms = jnp.exp(part - peak)
            total = total + jnp.sum(terms, 0, keepdims=True)
            out = out + dot(vt[:, low:high], terms.astype(BF), 1, 0)
        wide_ref[0, :, start:end] = out * (1.0 / total)
        lse_ref[0, :, start:end] = peak + jnp.log(total)
    for index in range(slabs):
        o_ref[index] = wide_ref[0, :, index * slab : (index + 1) * slab].astype(BF)


def bwd_kernel(
    qkv_ref, seg_ref, band_ref, wide_ref, lse_ref, do_ref, d_ref, hist_ref,
    qt, kt, vt, k_rows, v_rows, do_t, dq, dk, dv,
):
    slabs, _, slab = qkv_ref.shape
    load_pair(qkv_ref, seg_ref, qt, kt, vt)
    k_rows[...] = kt[...].T
    v_rows[...] = vt[...].T
    for index in range(slabs):
        do_t[:, index * slab : (index + 1) * slab] = do_ref[index]
    dk[...] = jnp.zeros_like(dk)
    dv[...] = jnp.zeros_like(dv)
    hist_ref[...] = jnp.zeros_like(hist_ref)
    for block in range(SEQ_LEN // QB):
        start, end = block * QB, (block + 1) * QB
        query, grad = qt[:, start:end], do_t[:, start:end]
        delta = jnp.sum(grad.astype(F32) * wide_ref[0, :, start:end], 0, keepdims=True)
        lse = lse_ref[0, :, start:end]
        grad_query = 0.0
        for low, high in key_parts(block):
            part = dot(k_rows[low:high], query, 1, 0)
            off = BAND - (high - low)
            if high == end:
                part = part + band_ref[0, off:, :]
            probs = jnp.exp(part - lse)
            grad_probs = dot(v_rows[low:high], grad, 1, 0)
            grad_scores = (probs * (grad_probs - delta)).astype(BF)
            if high == end:
                hist_ref[0, off:, :] += grad_scores.astype(F32)
            dv[:, low:high] += dot(grad, probs.astype(BF), 1, 1)
            dk[:, low:high] += dot(query[0:64], grad_scores, 1, 1)
            grad_query = grad_query + dot(kt[0:64, low:high], grad_scores, 1, 0)
        dq[:, start:end] = grad_query * 0.125
    for index in range(slabs):
        cols = slice(index * slab, (index + 1) * slab)
        d_ref[index, 0:64, :] = dq[:, cols].astype(BF)
        d_ref[index, 64:128, :] = dk[:, cols].astype(BF)
        d_ref[index, 128:192, :] = dv[:, cols].astype(BF)


def attention_specs(slabs, slab):
    qkv = pl.BlockSpec((slabs, 192, slab), lambda p: (0, p, 0))
    one = pl.BlockSpec((slabs, 64, slab), lambda p: (0, p, 0))
    seg = pl.BlockSpec((1, SEQ_LEN), lambda p: (0, 0))
    band = pl.BlockSpec((1, BAND, QB), lambda p: (p, 0, 0))
    wide = pl.BlockSpec((1, 64, SEQ_LEN), lambda p: (p, 0, 0))
    lse = pl.BlockSpec((1, 1, SEQ_LEN), lambda p: (p, 0, 0))
    return qkv, one, seg, band, wide, lse


def attention_fwd(qkv, seg, bands):
    slabs, rows, slab = qkv.shape
    pairs = rows // 192
    qkv_s, one_s, seg_s, band_s, wide_s, lse_s = attention_specs(slabs, slab)
    return pl.pallas_call(
        fwd_kernel,
        grid=(pairs,),
        out_shape=(
            shape((slabs, 64 * pairs, slab), BF),
            shape((pairs, 64, SEQ_LEN), F32),
            shape((pairs, 1, SEQ_LEN), F32),
        ),
        in_specs=[qkv_s, seg_s, band_s],
        out_specs=(one_s, wide_s, lse_s),
        scratch_shapes=[
            pltpu.VMEM((80, SEQ_LEN), BF),
            pltpu.VMEM((80, SEQ_LEN), BF),
            pltpu.VMEM((64, SEQ_LEN), BF),
            pltpu.VMEM((SEQ_LEN, 80), BF),
        ],
        compiler_params=params(),
        cost_estimate=cost(pairs * 6e9, pairs * 2e6, pairs * 2.4e6),
    )(qkv, seg, bands)


def attention_bwd(qkv, seg, bands, wide, lse, grad):
    slabs, rows, slab = qkv.shape
    pairs = rows // 192
    qkv_s, one_s, seg_s, band_s, wide_s, lse_s = attention_specs(slabs, slab)
    return pl.pallas_call(
        bwd_kernel,
        grid=(pairs,),
        out_shape=(shape(qkv.shape, BF), shape((pairs, BAND, QB), F32)),
        in_specs=[qkv_s, seg_s, band_s, wide_s, lse_s, one_s],
        out_specs=(qkv_s, band_s),
        scratch_shapes=[
            pltpu.VMEM((80, SEQ_LEN), BF),
            pltpu.VMEM((80, SEQ_LEN), BF),
            pltpu.VMEM((64, SEQ_LEN), BF),
            pltpu.VMEM((SEQ_LEN, 80), BF),
            pltpu.VMEM((SEQ_LEN, 64), BF),
            pltpu.VMEM((64, SEQ_LEN), BF),
            pltpu.VMEM((64, SEQ_LEN), F32),
            pltpu.VMEM((64, SEQ_LEN), F32),
            pltpu.VMEM((64, SEQ_LEN), F32),
        ],
        compiler_params=params(),
        cost_estimate=cost(pairs * 10e9, pairs * 3e6, pairs * 2.4e6),
    )(qkv, seg, bands, wide, lse, grad)


def rms(values):
    return lax.rsqrt(jnp.mean(values * values, -1, keepdims=True) + EPS)


def one_step(kernel, outs, operands, flops, scratch=(), smem=0):
    size = sum(math.prod(a.shape) * a.dtype.itemsize for a in (*operands, *outs))
    return pl.pallas_call(
        kernel,
        out_shape=tuple(outs),
        in_specs=[pl.BlockSpec(memory_space=pltpu.SMEM)] * smem
        + [pl.BlockSpec(memory_space=pltpu.VMEM)] * (len(operands) - smem),
        out_specs=tuple([pl.BlockSpec(memory_space=pltpu.VMEM)] * len(outs)),
        scratch_shapes=list(scratch),
        compiler_params=params(),
        cost_estimate=cost(flops * FILLER, size * FILLER),
    )(*operands)


BIAS_ROW, B_ROW, ROUTER_ROW = 2, 5, 8


def pack_kernel(hg_ref, w_ref, o_ref, attn_ref, ffn_ref, bias_ref, b_ref, router_ref, out_ref, lines):
    part = o_ref.shape[0]
    local, experts = b_ref.shape[0], router_ref.shape[0]
    width = (out_ref.shape[1] - D - 128) // 3
    pairs = width // 64
    out_ref[:, 0:D] = o_ref[...]
    lines[...] = jnp.zeros_like(lines)
    lines[0:1, 0:part] = attn_ref[...].astype(F32)
    lines[1:2, 0:part] = ffn_ref[...].astype(F32)
    lines[B_ROW : B_ROW + local, 0:part] = b_ref[...].astype(F32)
    lines[ROUTER_ROW : ROUTER_ROW + experts, 0:part] = router_ref[...].astype(F32)
    out_ref[:, D : D + 128] = lines[...].T[0:part].astype(BF)
    for mine in range(D // width):

        @pl.when(hg_ref[0] == mine)
        def _():
            for which in range(3):
                source, to = which * D + mine * width, D + 128 + which * width
                out_ref[:, to : to + width] = w_ref[:, source : source + width]
            out_ref[0 : bias_ref.shape[0], D + BIAS_ROW : D + BIAS_ROW + pairs] = bias_ref[
                :, mine * pairs : (mine + 1) * pairs
            ]


def unpack_kernel(me_ref, *refs, offsets, pairs):
    part_refs, (w_ref, o_ref, small_ref, band_ref, narrow) = refs[: len(offsets)], refs[len(offsets) :]
    rows = part_refs[0].shape[0]
    for offset, ref in zip(offsets, part_refs):
        at = pl.ds(pl.multiple_of((me_ref[0] ^ offset) * rows, 32), rows)
        o_ref[at, :] = ref[:, 0:D]
        narrow[at, :] = ref[:, D : D + 128].astype(F32)
        w_ref[at, :] = ref[:, D + 128 :]
    small_ref[...] = narrow[...].T
    row = lax.broadcasted_iota(jnp.int32, (BAND, QB), 0)
    col = lax.broadcasted_iota(jnp.int32, (BAND, QB), 1)
    distance = col + (BAND - QB) - row
    per_owner = BUCKETS * rows // D
    for pair in range(pairs):
        source = BIAS_ROW + pair

        def entry(index_b):
            lane = index_b // per_owner * rows + index_b % per_owner
            return small_ref[source : source + 1, lane : lane + 1]

        last = entry(BUCKETS - 1)
        table = jnp.where(distance < 0, NEG, entry(0) - last)
        for index_b in range(1, BUCKETS):
            table = jnp.where(distance >= bucket_starts[index_b], entry(index_b) - last, table)
        band_ref[pair] = table


def project_kernel(me_ref, small_ref, w_ref, *refs, offsets):
    tok_refs, (qkv_ref, first_ref) = refs[:-2], refs[-2:]
    pairs = w_ref.shape[1] // 192
    for offset, ref in zip(offsets, tok_refs):
        at = me_ref[0] ^ offset
        x = ref[...].astype(F32)
        first = (x * rms(x) * small_ref[0:1, :]).astype(BF)
        first_ref[at] = first
        result = dot(w_ref[...], first, 0, 1).astype(BF)
        for pair in range(pairs):
            for which in range(3):
                to, source = pair * 192 + which * 64, (which * pairs + pair) * 64
                qkv_ref[at, to : to + 64, :] = result[source : source + 64, :]


def route_kernel(
    col_ref, row_ref, base_col_ref, base_row_ref, g_ref, sc_ref, sr_ref, other_ref, *gd_refs,
    experts, capacity,
):
    count = col_ref.shape[0]
    each = gd_refs[0].shape[0]
    slots = each * len(gd_refs)
    r0, r1 = col_ref[:, 0:1], col_ref[:, 1:2]
    expert = lax.broadcasted_iota(jnp.int32, (count, experts), 1)
    is0, is1 = expert == r0, expert == r1
    hits = jnp.where(is0 | is1, 1.0, 0.0).astype(BF)
    row_i = lax.broadcasted_iota(jnp.int32, (count, count), 0)
    col_i = lax.broadcasted_iota(jnp.int32, (count, count), 1)
    earlier = jnp.where(col_i < row_i, 1.0, 0.0).astype(BF)
    ranks = dot(earlier, hits, 1, 0)
    for k, own in ((0, is0), (1, is1)):
        rank = jnp.sum(jnp.where(own, ranks, 0.0), 1, keepdims=True).astype(jnp.int32)
        sc_ref[:, k : k + 1] = jnp.where(rank < capacity, base_col_ref[:, k : k + 1] + rank, -1)
    expert = lax.broadcasted_iota(jnp.int32, (experts, count), 0)
    is0, is1 = expert == row_ref[0:1, :], expert == row_ref[1:2, :]
    hits = jnp.where(is0 | is1, 1.0, 0.0).astype(BF)
    later = jnp.where(row_i < col_i, 1.0, 0.0).astype(BF)
    ranks = dot(hits, later, 1, 0)
    slot_rows = []
    for k, own in ((0, is0), (1, is1)):
        rank = jnp.sum(jnp.where(own, ranks, 0.0), 0, keepdims=True).astype(jnp.int32)
        slot_rows.append(jnp.where(rank < capacity, base_row_ref[k : k + 1, :] + rank, -1))
        sr_ref[k : k + 1, :] = slot_rows[k]
    slot = lax.broadcasted_iota(jnp.int32, (slots, count), 0)
    at0 = jnp.where(slot == slot_rows[0], 1.0, 0.0).astype(BF)
    at1 = jnp.where(slot == slot_rows[1], 1.0, 0.0).astype(BF)
    both = at0 + at1
    for index, ref in enumerate(gd_refs):
        ref[...] = dot(both[index * each : (index + 1) * each], g_ref[...], 1, 0).astype(BF)
    r0 = jnp.broadcast_to(row_ref[0:1, :], (8, count)).astype(F32).astype(BF)
    r1 = jnp.broadcast_to(row_ref[1:2, :], (8, count)).astype(F32).astype(BF)
    other_ref[...] = dot(r1, at0, 1, 1) + dot(r0, at1, 1, 1)


def middle_kernel(
    tok_ref, small_ref, w_ref, col_ref, slot_ref, chunk_ref, mid_ref, gate_ref, *disp_refs, experts
):
    groups, slab, _ = tok_ref.shape
    per_group = chunk_ref.shape[0] // groups
    each = disp_refs[0].shape[0]
    count, slots = groups * slab, each * len(disp_refs)
    for group in range(groups):
        att = chunk_ref[group * per_group : (group + 1) * per_group].reshape(D, slab)
        mid_ref[group * slab : (group + 1) * slab, :] = tok_ref[group].astype(F32) + dot(
            att, w_ref[...], 0, 0
        )
    mid = mid_ref[...]
    second = (mid * rms(mid) * small_ref[1:2, :]).astype(BF)
    logits = dot(second, small_ref[ROUTER_ROW : ROUTER_ROW + experts].astype(BF), 1, 1)
    expert = lax.broadcasted_iota(jnp.int32, logits.shape, 1)
    c0 = jnp.sum(jnp.where(expert == col_ref[:, 0:1], logits, 0.0), 1, keepdims=True)
    c1 = jnp.sum(jnp.where(expert == col_ref[:, 1:2], logits, 0.0), 1, keepdims=True)
    top = jnp.maximum(c0, c1)
    e0, e1 = jnp.exp(c0 - top), jnp.exp(c1 - top)
    gate_ref[:, 0:1] = e0 / (e0 + e1)
    gate_ref[:, 1:2] = e1 / (e0 + e1)
    slot = lax.broadcasted_iota(jnp.int32, (slots, count), 0)
    at = jnp.where((slot == slot_ref[0:1, :]) | (slot == slot_ref[1:2, :]), 1.0, 0.0).astype(BF)
    for index, ref in enumerate(disp_refs):
        ref[...] = dot(at[index * each : (index + 1) * each], second, 1, 0).astype(BF)


def split_rows(me_ref, source_ref, keep_ref, send_ref):
    half, rows, _ = keep_ref.shape
    for index in range(2 * half):
        start = pl.multiple_of((me_ref[0] ^ index) * rows, 32)
        ref = send_ref if index % 2 else keep_ref
        ref[index // 2] = source_ref[pl.ds(start, rows), :].astype(BF)


def return_kernel(
    me_ref, dgate_ref, slot_ref, col_ref, gate_ref, mid_ref, g_ref, small_ref, w_ref, att_ref,
    *refs, local, experts,
):
    dd_refs, refs = refs[:local], refs[local:]
    gb_refs, refs = refs[:local], refs[local:]
    dmid_ref, datt_ref, keep_ref, send_ref, narrow, total = refs
    count = mid_ref.shape[0]
    each = dd_refs[0].shape[0]
    slots = each * local
    slabs, rows, slab = att_ref.shape
    groups = count // slab
    per_group = slabs // groups
    slot = lax.broadcasted_iota(jnp.int32, (count, slots), 1)
    own = [slot == slot_ref[:, k : k + 1] for k in range(TOP)]
    at = jnp.where(own[0] | own[1], 1.0, 0.0).astype(BF)
    dsecond = 0.0
    for index, ref in enumerate(dd_refs):
        dsecond = dsecond + dot(at[:, index * each : (index + 1) * each], ref[...], 1, 0)
    dgate = [jnp.sum(jnp.where(o, dgate_ref[...], 0.0), 1, keepdims=True) for o in own]
    gate = [gate_ref[:, k : k + 1] for k in range(TOP)]
    both = gate[0] * dgate[0] + gate[1] * dgate[1]
    expert = lax.broadcasted_iota(jnp.int32, (count, experts), 1)
    dlogits = jnp.zeros((count, experts), F32)
    for k in range(TOP):
        dlogits = jnp.where(expert == col_ref[:, k : k + 1], gate[k] * (dgate[k] - both), dlogits)
    dlogits = dlogits.astype(BF)
    mid = mid_ref[...]
    r = rms(mid)
    n = mid * r
    gain = small_ref[1:2, :]
    second = (n * gain).astype(BF)
    dsecond = dsecond + dot(dlogits, small_ref[ROUTER_ROW : ROUTER_ROW + experts].astype(BF), 1, 0)
    u = dsecond * gain
    dmid = g_ref[...].astype(F32) + r * (u - n * jnp.mean(u * n, -1, keepdims=True))
    dmid_ref[...] = dmid
    dproj = dmid.astype(BF)
    for group in range(groups):
        part = dproj[group * slab : (group + 1) * slab]
        datt = dot(w_ref[...], part, 1, 1).astype(BF)
        for index in range(per_group):
            datt_ref[group * per_group + index] = datt[index * rows : (index + 1) * rows]
        att = att_ref[group * per_group : (group + 1) * per_group].reshape(D, slab)
        term = dot(att, part, 1, 0)
        if group == 0:
            total[:, 0:D] = term
        else:
            total[:, 0:D] += term
    narrow[...] = jnp.zeros_like(narrow)
    narrow[0:1, :] = jnp.sum(dsecond * n, 0, keepdims=True)
    for index, ref in enumerate(gb_refs):
        narrow[1 + index : 2 + index, :] = ref[...]
    narrow[ROUTER_ROW : ROUTER_ROW + experts, :] = dot(dlogits, second, 0, 0)
    total[:, D : D + 128] = narrow[...].T
    total[:, D + 128 :] = jnp.zeros((D, 128), F32)
    split_rows(me_ref, total, keep_ref, send_ref)


def qkv_grad_kernel(
    me_ref, first_ref, d_ref, band_ref, keep_ref, send_ref, acc, total
):
    slabs, rows, _ = d_ref.shape
    pairs = rows // 192
    half, part, _ = keep_ref.shape
    value = 0.0
    for index in range(slabs):
        value = value + dot(d_ref[index], first_ref[index], 1, 0)
    for pair in range(pairs):
        for which in range(3):
            to, source = (which * pairs + pair) * 64, pair * 192 + which * 64
            acc[to : to + 64, :] = value[source : source + 64, :]
    total[:, rows : rows + 64] = jnp.zeros((D, 64), F32)
    total[:, 0:rows] = acc[...].T
    row = lax.broadcasted_iota(jnp.int32, (BAND, QB), 0)
    col = lax.broadcasted_iota(jnp.int32, (BAND, QB), 1)
    near = col + (BAND - QB) - row < 128
    bucket_at = lax.broadcasted_iota(jnp.int32, (BUCKETS, 128), 0)
    lane = lax.broadcasted_iota(jnp.int32, (BUCKETS, 128), 1)
    bucket = jnp.zeros_like(lane)
    for index_b in range(1, BUCKETS):
        bucket = jnp.where(lane >= bucket_starts[index_b], index_b, bucket)
    mask = (bucket == bucket_at) & (bucket_at < BUCKETS - 1)
    flip_row = lax.broadcasted_iota(jnp.int32, (BAND, BAND), 0)
    flip_col = lax.broadcasted_iota(jnp.int32, (BAND, BAND), 1)
    flip = jnp.where(flip_row + flip_col == BAND - 1, 1.0, 0.0).astype(BF)
    sub = lax.broadcasted_iota(jnp.int32, (BUCKETS, 1), 0)
    per_owner = BUCKETS // (2 * half)
    for pair in range(pairs):
        values = jnp.where(near, band_ref[pair], 0.0)
        high = values.astype(BF)
        values = dot(flip, high, 1, 0) + dot(flip, (values - high.astype(F32)).astype(BF), 1, 0)
        values = pltpu.roll(values, 1, 1, stride=1, stride_axis=0)
        line = jnp.sum(values, 0, keepdims=True)[:, 0:128]
        sums = jnp.sum(jnp.where(mask, line, 0.0), 1, keepdims=True)
        sums = jnp.where(sub == BUCKETS - 1, -jnp.sum(sums, 0, keepdims=True), sums)
        for owner in range(2 * half):
            total[owner * part : owner * part + per_owner, rows + pair : rows + pair + 1] = sums[
                owner * per_owner : (owner + 1) * per_owner
            ]
    split_rows(me_ref, total, keep_ref, send_ref)


def last_kernel(tok_ref, small_ref, w_ref, dmid_ref, d_ref, gtok_ref, full):
    groups, slab, _ = tok_ref.shape
    slabs, rows, _ = d_ref.shape
    per_dest = rows // 192
    per_group = slabs // groups
    for group in range(groups):
        for which in range(3):
            for head in range(HEADS):
                dest = group * per_group + head // per_dest
                row = (head % per_dest) * 192 + which * 64
                to = which * D + head * 64
                full[to : to + 64, :] = d_ref[dest, row : row + 64, :]
        x = tok_ref[group].astype(F32)
        r = rms(x)
        n = x * r
        u = dot(w_ref[...], full[...], 1, 0).T * small_ref[0:1, :]
        gtok_ref[group] = dmid_ref[group * slab : (group + 1) * slab, :] + r * (
            u - n * jnp.mean(u * n, -1, keepdims=True)
        )


def finish_kernel(mine_ref, w_ref, gain_ref, *refs, pairs, experts):
    block_refs, refs = refs[:-8], refs[-8:]
    gw_ref, gnorm_ref, gbias_ref, gwo_ref, gffn_ref, grouter_ref, mixed, square = refs
    rows = gw_ref.shape[0]
    width = pairs * 64
    buckets = gbias_ref.shape[0]
    per_group = len(block_refs)
    quarter = mixed.shape[1] // per_group
    for mine in range(per_group):

        @pl.when(mine_ref[0] == mine)
        def _():
            for offset, ref in enumerate(block_refs):
                hg = mine ^ offset
                for which in range(3):
                    to = which * D + hg * width
                    gw_ref[:, to : to + width] = ref[:, which * width : (which + 1) * width].astype(F32)
                gbias_ref[:, hg * pairs : (hg + 1) * pairs] = ref[
                    0:buckets, 3 * width : 3 * width + pairs
                ].astype(F32)
                mixed[:, hg * quarter : (hg + 1) * quarter] = ref[:, 3 * width + 64 :].astype(F32)

    gnorm = jnp.sum(gw_ref[...] * w_ref[...].astype(F32), 1, keepdims=True)
    gwo_ref[...] = mixed[:, 0:D]
    square[...] = jnp.zeros_like(square)
    square[0:rows, :] = mixed[:, D : D + 128]
    square[0:rows, 1:2] = gnorm
    lines = square[...].T[:, 0:rows]
    gffn_ref[...] = lines[0:1]
    gnorm_ref[...] = lines[1:2] / gain_ref[...].astype(F32)
    grouter_ref[...] = lines[ROUTER_ROW : ROUTER_ROW + experts]


def output_kernel(mid_ref, slot_ref, gate_ref, *refs):
    back_refs, out_ref = refs[:-1], refs[-1]
    count = mid_ref.shape[0]
    each = back_refs[0].shape[0]
    slot = lax.broadcasted_iota(jnp.int32, (count, each), 1)
    total = mid_ref[...]
    for k in range(TOP):
        rows = 0.0
        for index, ref in enumerate(back_refs):
            at = jnp.where(slot + index * each == slot_ref[:, k : k + 1], 1.0, 0.0).astype(BF)
            rows = rows + dot(at, ref[...], 1, 0)
        total = total + gate_ref[:, k : k + 1] * rows
    out_ref[...] = total.astype(BF)


def expert_kernel(
    own_ref, rows_ref, g_ref, other_ref, small_ref, w_ref,
    out_ref, dd_ref, dgate_ref, dslot_ref, act_ref, dpre_ref, gb_ref, acc_out, acc_dd,
    *, index, local, experts,
):
    step, steps = pl.program_id(0), pl.num_programs(0)
    rows = rows_ref[...]

    @pl.when(step == 0)
    def _():
        own = own_ref[0] * local + index
        logits = dot(rows, small_ref[8 : 8 + experts].astype(BF), 1, 1)
        expert = lax.broadcasted_iota(jnp.int32, logits.shape, 1)
        mine = jnp.sum(jnp.where(expert == own, logits, 0.0), 1, keepdims=True)
        theirs = jnp.sum(jnp.where(expert == other_ref[...], logits, 0.0), 1, keepdims=True)
        gate = 1.0 / (1.0 + jnp.exp(theirs - mine))
        dslot = (g_ref[...].astype(F32) * gate).astype(BF)
        dslot_ref[...] = dslot
        gb_ref[...] = jnp.sum(dslot.astype(F32), 0, keepdims=True)
        acc_out[...] = jnp.zeros_like(acc_out)
        acc_dd[...] = jnp.zeros_like(acc_dd)

    w_in, w_out = w_ref[0, 0], w_ref[0, 1]
    pre = dot(rows, w_in, 1, 1)
    dact = dot(dslot_ref[...], w_out, 1, 1)
    root = math.sqrt(2 / math.pi)
    square = pre * pre
    tanh = jnp.tanh(pre * (root + (root * 0.044715) * square))
    half = 0.5 + 0.5 * tanh
    act = (pre * half).astype(BF)
    slope = half + (pre * (half - half * half)) * (2 * root + (6 * root * 0.044715) * square)
    act_ref[0] = act
    dpre = (dact * slope).astype(BF)
    dpre_ref[0] = dpre
    acc_dd[...] += dot(dpre, w_in, 1, 0)
    acc_out[...] += dot(act, w_out, 1, 0)

    @pl.when(step == steps - 1)
    def _():
        out = (acc_out[...] + small_ref[B_ROW + index : B_ROW + index + 1, :]).astype(BF)
        out_ref[...] = out
        dd_ref[...] = acc_dd[...].astype(BF)
        dgate = jnp.sum(out.astype(F32) * g_ref[...].astype(F32), 1, keepdims=True)
        dgate = jnp.broadcast_to(dgate, (dgate.shape[0], 128)).T
        high = dgate.astype(BF).astype(F32)
        middle = (dgate - high).astype(BF).astype(F32)
        line = lax.broadcasted_iota(jnp.int32, dgate.shape, 0)
        parts = jnp.where(line == 0, high, jnp.where(line == 1, middle, dgate - high - middle))
        dgate_ref[...] = parts[0:16].astype(BF)


def expert_pass(index, local, experts, own, rows, g_rows, other, small, weights):
    count, _ = rows.shape
    parts, _, units, _ = weights.shape
    token_s = pl.BlockSpec((count, D), lambda f: (0, 0))
    narrow_s = pl.BlockSpec((count, 1), lambda f: (0, 0))
    line_s = pl.BlockSpec((16, count), lambda f: (0, 0))
    weight_s = pl.BlockSpec((1, 2, units, D), lambda f: (f, 0, 0, 0))
    bias_s = pl.BlockSpec((1, D), lambda f: (0, 0))
    hidden_s = pl.BlockSpec((1, count, units), lambda f: (f, 0, 0))
    hidden = shape((parts, count, units), BF)
    return pl.pallas_call(
        functools.partial(expert_kernel, index=index, local=local, experts=experts),
        grid=(parts,),
        out_shape=(
            shape(rows.shape, BF),
            shape(rows.shape, BF),
            shape((16, count), BF),
            shape(rows.shape, BF),
            hidden,
            hidden,
            shape((1, D), F32),
        ),
        in_specs=[
            pl.BlockSpec(memory_space=pltpu.SMEM),
            token_s,
            token_s,
            narrow_s,
            pl.BlockSpec(small.shape, lambda f: (0, 0)),
            weight_s,
        ],
        out_specs=(token_s, token_s, line_s, token_s, hidden_s, hidden_s, bias_s),
        scratch_shapes=[pltpu.VMEM((count, D), F32), pltpu.VMEM((count, D), F32)],
        compiler_params=params(),
        cost_estimate=cost(10 * count * D * units * parts, 6 * D * units * parts * 2),
    )(own, rows, g_rows, other, small, weights)


def weight_kernel(*refs, local, parts):
    out_ref = refs[-1]
    for index in range(local):
        rows_ref, dslot_ref, act_ref, dpre_ref = refs[4 * index : 4 * index + 4]

        @pl.when(pl.program_id(0) // parts == index)
        def _():
            out_ref[0, 0, 0] = dot(dpre_ref[0], rows_ref[...], 0, 0).astype(BF)
            out_ref[0, 0, 1] = dot(act_ref[0], dslot_ref[...], 0, 0).astype(BF)


def weight_grads(operands):
    local = len(operands)
    count = operands[0][0].shape[0]
    parts, _, units = operands[0][2].shape
    token_s = pl.BlockSpec((count, D), lambda i: (0, 0))

    def hidden_s(index):
        return pl.BlockSpec(
            (1, count, units),
            lambda i: (jnp.clip(i - index * parts, 0, parts - 1), 0, 0),
        )

    return pl.pallas_call(
        functools.partial(weight_kernel, local=local, parts=parts),
        grid=(local * parts,),
        out_shape=shape((parts, local, 2, units, D), BF),
        in_specs=[
            spec
            for index in range(local)
            for spec in (token_s, token_s, hidden_s(index), hidden_s(index))
        ],
        out_specs=pl.BlockSpec(
            (1, 1, 2, units, D), lambda i: (lax.rem(i, parts), i // parts, 0, 0, 0)
        ),
        compiler_params=params(),
        cost_estimate=cost(1e6, 1e6),
    )(*[a for of in operands for a in of])


def spread_kernel(x_ref, in_ref, out_ref):
    for index in range(x_ref.shape[0]):
        in_ref[:, index, :] = x_ref[index, 0].astype(F32)
        out_ref[:, index, :] = x_ref[index, 1].astype(F32)


def spread_grads(owned):
    local, _, units, _ = owned.shape
    rows = min(128, units)
    out_s = pl.BlockSpec((rows, local, D), lambda i: (i, 0, 0))
    return pl.pallas_call(
        spread_kernel,
        grid=(units // rows,),
        in_specs=[pl.BlockSpec((local, 2, rows, D), lambda i: (0, 0, i, 0))],
        out_specs=(out_s, out_s),
        out_shape=[shape((units, local, D), F32)] * 2,
        compiler_params=params(),
        cost_estimate=cost(1e6, 1e6),
    )(owned)


def after(array, *others):
    return lax.optimization_barrier((array, *others))[0]


def swap(array, axis, bit):
    size = lax.axis_size(axis)
    return lax.ppermute(array, axis, [(i, i ^ bit) for i in range(size)])


def gather_parts(array):
    bit = lax.axis_size("fsdp") // 2
    held = [(0, array)]
    while bit:
        held = held + [(off ^ bit, swap(a, "fsdp", bit)) for off, a in held]
        bit //= 2
    return [off for off, _ in held], [a for _, a in held]


def exchange(array):
    return lax.all_to_all(array, "seq", split_axis=0, concat_axis=0, tiled=True)


def add(*arrays):
    return sum(a.astype(F32) for a in arrays).astype(BF)


def fold_first(keep, send):
    send = swap(send, "fsdp", 1)
    return [add(keep[index], send[index]) for index in range(keep.shape[0])]


def fold_rest(held):
    bit = 2
    while len(held) > 1:
        held = [add(a, swap(b, "fsdp", bit)) for a, b in zip(held[::2], held[1::2])]
        bit *= 2
    return held[0]


def slabs_of_sequence(tokens, me, per_group, packed):
    slabs = lax.axis_size("seq")
    groups = tokens.shape[0]
    if (slabs, groups, per_group) == (8, 2, 4):
        mine = lax.dynamic_index_in_dim(tokens, me // 4, 0, keepdims=False)
        theirs = lax.dynamic_index_in_dim(tokens, 1 - me // 4, 0, keepdims=False)
        far = swap(theirs, "seq", 4)
        found = {0: mine, 4: far}
        for bit in (1, 2, 3):
            found[bit] = swap(mine, "seq", bit)
        far = after(far, packed, *[found[bit] for bit in (1, 2, 3)])
        for bit in (1, 2, 3):
            found[4 ^ bit] = swap(far, "seq", bit)
        return me, list(found), list(found.values())
    rows = exchange(jnp.repeat(tokens, per_group, axis=0))
    return me * 0, list(range(slabs)), [rows[index] for index in range(slabs)]


def scalar(value):
    return value.reshape(1).astype(jnp.int32)


def per_device(
    tokens, cotangent, segments, routes, norm_attn, w_qkv, w_o, rel_bias, norm_ffn, router, w_in,
    w_out, b_out,
):
    slabs, owners = lax.axis_size("seq"), lax.axis_size("fsdp")
    me = lax.axis_index("seq")
    me_f = scalar(lax.axis_index("fsdp"))
    groups, slab = tokens.shape[0], tokens.shape[1]
    count = groups * slab
    experts, local = router.shape[1], b_out.shape[0]
    capacity = max(2, 9 * count * TOP // (8 * experts))
    slots = experts * capacity
    each = slots // local
    pairs = groups * HEADS // slabs
    per_group = HEADS // pairs
    width = pairs * HEAD_DIM
    part = D // owners
    head_group = lax.rem(me, per_group)
    grad_flat = cotangent.reshape(count, D)

    pack = one_step(
        pack_kernel,
        [shape((part, D + 128 + 3 * width), BF)],
        (
            scalar(head_group), w_qkv, w_o, norm_attn[None], norm_ffn[None], rel_bias, b_out,
            router.T,
        ),
        1e9,
        scratch=[pltpu.VMEM((128, 256), F32)],
        smem=1,
    )[0]
    offsets, packed = gather_parts(pack)
    base, slab_offsets, slab_rows = slabs_of_sequence(tokens, me, per_group, packed[1])
    w_columns, w_o_full, small, bands = one_step(
        functools.partial(unpack_kernel, offsets=offsets, pairs=pairs),
        [
            shape((D, 3 * width), BF),
            shape((D, D), BF),
            shape((128, D), F32),
            shape((pairs, BAND, QB), F32),
        ],
        (me_f, *packed),
        3e9,
        scratch=[pltpu.VMEM((D, 128), F32)],
        smem=1,
    )

    route_col = after(routes, slab_rows[5], small).reshape(count, TOP)
    base_col = (route_col % local) * each + (route_col // local) * capacity
    slot_col, slot_row, other, *g_slots = one_step(
        functools.partial(route_kernel, experts=experts, capacity=capacity),
        [
            shape((count, TOP), jnp.int32),
            shape((TOP, count), jnp.int32),
            shape((8, slots), F32),
        ]
        + [shape((each, D), BF)] * local,
        (route_col, route_col.T, base_col, base_col.T, grad_flat),
        5e9,
    )

    def cross(array):
        return exchange(array.reshape(slabs, capacity, D)).reshape(each, D)

    ids = other[0].reshape(local, slabs, capacity).swapaxes(0, 1).reshape(slabs, 1, -1)
    ids = jnp.pad(ids.astype(BF), ((0, 0), (0, 7), (0, D - local * capacity)))
    g_all = jnp.concatenate([a.reshape(slabs, capacity, D) for a in g_slots] + [ids], 1)
    g_all = exchange(after(g_all, *slab_rows[:G_AFTER]))

    def g_part(index):
        return g_all[:, index * capacity : (index + 1) * capacity].reshape(each, D)

    def other_part(index):
        at = slice(index * capacity, (index + 1) * capacity)
        return g_all[:, local * capacity, at].reshape(each, 1).astype(jnp.int32)

    seg = lax.dynamic_slice_in_dim(segments, me // per_group, 1, 0)
    qkv, first = one_step(
        functools.partial(project_kernel, offsets=slab_offsets),
        [shape((slabs, 3 * width, slab), BF), shape((slabs, slab, D), BF)],
        (scalar(base), small, w_columns, *slab_rows),
        4 * SEQ_LEN * D * 3 * width,
        smem=1,
    )
    out, wide, lse = attention_fwd(qkv, seg, bands)
    out, g_all = lax.optimization_barrier((out, g_all))
    att = exchange(out)
    mid, gates, *disp = one_step(
        functools.partial(middle_kernel, experts=experts),
        [shape((count, D), F32), shape((count, TOP), F32)] + [shape((each, D), BF)] * local,
        (tokens, small, w_o_full, route_col, slot_row, att),
        4 * count * D * (D + slots),
    )

    relaid = jnp.stack([w_in, w_out]).transpose(2, 0, 1, 3)
    weights = [
        lax.all_gather(relaid[index], "fsdp", axis=0, tiled=False) for index in range(local)
    ]
    w_qkv_late, _ = lax.optimization_barrier((w_qkv, att))
    w_qkv_full = lax.all_gather(w_qkv_late, "fsdp", axis=0, tiled=True)
    rows, passes = [], []
    for index in range(local):
        rows.append(cross(after(disp[index], *rows)))
    for index in range(local):
        if index:
            rows[index] = after(rows[index], passes[-1][1])
        passes.append(
            expert_pass(
                index, local, experts, scalar(me), rows[index], g_part(index),
                other_part(index), small, weights[index],
            )
        )
    results, dd, dgate, dslot, act, dpre, grad_b = map(list, zip(*passes))
    parts = jnp.stack([a[0:3] for a in dgate], 1).reshape(3 * local, slabs, capacity)
    parts = parts.swapaxes(0, 1).reshape(slabs, 1, -1)
    parts = jnp.pad(parts, ((0, 0), (0, 7), (0, D - parts.shape[2])))
    dd_back = [cross(a) for a in dd[:-1]]
    last = jnp.concatenate([dd[-1].reshape(slabs, capacity, D), parts], 1)
    last = exchange(after(last, *dd_back))
    dd_back.append(last[:, :capacity].reshape(each, D))
    parts = last[:, capacity, : 3 * local * capacity].astype(F32)
    dgate_back = jnp.sum(parts.reshape(slabs, 3, local, capacity), 1)
    dgate_back = dgate_back.swapaxes(0, 1).reshape(1, slots)
    act = [after(a, dd[-1]) for a in act]
    big = weight_grads(list(zip(rows, dslot, act, dpre)))
    *dd_back, big = lax.optimization_barrier((*dd_back, big))
    big = lax.psum_scatter(big, "fsdp", scatter_dimension=0, tiled=True)[0]

    dmid, grad_att, keep, send = one_step(
        functools.partial(return_kernel, local=local, experts=experts),
        [shape((count, D), F32), shape((slabs, width, slab), BF)]
        + [shape((owners // 2, part, D + 256), BF)] * 2,
        (
            me_f, dgate_back, slot_col, route_col, gates, mid, grad_flat, small, w_o_full, att,
            *dd_back, *grad_b,
        ),
        4 * count * D * (slots + 2 * D),
        scratch=[pltpu.VMEM((128, D), F32), pltpu.VMEM((D, D + 256), F32)],
        smem=1,
    )
    results_back = [cross(after(results[0], *dd_back))]
    grad_heads = exchange(after(grad_att, *results_back))
    for a in results[1:]:
        results_back.append(cross(after(a, grad_heads, *results_back)))
    mixed = fold_first(after(keep, grad_heads), send)
    d_qkv, band_sums = attention_bwd(qkv, seg, bands, wide, lse, grad_heads)
    mixed[0] = after(mixed[0], d_qkv)
    mixed = fold_rest(mixed)
    d_back = exchange(after(d_qkv, *results_back))
    output = one_step(
        output_kernel,
        (shape((count, D), BF),),
        (after(mid, d_qkv), slot_col, gates, *results_back),
        4 * count * D * slots,
    )[0].reshape(groups, slab, D)

    keep, send = one_step(
        qkv_grad_kernel,
        [shape((owners // 2, part, 3 * width + 64), BF)] * 2,
        (me_f, first, d_qkv, band_sums),
        4 * SEQ_LEN * D * 3 * width,
        scratch=[pltpu.VMEM((3 * width, D), F32), pltpu.VMEM((D, 3 * width + 64), F32)],
        smem=1,
    )
    grad_tokens = one_step(
        last_kernel,
        [shape((groups, slab, D), F32)],
        (tokens, small, w_qkv_full, dmid, after(d_back, keep, output)),
        4 * count * D * 3 * D,
        scratch=[pltpu.VMEM((3 * D, slab), BF)],
    )[0]
    grad_qkv = fold_rest(fold_first(keep, send))
    grad_b_own = mixed[:, D + 1 : D + 1 + local].astype(F32).T
    quarter = (D + 256) // per_group

    def quarter_of(offset):
        return lax.dynamic_slice_in_dim(mixed, (head_group ^ offset) * quarter, quarter, 1)

    mixed = add(quarter_of(0), *[swap(quarter_of(k), "seq", k) for k in range(1, per_group)])
    block = jnp.concatenate([grad_qkv, mixed], 1)
    bit = per_group
    while bit < slabs:
        block = add(after(block, output), swap(block, "seq", bit))
        bit *= 2
    blocks = [block] + [swap(block, "seq", k) for k in range(1, per_group)]
    big = after(big, grad_tokens)
    grad_w_in, grad_w_out = spread_grads(big)
    blocks[0], grad_w_in, grad_w_out = lax.optimization_barrier((blocks[0], grad_w_in, grad_w_out))
    grad_wqkv, grad_gain_attn, grad_bias, grad_wo, grad_gain_ffn, grad_router = one_step(
        functools.partial(finish_kernel, pairs=pairs, experts=experts),
        [
            shape((part, 3 * D), F32),
            shape((1, part), F32),
            shape(rel_bias.shape, F32),
            shape((part, D), F32),
            shape((1, part), F32),
            shape((experts, part), F32),
        ],
        (scalar(head_group), w_qkv, norm_attn[None], *blocks),
        1e9,
        scratch=[pltpu.VMEM((part, D + 256), F32), pltpu.VMEM((256, 128), F32)],
        smem=1,
    )
    return (
        output,
        grad_tokens,
        grad_gain_attn[0],
        grad_wqkv,
        grad_wo,
        grad_bias,
        grad_gain_ffn[0],
        grad_router.T,
        grad_w_in,
        grad_w_out,
        grad_b_own,
    )


def solution(mesh):
    in_specs = (
        P("fsdp", "seq", None),
        P("fsdp", "seq", None),
        P("fsdp", None),
        P("fsdp", "seq", None),
        P("fsdp"),
        P("fsdp", None),
        P("fsdp", None),
        P("fsdp", None),
        P("fsdp"),
        P("fsdp", None),
        P("fsdp", "seq", None),
        P("fsdp", "seq", None),
        P("seq", "fsdp"),
    )
    out_specs = (
        P("fsdp", "seq", None),
        P("fsdp", "seq", None),
        P("fsdp"),
        P("fsdp", None),
        P("fsdp", None),
        P("fsdp", None),
        P("fsdp"),
        P("fsdp", None),
        P("fsdp", "seq", None),
        P("fsdp", "seq", None),
        P("seq", "fsdp"),
    )
    return jax.shard_map(
        per_device, mesh=mesh, in_specs=in_specs, out_specs=out_specs, check_vma=False
    )
```

```python
import functools
import math

import jax
import jax.numpy as jnp
from jax import lax
from jax.experimental import pallas as pl
from jax.experimental.pallas import tpu as pltpu
from jax.sharding import PartitionSpec as P

D = 768
HEADS = 12
HEAD_DIM = 64
TOP = 2
SEQ_LEN = 2048
BUCKETS = 32
DOCS = 8
QB = 256
BAND = QB + 128
EPS = 1e-06
NEG = -1e30
F32 = jnp.float32
BF = jnp.bfloat16
bucket_starts = tuple(range(17)) + tuple(
    int(math.ceil(16 * 8 ** (step_k / 16))) for step_k in range(1, 16)
)
VMEM_MOST = 56 << 20
COST_SHARE = 0.4
FILLER = 0.2
G_AFTER = 8


def dot(lhs, rhs, lhs_dim, rhs_dim):
    return lax.dot_general(
        lhs, rhs, (((lhs_dim,), (rhs_dim,)), ((), ())), preferred_element_type=F32
    )


def params():
    return pltpu.CompilerParams(vmem_limit_bytes=VMEM_MOST)


def cost(flops, bytes_accessed, transcendentals=0):
    return pl.CostEstimate(
        flops=int(flops * COST_SHARE), bytes_accessed=int(bytes_accessed * COST_SHARE),
        transcendentals=int(transcendentals * COST_SHARE),
    )


def shape(dims, dtype):
    return jax.ShapeDtypeStruct(dims, dtype)


def load_pair(qkv_ref, seg_ref, qt, kt, vt):
    slabs, _, slab = qkv_ref.shape
    for index in range(slabs):
        cols = slice(index * slab, (index + 1) * slab)
        qt[0:64, cols] = qkv_ref[index, 0:64, :] * jnp.asarray(0.125, BF)
        kt[0:64, cols] = qkv_ref[index, 64:128, :]
        vt[0:64, cols] = qkv_ref[index, 128:192, :]
    row = lax.broadcasted_iota(jnp.int32, (16, SEQ_LEN), 0)
    same = seg_ref[...] == row
    kt[64:80, :] = jnp.where(same, 1.0, 0.0).astype(BF)
    qt[64:80, :] = jnp.where(same | (row >= DOCS), 0.0, NEG).astype(BF)


def key_parts(block):
    end = (block + 1) * QB
    near = max(end - BAND, 0)
    return [(near, end)] + ([(0, near)] if near > 0 else [])


def fwd_kernel(qkv_ref, seg_ref, band_ref, o_ref, wide_ref, lse_ref, qt, kt, vt, k_rows):
    slabs, _, slab = qkv_ref.shape
    load_pair(qkv_ref, seg_ref, qt, kt, vt)
    k_rows[...] = kt[...].T
    for block in range(SEQ_LEN // QB):
        start, end = block * QB, (block + 1) * QB
        query = qt[:, start:end]
        scores = []
        for low, high in key_parts(block):
            part = dot(k_rows[low:high], query, 1, 0)
            if high == end:
                part = part + band_ref[0, BAND - (high - low) :, :]
            scores.append((low, high, part))
        peak = functools.reduce(
            jnp.maximum, [jnp.max(part, 0, keepdims=True) for _, _, part in scores]
        )
        total, out = 0.0, 0.0
        for low, high, part in scores:
            terms = jnp.exp(part - peak)
            total = total + jnp.sum(terms, 0, keepdims=True)
            out = out + dot(vt[:, low:high], terms.astype(BF), 1, 0)
        wide_ref[0, :, start:end] = out * (1.0 / total)
        lse_ref[0, :, start:end] = peak + jnp.log(total)
    for index in range(slabs):
        o_ref[index] = wide_ref[0, :, index * slab : (index + 1) * slab].astype(BF)


def bwd_kernel(
    qkv_ref, seg_ref, band_ref, wide_ref, lse_ref, do_ref, d_ref, hist_ref,
    qt, kt, vt, k_rows, v_rows, do_t, dq, dk, dv,
):
    slabs, _, slab = qkv_ref.shape
    load_pair(qkv_ref, seg_ref, qt, kt, vt)
    k_rows[...] = kt[...].T
    v_rows[...] = vt[...].T
    for index in range(slabs):
        do_t[:, index * slab : (index + 1) * slab] = do_ref[index]
    dk[...] = jnp.zeros_like(dk)
    dv[...] = jnp.zeros_like(dv)
    hist_ref[...] = jnp.zeros_like(hist_ref)
    for block in range(SEQ_LEN // QB):
        start, end = block * QB, (block + 1) * QB
        query, grad = qt[:, start:end], do_t[:, start:end]
        delta = jnp.sum(grad.astype(F32) * wide_ref[0, :, start:end], 0, keepdims=True)
        lse = lse_ref[0, :, start:end]
        grad_query = 0.0
        for low, high in key_parts(block):
            part = dot(k_rows[low:high], query, 1, 0)
            off = BAND - (high - low)
            if high == end:
                part = part + band_ref[0, off:, :]
            probs = jnp.exp(part - lse)
            grad_probs = dot(v_rows[low:high], grad, 1, 0)
            grad_scores = (probs * (grad_probs - delta)).astype(BF)
            if high == end:
                hist_ref[0, off:, :] += grad_scores.astype(F32)
            dv[:, low:high] += dot(grad, probs.astype(BF), 1, 1)
            dk[:, low:high] += dot(query[0:64], grad_scores, 1, 1)
            grad_query = grad_query + dot(kt[0:64, low:high], grad_scores, 1, 0)
        dq[:, start:end] = grad_query * 0.125
    for index in range(slabs):
        cols = slice(index * slab, (index + 1) * slab)
        d_ref[index, 0:64, :] = dq[:, cols].astype(BF)
        d_ref[index, 64:128, :] = dk[:, cols].astype(BF)
        d_ref[index, 128:192, :] = dv[:, cols].astype(BF)


def attention_specs(slabs, slab):
    qkv = pl.BlockSpec((slabs, 192, slab), lambda p: (0, p, 0))
    one = pl.BlockSpec((slabs, 64, slab), lambda p: (0, p, 0))
    seg = pl.BlockSpec((1, SEQ_LEN), lambda p: (0, 0))
    band = pl.BlockSpec((1, BAND, QB), lambda p: (p, 0, 0))
    wide = pl.BlockSpec((1, 64, SEQ_LEN), lambda p: (p, 0, 0))
    lse = pl.BlockSpec((1, 1, SEQ_LEN), lambda p: (p, 0, 0))
    return qkv, one, seg, band, wide, lse


def attention_fwd(qkv, seg, bands):
    slabs, rows, slab = qkv.shape
    pairs = rows // 192
    qkv_s, one_s, seg_s, band_s, wide_s, lse_s = attention_specs(slabs, slab)
    return pl.pallas_call(
        fwd_kernel,
        grid=(pairs,),
        out_shape=(
            shape((slabs, 64 * pairs, slab), BF),
            shape((pairs, 64, SEQ_LEN), F32),
            shape((pairs, 1, SEQ_LEN), F32),
        ),
        in_specs=[qkv_s, seg_s, band_s],
        out_specs=(one_s, wide_s, lse_s),
        scratch_shapes=[
            pltpu.VMEM((80, SEQ_LEN), BF),
            pltpu.VMEM((80, SEQ_LEN), BF),
            pltpu.VMEM((64, SEQ_LEN), BF),
            pltpu.VMEM((SEQ_LEN, 80), BF),
        ],
        compiler_params=params(),
        cost_estimate=cost(pairs * 6e9, pairs * 2e6, pairs * 2.4e6),
    )(qkv, seg, bands)


def attention_bwd(qkv, seg, bands, wide, lse, grad):
    slabs, rows, slab = qkv.shape
    pairs = rows // 192
    qkv_s, one_s, seg_s, band_s, wide_s, lse_s = attention_specs(slabs, slab)
    return pl.pallas_call(
        bwd_kernel,
        grid=(pairs,),
        out_shape=(shape(qkv.shape, BF), shape((pairs, BAND, QB), F32)),
        in_specs=[qkv_s, seg_s, band_s, wide_s, lse_s, one_s],
        out_specs=(qkv_s, band_s),
        scratch_shapes=[
            pltpu.VMEM((80, SEQ_LEN), BF),
            pltpu.VMEM((80, SEQ_LEN), BF),
            pltpu.VMEM((64, SEQ_LEN), BF),
            pltpu.VMEM((SEQ_LEN, 80), BF),
            pltpu.VMEM((SEQ_LEN, 64), BF),
            pltpu.VMEM((64, SEQ_LEN), BF),
            pltpu.VMEM((64, SEQ_LEN), F32),
            pltpu.VMEM((64, SEQ_LEN), F32),
            pltpu.VMEM((64, SEQ_LEN), F32),
        ],
        compiler_params=params(),
        cost_estimate=cost(pairs * 10e9, pairs * 3e6, pairs * 2.4e6),
    )(qkv, seg, bands, wide, lse, grad)


def rms(values):
    return lax.rsqrt(jnp.mean(values * values, -1, keepdims=True) + EPS)


def one_step(kernel, outs, operands, flops, scratch=(), smem=0):
    size = sum(math.prod(a.shape) * a.dtype.itemsize for a in (*operands, *outs))
    return pl.pallas_call(
        kernel,
        out_shape=tuple(outs),
        in_specs=[pl.BlockSpec(memory_space=pltpu.SMEM)] * smem
        + [pl.BlockSpec(memory_space=pltpu.VMEM)] * (len(operands) - smem),
        out_specs=tuple([pl.BlockSpec(memory_space=pltpu.VMEM)] * len(outs)),
        scratch_shapes=list(scratch),
        compiler_params=params(),
        cost_estimate=cost(flops * FILLER, size * FILLER),
    )(*operands)


BIAS_ROW, B_ROW, ROUTER_ROW = 2, 5, 8


def pack_kernel(hg_ref, w_ref, o_ref, attn_ref, ffn_ref, bias_ref, b_ref, router_ref, out_ref, lines):
    part = o_ref.shape[0]
    local, experts = b_ref.shape[0], router_ref.shape[0]
    width = (out_ref.shape[1] - D - 128) // 3
    pairs = width // 64
    out_ref[:, 0:D] = o_ref[...]
    lines[...] = jnp.zeros_like(lines)
    lines[0:1, 0:part] = attn_ref[...].astype(F32)
    lines[1:2, 0:part] = ffn_ref[...].astype(F32)
    lines[B_ROW : B_ROW + local, 0:part] = b_ref[...].astype(F32)
    lines[ROUTER_ROW : ROUTER_ROW + experts, 0:part] = router_ref[...].astype(F32)
    out_ref[:, D : D + 128] = lines[...].T[0:part].astype(BF)
    for mine in range(D // width):

        @pl.when(hg_ref[0] == mine)
        def _():
            for which in range(3):
                source, to = which * D + mine * width, D + 128 + which * width
                out_ref[:, to : to + width] = w_ref[:, source : source + width]
            out_ref[0 : bias_ref.shape[0], D + BIAS_ROW : D + BIAS_ROW + pairs] = bias_ref[
                :, mine * pairs : (mine + 1) * pairs
            ]


def unpack_kernel(me_ref, *refs, offsets, pairs):
    part_refs, (w_ref, o_ref, small_ref, band_ref, narrow) = refs[: len(offsets)], refs[len(offsets) :]
    rows = part_refs[0].shape[0]
    for offset, ref in zip(offsets, part_refs):
        at = pl.ds(pl.multiple_of((me_ref[0] ^ offset) * rows, 32), rows)
        o_ref[at, :] = ref[:, 0:D]
        narrow[at, :] = ref[:, D : D + 128].astype(F32)
        w_ref[at, :] = ref[:, D + 128 :]
    small_ref[...] = narrow[...].T
    row = lax.broadcasted_iota(jnp.int32, (BAND, QB), 0)
    col = lax.broadcasted_iota(jnp.int32, (BAND, QB), 1)
    distance = col + (BAND - QB) - row
    per_owner = BUCKETS * rows // D
    for pair in range(pairs):
        source = BIAS_ROW + pair

        def entry(index_b):
            lane = index_b // per_owner * rows + index_b % per_owner
            return small_ref[source : source + 1, lane : lane + 1]

        last = entry(BUCKETS - 1)
        table = jnp.where(distance < 0, NEG, entry(0) - last)
        for index_b in range(1, BUCKETS):
            table = jnp.where(distance >= bucket_starts[index_b], entry(index_b) - last, table)
        band_ref[pair] = table


def project_kernel(me_ref, small_ref, w_ref, *refs, offsets):
    tok_refs, (qkv_ref, first_ref) = refs[:-2], refs[-2:]
    pairs = w_ref.shape[1] // 192
    for offset, ref in zip(offsets, tok_refs):
        at = me_ref[0] ^ offset
        x = ref[...].astype(F32)
        first = (x * rms(x) * small_ref[0:1, :]).astype(BF)
        first_ref[at] = first
        result = dot(w_ref[...], first, 0, 1).astype(BF)
        for pair in range(pairs):
            for which in range(3):
                to, source = pair * 192 + which * 64, (which * pairs + pair) * 64
                qkv_ref[at, to : to + 64, :] = result[source : source + 64, :]


def route_kernel(
    col_ref, row_ref, base_col_ref, base_row_ref, g_ref, sc_ref, sr_ref, other_ref, *gd_refs,
    experts, capacity,
):
    count = col_ref.shape[0]
    each = gd_refs[0].shape[0]
    slots = each * len(gd_refs)
    r0, r1 = col_ref[:, 0:1], col_ref[:, 1:2]
    expert = lax.broadcasted_iota(jnp.int32, (count, experts), 1)
    is0, is1 = expert == r0, expert == r1
    hits = jnp.where(is0 | is1, 1.0, 0.0).astype(BF)
    row_i = lax.broadcasted_iota(jnp.int32, (count, count), 0)
    col_i = lax.broadcasted_iota(jnp.int32, (count, count), 1)
    earlier = jnp.where(col_i < row_i, 1.0, 0.0).astype(BF)
    ranks = dot(earlier, hits, 1, 0)
    for k, own in ((0, is0), (1, is1)):
        rank = jnp.sum(jnp.where(own, ranks, 0.0), 1, keepdims=True).astype(jnp.int32)
        sc_ref[:, k : k + 1] = jnp.where(rank < capacity, base_col_ref[:, k : k + 1] + rank, -1)
    expert = lax.broadcasted_iota(jnp.int32, (experts, count), 0)
    is0, is1 = expert == row_ref[0:1, :], expert == row_ref[1:2, :]
    hits = jnp.where(is0 | is1, 1.0, 0.0).astype(BF)
    later = jnp.where(row_i < col_i, 1.0, 0.0).astype(BF)
    ranks = dot(hits, later, 1, 0)
    slot_rows = []
    for k, own in ((0, is0), (1, is1)):
        rank = jnp.sum(jnp.where(own, ranks, 0.0), 0, keepdims=True).astype(jnp.int32)
        slot_rows.append(jnp.where(rank < capacity, base_row_ref[k : k + 1, :] + rank, -1))
        sr_ref[k : k + 1, :] = slot_rows[k]
    slot = lax.broadcasted_iota(jnp.int32, (slots, count), 0)
    at0 = jnp.where(slot == slot_rows[0], 1.0, 0.0).astype(BF)
    at1 = jnp.where(slot == slot_rows[1], 1.0, 0.0).astype(BF)
    both = at0 + at1
    for index, ref in enumerate(gd_refs):
        ref[...] = dot(both[index * each : (index + 1) * each], g_ref[...], 1, 0).astype(BF)
    r0 = jnp.broadcast_to(row_ref[0:1, :], (8, count)).astype(F32).astype(BF)
    r1 = jnp.broadcast_to(row_ref[1:2, :], (8, count)).astype(F32).astype(BF)
    other_ref[...] = dot(r1, at0, 1, 1) + dot(r0, at1, 1, 1)


def middle_kernel(
    tok_ref, small_ref, w_ref, col_ref, slot_ref, chunk_ref, mid_ref, gate_ref, *disp_refs, experts
):
    groups, slab, _ = tok_ref.shape
    per_group = chunk_ref.shape[0] // groups
    each = disp_refs[0].shape[0]
    count, slots = groups * slab, each * len(disp_refs)
    for group in range(groups):
        att = chunk_ref[group * per_group : (group + 1) * per_group].reshape(D, slab)
        mid_ref[group * slab : (group + 1) * slab, :] = tok_ref[group].astype(F32) + dot(
            att, w_ref[...], 0, 0
        )
    mid = mid_ref[...]
    second = (mid * rms(mid) * small_ref[1:2, :]).astype(BF)
    logits = dot(second, small_ref[ROUTER_ROW : ROUTER_ROW + experts].astype(BF), 1, 1)
    expert = lax.broadcasted_iota(jnp.int32, logits.shape, 1)
    c0 = jnp.sum(jnp.where(expert == col_ref[:, 0:1], logits, 0.0), 1, keepdims=True)
    c1 = jnp.sum(jnp.where(expert == col_ref[:, 1:2], logits, 0.0), 1, keepdims=True)
    top = jnp.maximum(c0, c1)
    e0, e1 = jnp.exp(c0 - top), jnp.exp(c1 - top)
    gate_ref[:, 0:1] = e0 / (e0 + e1)
    gate_ref[:, 1:2] = e1 / (e0 + e1)
    slot = lax.broadcasted_iota(jnp.int32, (slots, count), 0)
    at = jnp.where((slot == slot_ref[0:1, :]) | (slot == slot_ref[1:2, :]), 1.0, 0.0).astype(BF)
    for index, ref in enumerate(disp_refs):
        ref[...] = dot(at[index * each : (index + 1) * each], second, 1, 0).astype(BF)


def split_rows(me_ref, source_ref, keep_ref, send_ref):
    half, rows, _ = keep_ref.shape
    for index in range(2 * half):
        start = pl.multiple_of((me_ref[0] ^ index) * rows, 32)
        ref = send_ref if index % 2 else keep_ref
        ref[index // 2] = source_ref[pl.ds(start, rows), :].astype(BF)


def return_kernel(
    me_ref, dgate_ref, slot_ref, col_ref, gate_ref, mid_ref, g_ref, small_ref, w_ref, att_ref,
    *refs, local, experts,
):
    dd_refs, refs = refs[:local], refs[local:]
    gb_refs, refs = refs[:local], refs[local:]
    dmid_ref, datt_ref, keep_ref, send_ref, narrow, total = refs
    count = mid_ref.shape[0]
    each = dd_refs[0].shape[0]
    slots = each * local
    slabs, rows, slab = att_ref.shape
    groups = count // slab
    per_group = slabs // groups
    slot = lax.broadcasted_iota(jnp.int32, (count, slots), 1)
    own = [slot == slot_ref[:, k : k + 1] for k in range(TOP)]
    at = jnp.where(own[0] | own[1], 1.0, 0.0).astype(BF)
    dsecond = 0.0
    for index, ref in enumerate(dd_refs):
        dsecond = dsecond + dot(at[:, index * each : (index + 1) * each], ref[...], 1, 0)
    dgate = [jnp.sum(jnp.where(o, dgate_ref[...], 0.0), 1, keepdims=True) for o in own]
    gate = [gate_ref[:, k : k + 1] for k in range(TOP)]
    both = gate[0] * dgate[0] + gate[1] * dgate[1]
    expert = lax.broadcasted_iota(jnp.int32, (count, experts), 1)
    dlogits = jnp.zeros((count, experts), F32)
    for k in range(TOP):
        dlogits = jnp.where(expert == col_ref[:, k : k + 1], gate[k] * (dgate[k] - both), dlogits)
    dlogits = dlogits.astype(BF)
    mid = mid_ref[...]
    r = rms(mid)
    n = mid * r
    gain = small_ref[1:2, :]
    second = (n * gain).astype(BF)
    dsecond = dsecond + dot(dlogits, small_ref[ROUTER_ROW : ROUTER_ROW + experts].astype(BF), 1, 0)
    u = dsecond * gain
    dmid = g_ref[...].astype(F32) + r * (u - n * jnp.mean(u * n, -1, keepdims=True))
    dmid_ref[...] = dmid
    dproj = dmid.astype(BF)
    for group in range(groups):
        part = dproj[group * slab : (group + 1) * slab]
        datt = dot(w_ref[...], part, 1, 1).astype(BF)
        for index in range(per_group):
            datt_ref[group * per_group + index] = datt[index * rows : (index + 1) * rows]
        att = att_ref[group * per_group : (group + 1) * per_group].reshape(D, slab)
        term = dot(att, part, 1, 0)
        if group == 0:
            total[:, 0:D] = term
        else:
            total[:, 0:D] += term
    narrow[...] = jnp.zeros_like(narrow)
    narrow[0:1, :] = jnp.sum(dsecond * n, 0, keepdims=True)
    for index, ref in enumerate(gb_refs):
        narrow[1 + index : 2 + index, :] = ref[...]
    narrow[ROUTER_ROW : ROUTER_ROW + experts, :] = dot(dlogits, second, 0, 0)
    total[:, D : D + 128] = narrow[...].T
    total[:, D + 128 :] = jnp.zeros((D, 128), F32)
    split_rows(me_ref, total, keep_ref, send_ref)


def qkv_grad_kernel(
    me_ref, first_ref, d_ref, band_ref, keep_ref, send_ref, acc, total
):
    slabs, rows, _ = d_ref.shape
    pairs = rows // 192
    half, part, _ = keep_ref.shape
    value = 0.0
    for index in range(slabs):
        value = value + dot(d_ref[index], first_ref[index], 1, 0)
    for pair in range(pairs):
        for which in range(3):
            to, source = (which * pairs + pair) * 64, pair * 192 + which * 64
            acc[to : to + 64, :] = value[source : source + 64, :]
    total[:, rows : rows + 64] = jnp.zeros((D, 64), F32)
    total[:, 0:rows] = acc[...].T
    row = lax.broadcasted_iota(jnp.int32, (BAND, QB), 0)
    col = lax.broadcasted_iota(jnp.int32, (BAND, QB), 1)
    near = col + (BAND - QB) - row < 128
    bucket_at = lax.broadcasted_iota(jnp.int32, (BUCKETS, 128), 0)
    lane = lax.broadcasted_iota(jnp.int32, (BUCKETS, 128), 1)
    bucket = jnp.zeros_like(lane)
    for index_b in range(1, BUCKETS):
        bucket = jnp.where(lane >= bucket_starts[index_b], index_b, bucket)
    mask = (bucket == bucket_at) & (bucket_at < BUCKETS - 1)
    flip_row = lax.broadcasted_iota(jnp.int32, (BAND, BAND), 0)
    flip_col = lax.broadcasted_iota(jnp.int32, (BAND, BAND), 1)
    flip = jnp.where(flip_row + flip_col == BAND - 1, 1.0, 0.0).astype(BF)
    sub = lax.broadcasted_iota(jnp.int32, (BUCKETS, 1), 0)
    per_owner = BUCKETS // (2 * half)
    for pair in range(pairs):
        values = jnp.where(near, band_ref[pair], 0.0)
        high = values.astype(BF)
        values = dot(flip, high, 1, 0) + dot(flip, (values - high.astype(F32)).astype(BF), 1, 0)
        values = pltpu.roll(values, 1, 1, stride=1, stride_axis=0)
        line = jnp.sum(values, 0, keepdims=True)[:, 0:128]
        sums = jnp.sum(jnp.where(mask, line, 0.0), 1, keepdims=True)
        sums = jnp.where(sub == BUCKETS - 1, -jnp.sum(sums, 0, keepdims=True), sums)
        for owner in range(2 * half):
            total[owner * part : owner * part + per_owner, rows + pair : rows + pair + 1] = sums[
                owner * per_owner : (owner + 1) * per_owner
            ]
    split_rows(me_ref, total, keep_ref, send_ref)


def last_kernel(tok_ref, small_ref, w_ref, dmid_ref, d_ref, gtok_ref, full):
    groups, slab, _ = tok_ref.shape
    slabs, rows, _ = d_ref.shape
    per_dest = rows // 192
    per_group = slabs // groups
    for group in range(groups):
        for which in range(3):
            for head in range(HEADS):
                dest = group * per_group + head // per_dest
                row = (head % per_dest) * 192 + which * 64
                to = which * D + head * 64
                full[to : to + 64, :] = d_ref[dest, row : row + 64, :]
        x = tok_ref[group].astype(F32)
        r = rms(x)
        n = x * r
        u = dot(w_ref[...], full[...], 1, 0).T * small_ref[0:1, :]
        gtok_ref[group] = dmid_ref[group * slab : (group + 1) * slab, :] + r * (
            u - n * jnp.mean(u * n, -1, keepdims=True)
        )


def finish_kernel(mine_ref, w_ref, gain_ref, *refs, pairs, experts):
    block_refs, refs = refs[:-8], refs[-8:]
    gw_ref, gnorm_ref, gbias_ref, gwo_ref, gffn_ref, grouter_ref, mixed, square = refs
    rows = gw_ref.shape[0]
    width = pairs * 64
    buckets = gbias_ref.shape[0]
    per_group = len(block_refs)
    quarter = mixed.shape[1] // per_group
    for mine in range(per_group):

        @pl.when(mine_ref[0] == mine)
        def _():
            for offset, ref in enumerate(block_refs):
                hg = mine ^ offset
                for which in range(3):
                    to = which * D + hg * width
                    gw_ref[:, to : to + width] = ref[:, which * width : (which + 1) * width].astype(F32)
                gbias_ref[:, hg * pairs : (hg + 1) * pairs] = ref[
                    0:buckets, 3 * width : 3 * width + pairs
                ].astype(F32)
                mixed[:, hg * quarter : (hg + 1) * quarter] = ref[:, 3 * width + 64 :].astype(F32)

    gnorm = jnp.sum(gw_ref[...] * w_ref[...].astype(F32), 1, keepdims=True)
    gwo_ref[...] = mixed[:, 0:D]
    square[...] = jnp.zeros_like(square)
    square[0:rows, :] = mixed[:, D : D + 128]
    square[0:rows, 1:2] = gnorm
    lines = square[...].T[:, 0:rows]
    gffn_ref[...] = lines[0:1]
    gnorm_ref[...] = lines[1:2] / gain_ref[...].astype(F32)
    grouter_ref[...] = lines[ROUTER_ROW : ROUTER_ROW + experts]


def output_kernel(mid_ref, slot_ref, gate_ref, *refs):
    back_refs, out_ref = refs[:-1], refs[-1]
    count = mid_ref.shape[0]
    each = back_refs[0].shape[0]
    slot = lax.broadcasted_iota(jnp.int32, (count, each), 1)
    total = mid_ref[...]
    for k in range(TOP):
        rows = 0.0
        for index, ref in enumerate(back_refs):
            at = jnp.where(slot + index * each == slot_ref[:, k : k + 1], 1.0, 0.0).astype(BF)
            rows = rows + dot(at, ref[...], 1, 0)
        total = total + gate_ref[:, k : k + 1] * rows
    out_ref[...] = total.astype(BF)


def expert_kernel(
    own_ref, rows_ref, g_ref, other_ref, small_ref, w_ref,
    out_ref, dd_ref, dgate_ref, dslot_ref, act_ref, dpre_ref, gb_ref, acc_out, acc_dd,
    *, index, local, experts,
):
    step, steps = pl.program_id(0), pl.num_programs(0)
    rows = rows_ref[...]

    @pl.when(step == 0)
    def _():
        own = own_ref[0] * local + index
        logits = dot(rows, small_ref[8 : 8 + experts].astype(BF), 1, 1)
        expert = lax.broadcasted_iota(jnp.int32, logits.shape, 1)
        mine = jnp.sum(jnp.where(expert == own, logits, 0.0), 1, keepdims=True)
        theirs = jnp.sum(jnp.where(expert == other_ref[...], logits, 0.0), 1, keepdims=True)
        gate = 1.0 / (1.0 + jnp.exp(theirs - mine))
        dslot = (g_ref[...].astype(F32) * gate).astype(BF)
        dslot_ref[...] = dslot
        gb_ref[...] = jnp.sum(dslot.astype(F32), 0, keepdims=True)
        acc_out[...] = jnp.zeros_like(acc_out)
        acc_dd[...] = jnp.zeros_like(acc_dd)

    w_in, w_out = w_ref[0, 0], w_ref[0, 1]
    pre = dot(rows, w_in, 1, 1)
    dact = dot(dslot_ref[...], w_out, 1, 1)
    root = math.sqrt(2 / math.pi)
    square = pre * pre
    tanh = jnp.tanh(pre * (root + (root * 0.044715) * square))
    half = 0.5 + 0.5 * tanh
    act = (pre * half).astype(BF)
    slope = half + (pre * (half - half * half)) * (2 * root + (6 * root * 0.044715) * square)
    act_ref[0] = act
    dpre = (dact * slope).astype(BF)
    dpre_ref[0] = dpre
    acc_dd[...] += dot(dpre, w_in, 1, 0)
    acc_out[...] += dot(act, w_out, 1, 0)

    @pl.when(step == steps - 1)
    def _():
        out = (acc_out[...] + small_ref[B_ROW + index : B_ROW + index + 1, :]).astype(BF)
        out_ref[...] = out
        dd_ref[...] = acc_dd[...].astype(BF)
        dgate = jnp.sum(out.astype(F32) * g_ref[...].astype(F32), 1, keepdims=True)
        dgate = jnp.broadcast_to(dgate, (dgate.shape[0], 128)).T
        high = dgate.astype(BF).astype(F32)
        middle = (dgate - high).astype(BF).astype(F32)
        line = lax.broadcasted_iota(jnp.int32, dgate.shape, 0)
        parts = jnp.where(line == 0, high, jnp.where(line == 1, middle, dgate - high - middle))
        dgate_ref[...] = parts[0:16].astype(BF)


def expert_pass(index, local, experts, own, rows, g_rows, other, small, weights):
    count, _ = rows.shape
    parts, _, units, _ = weights.shape
    token_s = pl.BlockSpec((count, D), lambda f: (0, 0))
    narrow_s = pl.BlockSpec((count, 1), lambda f: (0, 0))
    line_s = pl.BlockSpec((16, count), lambda f: (0, 0))
    weight_s = pl.BlockSpec((1, 2, units, D), lambda f: (f, 0, 0, 0))
    bias_s = pl.BlockSpec((1, D), lambda f: (0, 0))
    hidden_s = pl.BlockSpec((1, count, units), lambda f: (f, 0, 0))
    hidden = shape((parts, count, units), BF)
    return pl.pallas_call(
        functools.partial(expert_kernel, index=index, local=local, experts=experts),
        grid=(parts,),
        out_shape=(
            shape(rows.shape, BF),
            shape(rows.shape, BF),
            shape((16, count), BF),
            shape(rows.shape, BF),
            hidden,
            hidden,
            shape((1, D), F32),
        ),
        in_specs=[
            pl.BlockSpec(memory_space=pltpu.SMEM),
            token_s,
            token_s,
            narrow_s,
            pl.BlockSpec(small.shape, lambda f: (0, 0)),
            weight_s,
        ],
        out_specs=(token_s, token_s, line_s, token_s, hidden_s, hidden_s, bias_s),
        scratch_shapes=[pltpu.VMEM((count, D), F32), pltpu.VMEM((count, D), F32)],
        compiler_params=params(),
        cost_estimate=cost(10 * count * D * units * parts, 6 * D * units * parts * 2),
    )(own, rows, g_rows, other, small, weights)


def weight_kernel(*refs, local, parts):
    out_ref = refs[-1]
    for index in range(local):
        rows_ref, dslot_ref, act_ref, dpre_ref = refs[4 * index : 4 * index + 4]

        @pl.when(pl.program_id(0) // parts == index)
        def _():
            out_ref[0, 0, 0] = dot(dpre_ref[0], rows_ref[...], 0, 0).astype(BF)
            out_ref[0, 0, 1] = dot(act_ref[0], dslot_ref[...], 0, 0).astype(BF)


def weight_grads(operands):
    local = len(operands)
    count = operands[0][0].shape[0]
    parts, _, units = operands[0][2].shape
    token_s = pl.BlockSpec((count, D), lambda i: (0, 0))

    def hidden_s(index):
        return pl.BlockSpec(
            (1, count, units),
            lambda i: (jnp.clip(i - index * parts, 0, parts - 1), 0, 0),
        )

    return pl.pallas_call(
        functools.partial(weight_kernel, local=local, parts=parts),
        grid=(local * parts,),
        out_shape=shape((parts, local, 2, units, D), BF),
        in_specs=[
            spec
            for index in range(local)
            for spec in (token_s, token_s, hidden_s(index), hidden_s(index))
        ],
        out_specs=pl.BlockSpec(
            (1, 1, 2, units, D), lambda i: (lax.rem(i, parts), i // parts, 0, 0, 0)
        ),
        compiler_params=params(),
        cost_estimate=cost(1e6, 1e6),
    )(*[a for of in operands for a in of])


def spread_kernel(x_ref, in_ref, out_ref):
    for index in range(x_ref.shape[0]):
        in_ref[:, index, :] = x_ref[index, 0].astype(F32)
        out_ref[:, index, :] = x_ref[index, 1].astype(F32)


def spread_grads(owned):
    local, _, units, _ = owned.shape
    rows = min(128, units)
    out_s = pl.BlockSpec((rows, local, D), lambda i: (i, 0, 0))
    return pl.pallas_call(
        spread_kernel,
        grid=(units // rows,),
        in_specs=[pl.BlockSpec((local, 2, rows, D), lambda i: (0, 0, i, 0))],
        out_specs=(out_s, out_s),
        out_shape=[shape((units, local, D), F32)] * 2,
        compiler_params=params(),
        cost_estimate=cost(1e6, 1e6),
    )(owned)


def after(array, *others):
    return lax.optimization_barrier((array, *others))[0]


def swap(array, axis, bit):
    size = lax.axis_size(axis)
    return lax.ppermute(array, axis, [(i, i ^ bit) for i in range(size)])


def gather_parts(array):
    bit = lax.axis_size("fsdp") // 2
    held = [(0, array)]
    while bit:
        held = held + [(off ^ bit, swap(a, "fsdp", bit)) for off, a in held]
        bit //= 2
    return [off for off, _ in held], [a for _, a in held]


def exchange(array):
    return lax.all_to_all(array, "seq", split_axis=0, concat_axis=0, tiled=True)


def add(*arrays):
    return sum(a.astype(F32) for a in arrays).astype(BF)


def fold_first(keep, send):
    send = swap(send, "fsdp", 1)
    return [add(keep[index], send[index]) for index in range(keep.shape[0])]


def fold_rest(held):
    bit = 2
    while len(held) > 1:
        held = [add(a, swap(b, "fsdp", bit)) for a, b in zip(held[::2], held[1::2])]
        bit *= 2
    return held[0]


def slabs_of_sequence(tokens, me, per_group, packed):
    slabs = lax.axis_size("seq")
    groups = tokens.shape[0]
    if (slabs, groups, per_group) == (8, 2, 4):
        mine = lax.dynamic_index_in_dim(tokens, me // 4, 0, keepdims=False)
        theirs = lax.dynamic_index_in_dim(tokens, 1 - me // 4, 0, keepdims=False)
        far = swap(theirs, "seq", 4)
        found = {0: mine, 4: far}
        for bit in (1, 2, 3):
            found[bit] = swap(mine, "seq", bit)
        far = after(far, packed, *[found[bit] for bit in (1, 2, 3)])
        for bit in (1, 2, 3):
            found[4 ^ bit] = swap(far, "seq", bit)
        return me, list(found), list(found.values())
    rows = exchange(jnp.repeat(tokens, per_group, axis=0))
    return me * 0, list(range(slabs)), [rows[index] for index in range(slabs)]


def scalar(value):
    return value.reshape(1).astype(jnp.int32)


def per_device(
    tokens, cotangent, segments, routes, norm_attn, w_qkv, w_o, rel_bias, norm_ffn, router, w_in,
    w_out, b_out,
):
    slabs, owners = lax.axis_size("seq"), lax.axis_size("fsdp")
    me = lax.axis_index("seq")
    me_f = scalar(lax.axis_index("fsdp"))
    groups, slab = tokens.shape[0], tokens.shape[1]
    count = groups * slab
    experts, local = router.shape[1], b_out.shape[0]
    capacity = max(2, 9 * count * TOP // (8 * experts))
    slots = experts * capacity
    each = slots // local
    pairs = groups * HEADS // slabs
    per_group = HEADS // pairs
    width = pairs * HEAD_DIM
    part = D // owners
    head_group = lax.rem(me, per_group)
    grad_flat = cotangent.reshape(count, D)

    pack = one_step(
        pack_kernel,
        [shape((part, D + 128 + 3 * width), BF)],
        (
            scalar(head_group), w_qkv, w_o, norm_attn[None], norm_ffn[None], rel_bias, b_out,
            router.T,
        ),
        1e9,
        scratch=[pltpu.VMEM((128, 256), F32)],
        smem=1,
    )[0]
    offsets, packed = gather_parts(pack)
    base, slab_offsets, slab_rows = slabs_of_sequence(tokens, me, per_group, packed[1])
    w_columns, w_o_full, small, bands = one_step(
        functools.partial(unpack_kernel, offsets=offsets, pairs=pairs),
        [
            shape((D, 3 * width), BF),
            shape((D, D), BF),
            shape((128, D), F32),
            shape((pairs, BAND, QB), F32),
        ],
        (me_f, *packed),
        3e9,
        scratch=[pltpu.VMEM((D, 128), F32)],
        smem=1,
    )

    route_col = after(routes, slab_rows[5], small).reshape(count, TOP)
    base_col = (route_col % local) * each + (route_col // local) * capacity
    slot_col, slot_row, other, *g_slots = one_step(
        functools.partial(route_kernel, experts=experts, capacity=capacity),
        [
            shape((count, TOP), jnp.int32),
            shape((TOP, count), jnp.int32),
            shape((8, slots), F32),
        ]
        + [shape((each, D), BF)] * local,
        (route_col, route_col.T, base_col, base_col.T, grad_flat),
        5e9,
    )

    def cross(array):
        return exchange(array.reshape(slabs, capacity, D)).reshape(each, D)

    ids = other[0].reshape(local, slabs, capacity).swapaxes(0, 1).reshape(slabs, 1, -1)
    ids = jnp.pad(ids.astype(BF), ((0, 0), (0, 7), (0, D - local * capacity)))
    g_all = jnp.concatenate([a.reshape(slabs, capacity, D) for a in g_slots] + [ids], 1)
    g_all = exchange(after(g_all, *slab_rows[:G_AFTER]))

    def g_part(index):
        return g_all[:, index * capacity : (index + 1) * capacity].reshape(each, D)

    def other_part(index):
        at = slice(index * capacity, (index + 1) * capacity)
        return g_all[:, local * capacity, at].reshape(each, 1).astype(jnp.int32)

    seg = lax.dynamic_slice_in_dim(segments, me // per_group, 1, 0)
    qkv, first = one_step(
        functools.partial(project_kernel, offsets=slab_offsets),
        [shape((slabs, 3 * width, slab), BF), shape((slabs, slab, D), BF)],
        (scalar(base), small, w_columns, *slab_rows),
        4 * SEQ_LEN * D * 3 * width,
        smem=1,
    )
    out, wide, lse = attention_fwd(qkv, seg, bands)
    out, g_all = lax.optimization_barrier((out, g_all))
    att = exchange(out)
    mid, gates, *disp = one_step(
        functools.partial(middle_kernel, experts=experts),
        [shape((count, D), F32), shape((count, TOP), F32)] + [shape((each, D), BF)] * local,
        (tokens, small, w_o_full, route_col, slot_row, att),
        4 * count * D * (D + slots),
    )

    relaid = jnp.stack([w_in, w_out]).transpose(2, 0, 1, 3)
    weights = [
        lax.all_gather(relaid[index], "fsdp", axis=0, tiled=False) for index in range(local)
    ]
    w_qkv_late, _ = lax.optimization_barrier((w_qkv, att))
    w_qkv_full = lax.all_gather(w_qkv_late, "fsdp", axis=0, tiled=True)
    rows, passes = [], []
    for index in range(local):
        rows.append(cross(after(disp[index], *rows)))
    for index in range(local):
        if index:
            rows[index] = after(rows[index], passes[-1][1])
        passes.append(
            expert_pass(
                index, local, experts, scalar(me), rows[index], g_part(index),
                other_part(index), small, weights[index],
            )
        )
    results, dd, dgate, dslot, act, dpre, grad_b = map(list, zip(*passes))
    parts = jnp.stack([a[0:3] for a in dgate], 1).reshape(3 * local, slabs, capacity)
    parts = parts.swapaxes(0, 1).reshape(slabs, 1, -1)
    parts = jnp.pad(parts, ((0, 0), (0, 7), (0, D - parts.shape[2])))
    dd_back = [cross(a) for a in dd[:-1]]
    last = jnp.concatenate([dd[-1].reshape(slabs, capacity, D), parts], 1)
    last = exchange(after(last, *dd_back))
    dd_back.append(last[:, :capacity].reshape(each, D))
    parts = last[:, capacity, : 3 * local * capacity].astype(F32)
    dgate_back = jnp.sum(parts.reshape(slabs, 3, local, capacity), 1)
    dgate_back = dgate_back.swapaxes(0, 1).reshape(1, slots)
    act = [after(a, dd[-1]) for a in act]
    big = weight_grads(list(zip(rows, dslot, act, dpre)))
    *dd_back, big = lax.optimization_barrier((*dd_back, big))
    big = lax.psum_scatter(big, "fsdp", scatter_dimension=0, tiled=True)[0]

    dmid, grad_att, keep, send = one_step(
        functools.partial(return_kernel, local=local, experts=experts),
        [shape((count, D), F32), shape((slabs, width, slab), BF)]
        + [shape((owners // 2, part, D + 256), BF)] * 2,
        (
            me_f, dgate_back, slot_col, route_col, gates, mid, grad_flat, small, w_o_full, att,
            *dd_back, *grad_b,
        ),
        4 * count * D * (slots + 2 * D),
        scratch=[pltpu.VMEM((128, D), F32), pltpu.VMEM((D, D + 256), F32)],
        smem=1,
    )
    results_back = [cross(after(results[0], *dd_back))]
    grad_heads = exchange(after(grad_att, *results_back))
    for a in results[1:]:
        results_back.append(cross(after(a, grad_heads, *results_back)))
    mixed = fold_first(after(keep, grad_heads), send)
    d_qkv, band_sums = attention_bwd(qkv, seg, bands, wide, lse, grad_heads)
    mixed[0] = after(mixed[0], d_qkv)
    mixed = fold_rest(mixed)
    d_back = exchange(after(d_qkv, *results_back))
    output = one_step(
        output_kernel,
        (shape((count, D), BF),),
        (after(mid, d_qkv), slot_col, gates, *results_back),
        4 * count * D * slots,
    )[0].reshape(groups, slab, D)

    keep, send = one_step(
        qkv_grad_kernel,
        [shape((owners // 2, part, 3 * width + 64), BF)] * 2,
        (me_f, first, d_qkv, band_sums),
        4 * SEQ_LEN * D * 3 * width,
        scratch=[pltpu.VMEM((3 * width, D), F32), pltpu.VMEM((D, 3 * width + 64), F32)],
        smem=1,
    )
    grad_tokens = one_step(
        last_kernel,
        [shape((groups, slab, D), F32)],
        (tokens, small, w_qkv_full, dmid, after(d_back, keep, output)),
        4 * count * D * 3 * D,
        scratch=[pltpu.VMEM((3 * D, slab), BF)],
    )[0]
    grad_qkv = fold_rest(fold_first(keep, send))
    grad_b_own = mixed[:, D + 1 : D + 1 + local].astype(F32).T
    quarter = (D + 256) // per_group

    def quarter_of(offset):
        return lax.dynamic_slice_in_dim(mixed, (head_group ^ offset) * quarter, quarter, 1)

    mixed = add(quarter_of(0), *[swap(quarter_of(k), "seq", k) for k in range(1, per_group)])
    block = jnp.concatenate([grad_qkv, mixed], 1)
    bit = per_group
    while bit < slabs:
        block = add(after(block, output), swap(block, "seq", bit))
        bit *= 2
    blocks = [block] + [swap(block, "seq", k) for k in range(1, per_group)]
    big = after(big, grad_tokens)
    grad_w_in, grad_w_out = spread_grads(big)
    blocks[0], grad_w_in, grad_w_out = lax.optimization_barrier((blocks[0], grad_w_in, grad_w_out))
    grad_wqkv, grad_gain_attn, grad_bias, grad_wo, grad_gain_ffn, grad_router = one_step(
        functools.partial(finish_kernel, pairs=pairs, experts=experts),
        [
            shape((part, 3 * D), F32),
            shape((1, part), F32),
            shape(rel_bias.shape, F32),
            shape((part, D), F32),
            shape((1, part), F32),
            shape((experts, part), F32),
        ],
        (scalar(head_group), w_qkv, norm_attn[None], *blocks),
        1e9,
        scratch=[pltpu.VMEM((part, D + 256), F32), pltpu.VMEM((256, 128), F32)],
        smem=1,
    )
    return (
        output,
        grad_tokens,
        grad_gain_attn[0],
        grad_wqkv,
        grad_wo,
        grad_bias,
        grad_gain_ffn[0],
        grad_router.T,
        grad_w_in,
        grad_w_out,
        grad_b_own,
    )


def solution(mesh):
    in_specs = (
        P("fsdp", "seq", None),
        P("fsdp", "seq", None),
        P("fsdp", None),
        P("fsdp", "seq", None),
        P("fsdp"),
        P("fsdp", None),
        P("fsdp", None),
        P("fsdp", None),
        P("fsdp"),
        P("fsdp", None),
        P("fsdp", "seq", None),
        P("fsdp", "seq", None),
        P("seq", "fsdp"),
    )
    out_specs = (
        P("fsdp", "seq", None),
        P("fsdp", "seq", None),
        P("fsdp"),
        P("fsdp", None),
        P("fsdp", None),
        P("fsdp", None),
        P("fsdp"),
        P("fsdp", None),
        P("fsdp", "seq", None),
        P("fsdp", "seq", None),
        P("seq", "fsdp"),
    )
    return jax.shard_map(
        per_device, mesh=mesh, in_specs=in_specs, out_specs=out_specs, check_vma=False
    )
```
